32 devices in a mesh: chain: 2 (over x), tile: 16 (over z, y, core).
Axes of the slice: x: 2, y: 2, z: 4, core: 2. Of those that a mesh axis runs over, the one named last changes fastest.
Arguments:
- right_side: float32 [3, 2, 32, 8192], P(None, None, None, ('chain', 'tile')), may hold values from -6 to 6
- diag_inverse: float32 [2, 8192, 4096], P(None, ('chain', 'tile'))
- coupling: float32 [2, 8192, 4096], P(None, ('chain', 'tile')), may hold values from -0.0390625 to 0.0390625
- updates: float32 [8192, 192], P(('chain', 'tile')), may hold values from -2.4 to 2.4
- update_rows: int32 [8192], P(('chain', 'tile')), may hold values from 0 to 4095, as said below
- tile_counts: int32 [64], P(('chain', 'tile')), may hold values from 32 to 128, as said below
Outputs:
- solution: float32 [3, 2, 32, 8192], P(None, None, None, ('chain', 'tile'))
The draws below stay inside these ranges and needn't reach their ends.
Inputs may be any that keep to these rules, and one draw needn't show every extreme that they name: `update_rows`: rows are counted within the supernode of the group that holds the entry. In each aligned block of 256 entries (the update rows of one device) at most 32 entries fall in any one aligned range of 256 rows, and in each run of 16 aligned blocks one such range receives exactly 32 entries from every block of the run. Padding rows carry entries too. `tile_counts`: one tile has all 128 rows live.
All inputs are finite; a program needn't handle non-finite values.
Results may differ from the reference program's by a relative error of at most 0.0001.
Values sent between devices are 32-bit elements; how exact they have to be, the bound alone decides.
No kernel may reach another device: no remote copies, remote signals or barrier semaphores. Data moves between devices by JAX's collectives and lax.ppermute only.
A program may use at most 64 MiB of HBM per device.

```python
import math
import jax
import jax.numpy as jnp
from jax import lax

S = 4096
R = 32
NB = 3
UT = 2
TR = 128
NSUP = 2
GROUP = 16
BR = 256
CAP = 32


def draw_diag_inverse(key, part):
    total_rows = NSUP * S
    local_row = (jnp.arange(total_rows, dtype=jnp.int32) % S)[:, None]
    column = jnp.arange(S, dtype=jnp.int32)[None, :]
    spread = jax.random.normal(jax.random.fold_in(key, 31), (2, total_rows, S), jnp.float32) * (0.6 / math.sqrt(S))
    real_diag = jax.random.uniform(jax.random.fold_in(key, 32), (total_rows, 1), jnp.float32, 0.8, 1.4)
    imag_diag = jax.random.uniform(jax.random.fold_in(key, 33), (total_rows, 1), jnp.float32, -0.3, 0.3)
    diag_vals = jnp.stack([real_diag, imag_diag], axis=0)
    lower = jnp.where((column < local_row)[None, :, :], spread, 0.0)
    return lower + jnp.where((column == local_row)[None, :, :], diag_vals, 0.0)


def draw_update_rows(key, part):
    devices_all = NSUP * GROUP
    per_device = UT * TR
    slot_total = GROUP * CAP
    hot_owner = jax.random.randint(jax.random.fold_in(key, 11), (NSUP,), 0, GROUP)
    hot_device = jnp.repeat(hot_owner, GROUP)
    scores = jax.random.randint(jax.random.fold_in(key, 12), (devices_all, slot_total), 0, 1 << 20)
    slot_ids = jnp.arange(slot_total, dtype=jnp.int32)[None, :]
    scores = jnp.where(slot_ids // CAP == hot_device[:, None], -1 - slot_ids, scores)
    chosen = jnp.argsort(scores, axis=1, stable=True)[:, :per_device]
    owners = (chosen // CAP).astype(jnp.int32)
    shuffle_keys = jax.random.split(jax.random.fold_in(key, 13), devices_all)
    shuffles = jax.vmap(lambda single: jax.random.permutation(single, per_device))(shuffle_keys)
    owners = jnp.take_along_axis(owners, shuffles, axis=1)
    local_rows = jax.random.randint(jax.random.fold_in(key, 14), (devices_all, per_device), 0, BR)
    return (owners * BR + local_rows).reshape(-1).astype(jnp.int32)


def draw_tile_counts(key, part):
    tiles_all = NSUP * GROUP * UT
    counts = jax.random.randint(jax.random.fold_in(key, 21), (tiles_all,), TR // 4, TR + 1)
    full_tile = jax.random.randint(jax.random.fold_in(key, 22), (), 0, tiles_all)
    return jnp.where(jnp.arange(tiles_all, dtype=jnp.int32) == full_tile, TR, counts).astype(jnp.int32)


def shard_levels(stream_key, dims, cuts, least, top_value):
    factor_of = 1.0
    for dim, shards_of in cuts:
        heights = jax.random.uniform(jax.random.fold_in(jax.random.fold_in(stream_key, 6), dim), (shards_of,), jnp.float32, least / len(cuts), top_value / len(cuts))
        factor_of = factor_of * jnp.repeat(jnp.exp(heights), dims[dim] // shards_of).reshape((-1,) + (1,) * (len(dims) - 1 - dim))
    return factor_of


def bell_draw(key, shape, deviation, most, cuts=(), kind=jnp.bfloat16):
    result = deviation * jax.random.normal(key, shape, jnp.float32)
    if cuts:
        result = result * shard_levels(key, shape, cuts, -0.22, 0.18)
    return jnp.clip(result, -most, most).astype(kind)


def setup_inputs(seed: int = 0) -> dict:
    splits = jax.random.split(jax.random.key(seed), 7)
    return {
        "right_side": bell_draw(splits[0], (NB, 2, R, NSUP * S), 1.0, 6.0, ((3, 32),), jnp.float32),
        "diag_inverse": draw_diag_inverse(jax.random.fold_in(splits[6], 71), 0),
        "coupling": bell_draw(splits[2], (2, NSUP * S, S), (6 * S) ** -0.5, 0.0390625, ((1, 32),), jnp.float32),
        "updates": bell_draw(splits[3], (NSUP * GROUP * UT * TR, NB * 2 * R), 0.4, 2.4, ((0, 32),), jnp.float32),
        "update_rows": draw_update_rows(jax.random.fold_in(splits[6], 71), 0),
        "tile_counts": draw_tile_counts(jax.random.fold_in(splits[6], 71), 0),
    }


def complex_apply(matrix, reduced):
    products = jnp.einsum('bjrs,kis->bkjri', reduced, matrix, precision=lax.Precision.HIGHEST)
    real_part = products[:, 0, 0] - products[:, 1, 1]
    imag_part = products[:, 0, 1] + products[:, 1, 0]
    return jnp.stack([real_part, imag_part], axis=1)


def reference(right_side, diag_inverse, coupling, updates, update_rows, tile_counts):
    count_rows = updates.shape[0]
    row_index = jnp.arange(count_rows, dtype=jnp.int32)
    limits = jnp.repeat(tile_counts, TR)
    is_live = (row_index % TR) < limits
    live_updates = jnp.where(is_live[:, None], updates, jnp.zeros_like(updates))
    group_of = row_index // (GROUP * UT * TR)
    target = (group_of * S + update_rows).astype(jnp.int32)
    accumulated = jax.ops.segment_sum(live_updates, target, num_segments=NSUP * S)
    arranged = accumulated.reshape(NSUP * S, NB, 2, R).transpose(1, 2, 3, 0)
    reduced_all = right_side - arranged
    carried = jnp.zeros((NB, 2, R, S), jnp.float32)
    pieces = []
    for chain_step in range(NSUP):
        offset = chain_step * S
        reduced = reduced_all[:, :, :, offset:offset + S] - carried
        pieces.append(complex_apply(diag_inverse[:, offset:offset + S, :], reduced))
        carried = complex_apply(coupling[:, offset:offset + S, :], reduced)
    return jnp.concatenate(pieces, axis=3)
```

```python
import functools

import jax
import jax.numpy as jnp
from jax import lax
from jax.experimental import pallas as pl
from jax.experimental.pallas import tpu as pltpu
from jax.sharding import PartitionSpec as P

MIB = 1 << 20
f32 = jnp.float32
bf16 = jnp.bfloat16


def halves_of(value):
    high = value.astype(bf16)
    return high, (value - high.astype(f32)).astype(bf16)


def thirds_of(value):
    high = value.astype(bf16)
    rest = value - high.astype(f32)
    middle = rest.astype(bf16)
    return high, middle, (rest - middle.astype(f32)).astype(bf16)


def pack_kernel(own_rows, cap, columns, tile_rows, counts_ref, lane_rows_ref, column_rows_ref, updates_ref, packed_ref):
    entries = updates_ref.shape[0]
    slots, width = packed_ref.shape
    entry = lax.broadcasted_iota(jnp.int32, (entries, 1), 0)
    live = jnp.zeros((entries, 1), jnp.bool_)
    for tile in range(entries // tile_rows):
        start = tile * tile_rows
        live = live | ((entry >= start) & (entry < start + counts_ref[tile]))
    column_rows = column_rows_ref[...]
    lane_rows = lane_rows_ref[...]
    column_owner = column_rows // own_rows
    lane_owner = lane_rows // own_rows
    earlier = lax.broadcasted_iota(jnp.int32, (entries, entries), 0) < lax.broadcasted_iota(jnp.int32, (entries, entries), 1)
    rank = jnp.sum(jnp.where(earlier & (column_owner == lane_owner), 1, 0), axis=0, keepdims=True)
    slot = lane_owner * cap + rank
    choose = jnp.where(lax.broadcasted_iota(jnp.int32, (slots, entries), 0) == slot, 1.0, 0.0).astype(bf16)
    data = jnp.where(live, updates_ref[...], 0.0)
    local_row = (column_rows - column_owner * own_rows).astype(f32)
    tail = jnp.where(lax.broadcasted_iota(jnp.int32, (entries, width - columns), 1) == 0, local_row, 0.0)
    data = jnp.concatenate([data, tail], axis=1)
    packed = jnp.zeros((slots, width), f32)
    for piece in thirds_of(data):
        packed += jnp.dot(choose, piece, preferred_element_type=f32)
    packed_ref[...] = packed


def reduce_kernel(columns, received_ref, right_ref, reduced_ref):
    slots = received_ref.shape[0]
    own_rows = reduced_ref.shape[1]
    received = received_ref[...]
    local_row = received[:, columns:columns + 1].astype(jnp.int32)
    place = jnp.where(lax.broadcasted_iota(jnp.int32, (slots, own_rows), 1) == local_row, 1.0, 0.0).astype(bf16)
    total = jnp.zeros(reduced_ref.shape, f32)
    for piece in thirds_of(received[:, :columns].T):
        total += jnp.dot(piece, place, preferred_element_type=f32)
    reduced_ref[...] = right_ref[...] - total


def product_kernel(halves, sources, x_ref, k_ref, out_ref, total_ref):
    step = pl.program_id(0)
    parts, own_rows, width = k_ref.shape
    columns = x_ref.shape[1]
    x = jnp.concatenate([x_ref[i] for i in range(x_ref.shape[0])], axis=1)
    k = k_ref[...].reshape(parts * own_rows, width)
    x_high, x_low = halves_of(x)
    k_high, k_low = halves_of(k)
    contract = (((1,), (1,)), ((), ()))
    both = lax.dot_general(jnp.concatenate([x_high, x_low], axis=0), k_high, contract, preferred_element_type=f32)
    part = both[:columns] + both[columns:] + lax.dot_general(x_high, k_low, contract, preferred_element_type=f32)

    @pl.when(step == 0)
    def _():
        total_ref[...] = part

    @pl.when(step > 0)
    def _():
        total_ref[...] += part

    @pl.when(step == pl.num_programs(0) - 1)
    def _():
        group = halves * sources
        for batch in range(columns // group):
            real = pl.ds(batch * group, sources)
            imag = pl.ds(batch * group + sources, sources)
            out_ref[real, :] = total_ref[real, :own_rows] - total_ref[imag, own_rows:]
            out_ref[imag, :] = total_ref[imag, :own_rows] + total_ref[real, own_rows:]


def complex_apply(matrix, blocks, halves, sources):
    parts, own_rows, full_rows = matrix.shape
    count, columns, block = blocks.shape
    per_step = min(count, max(1, 1024 // block))
    width = per_step * block
    return pl.pallas_call(
        functools.partial(product_kernel, halves, sources),
        grid=(full_rows // width,),
        in_specs=[
            pl.BlockSpec((per_step, columns, block), lambda i: (i, 0, 0)),
            pl.BlockSpec((parts, own_rows, width), lambda i: (0, 0, i)),
        ],
        out_specs=pl.BlockSpec((columns, own_rows), lambda i: (0, 0)),
        out_shape=jax.ShapeDtypeStruct((columns, own_rows), f32),
        scratch_shapes=[pltpu.VMEM((columns, parts * own_rows), f32)],
        compiler_params=pltpu.CompilerParams(vmem_limit_bytes=32 * MIB),
        cost_estimate=pl.CostEstimate(flops=6 * columns * parts * own_rows * full_rows, bytes_accessed=4 * matrix.size, transcendentals=0),
    )(blocks, matrix)


def gather_blocks(reduced):
    columns, own_rows = reduced.shape
    gathered = lax.all_gather(reduced, "tile", axis=0, tiled=False)
    if own_rows % 128 == 0:
        return gathered
    block = 256
    whole = gathered.transpose(1, 0, 2).reshape(columns, -1, block)
    return whole.transpose(1, 0, 2)


def body(right_side, diag_inverse, coupling, updates, update_rows, tile_counts):
    batches, halves, sources, own_rows = right_side.shape
    chain_size = lax.axis_size("chain")
    tile_size = lax.axis_size("tile")
    entries, columns = updates.shape
    tile_rows = entries // tile_counts.shape[0]
    cap = 2 * entries // tile_size
    slots = tile_size * cap
    width = -(-(columns + 1) // 128) * 128
    vmem = pl.BlockSpec(memory_space=pltpu.VMEM)
    smem = pl.BlockSpec(memory_space=pltpu.SMEM)
    packed = pl.pallas_call(
        functools.partial(pack_kernel, own_rows, cap, columns, tile_rows),
        in_specs=[smem, vmem, vmem, vmem],
        out_specs=vmem,
        out_shape=jax.ShapeDtypeStruct((slots, width), f32),
        compiler_params=pltpu.CompilerParams(vmem_limit_bytes=32 * MIB),
    )(tile_counts, update_rows[None, :], update_rows[:, None], updates)
    received = lax.all_to_all(packed.reshape(tile_size, cap, width), "tile", 0, 0, tiled=False).reshape(slots, width)
    reduced_all = pl.pallas_call(
        functools.partial(reduce_kernel, columns),
        in_specs=[vmem, vmem],
        out_specs=vmem,
        out_shape=jax.ShapeDtypeStruct((columns, own_rows), f32),
        compiler_params=pltpu.CompilerParams(vmem_limit_bytes=32 * MIB),
    )(received, right_side.reshape(columns, own_rows))
    onward = [(i, i + 1) for i in range(chain_size - 1)]
    reduced = reduced_all
    for _ in range(chain_size - 1):
        carried = complex_apply(coupling, gather_blocks(reduced), halves, sources)
        reduced = reduced_all - lax.ppermute(carried, "chain", onward)
    solution = complex_apply(diag_inverse, gather_blocks(reduced), halves, sources)
    return solution.reshape(right_side.shape)


def solution(mesh):
    in_specs = (
        P(None, None, None, ("chain", "tile")),
        P(None, ("chain", "tile"), None),
        P(None, ("chain", "tile"), None),
        P(("chain", "tile"), None),
        P(("chain", "tile")),
        P(("chain", "tile")),
    )
    out_specs = P(None, None, None, ("chain", "tile"))
    return jax.shard_map(body, mesh=mesh, in_specs=in_specs, out_specs=out_specs, check_vma=False)
```

```python
import functools

import jax
import jax.numpy as jnp
from jax import lax
from jax.experimental import pallas as pl
from jax.experimental.pallas import tpu as pltpu
from jax.sharding import PartitionSpec as P

MIB = 1 << 20
CHUNKS = 2
f32 = jnp.float32
bf16 = jnp.bfloat16
lanes_contract = (((1,), (1,)), ((), ()))


def halves_of(value):
    high = value.astype(bf16)
    return high, (value - high.astype(f32)).astype(bf16)


def thirds_of(value):
    high = value.astype(bf16)
    rest = value - high.astype(f32)
    middle = rest.astype(bf16)
    return high, middle, (rest - middle.astype(f32)).astype(bf16)


def kernel_params():
    return pltpu.CompilerParams(vmem_limit_bytes=56 * MIB)


def pack_kernel(own_rows, cap, tile_rows, counts_ref, rows_ref, updates_ref, packed_ref):
    columns, entries = updates_ref.shape
    slots, width = packed_ref.shape
    entry = lax.broadcasted_iota(jnp.int32, (1, entries), 1)
    live = jnp.zeros((1, entries), jnp.bool_)
    for tile in range(entries // tile_rows):
        start = tile * tile_rows
        live = live | ((entry >= start) & (entry < start + counts_ref[tile]))
    rows = rows_ref[...]
    owner = rows // own_rows
    lane_owner = jnp.broadcast_to(owner.astype(f32), (entries, entries))
    earlier = lax.broadcasted_iota(jnp.int32, (entries, entries), 0) < lax.broadcasted_iota(jnp.int32, (entries, entries), 1)
    rank = jnp.sum(jnp.where(earlier & (lane_owner.T == lane_owner), 1, 0), axis=0, keepdims=True)
    slot = owner * cap + rank
    choose = jnp.where(lax.broadcasted_iota(jnp.int32, (slots, entries), 0) == slot, 1.0, 0.0).astype(bf16)
    data = jnp.where(live, updates_ref[...], 0.0)
    local_row = (rows - owner * own_rows).astype(f32)
    tail = jnp.where(lax.broadcasted_iota(jnp.int32, (width - columns, entries), 0) == 0, local_row, 0.0)
    data = jnp.concatenate([data, tail], axis=0)
    packed = jnp.zeros((slots, width), f32)
    for piece in thirds_of(data):
        packed += lax.dot_general(choose, piece, lanes_contract, preferred_element_type=f32)
    packed_ref[...] = packed


def reduce_kernel(received_ref, right_ref, *reduced_refs):
    slots = received_ref.shape[0]
    batches, halves, sources, own_rows = right_ref.shape
    columns = batches * halves * sources
    received = received_ref[...]
    local_row = received[:, columns:columns + 1].astype(jnp.int32)
    place = jnp.where(lax.broadcasted_iota(jnp.int32, (slots, own_rows), 1) == local_row, 1.0, 0.0).astype(bf16)
    total = jnp.zeros((columns, own_rows), f32)
    for piece in thirds_of(received[:, :columns].T):
        total += jnp.dot(piece, place, preferred_element_type=f32)
    reduced = right_ref[...].reshape(columns, own_rows) - total
    share = sources // len(reduced_refs)
    for group in range(batches * halves):
        for chunk, reduced_ref in enumerate(reduced_refs):
            start = group * sources + chunk * share
            reduced_ref[group * share:(group + 1) * share, :] = reduced[start:start + share]


def product_kernel(sources, blocks_count, *refs):
    x_refs = refs[:blocks_count]
    k_ref, out_ref, total_ref = refs[blocks_count:]
    step = pl.program_id(0)
    parts, own_rows, width = k_ref.shape
    columns = out_ref.shape[0]
    x = jnp.concatenate([x_refs[0][i] for i in range(x_refs[0].shape[0])], axis=1)
    for x_ref in x_refs[1:]:
        x -= jnp.concatenate([x_ref[i] for i in range(x_ref.shape[0])], axis=1)
    k = k_ref[...].reshape(parts * own_rows, width)
    x_high, x_low = halves_of(x)
    k_high, k_low = halves_of(k)
    both = lax.dot_general(jnp.concatenate([x_high, x_low], axis=0), k_high, lanes_contract, preferred_element_type=f32)
    part = both[:columns] + both[columns:] + lax.dot_general(x_high, k_low, lanes_contract, preferred_element_type=f32)

    @pl.when(step == 0)
    def _():
        total_ref[...] = part

    @pl.when(step > 0)
    def _():
        total_ref[...] += part

    @pl.when(step == pl.num_programs(0) - 1)
    def _():
        for batch in range(columns // (2 * sources)):
            real = pl.ds(batch * 2 * sources, sources)
            imag = pl.ds((batch * 2 + 1) * sources, sources)
            out_ref[real, :] = total_ref[real, :own_rows] - total_ref[imag, own_rows:]
            out_ref[imag, :] = total_ref[imag, :own_rows] + total_ref[real, own_rows:]


def complex_apply(matrix, blocks, sources):
    parts, own_rows, full_rows = matrix.shape
    count, columns, block = blocks[0].shape
    per_step = min(count, max(1, 512 // block))
    width = per_step * block
    return pl.pallas_call(
        functools.partial(product_kernel, sources, len(blocks)),
        grid=(full_rows // width,),
        in_specs=[pl.BlockSpec((per_step, columns, block), lambda i: (i, 0, 0)) for _ in blocks]
        + [pl.BlockSpec((parts, own_rows, width), lambda i: (0, 0, i))],
        out_specs=pl.BlockSpec((columns, own_rows), lambda i: (0, 0)),
        out_shape=jax.ShapeDtypeStruct((columns, own_rows), f32),
        scratch_shapes=[pltpu.VMEM((columns, parts * own_rows), f32)],
        compiler_params=kernel_params(),
        cost_estimate=pl.CostEstimate(flops=6 * columns * parts * own_rows * full_rows, bytes_accessed=4 * matrix.size, transcendentals=0),
    )(*blocks, matrix)


def gather_blocks(reduced):
    columns, own_rows = reduced.shape
    gathered = lax.all_gather(reduced, "tile", axis=0, tiled=False)
    if own_rows % 128 == 0:
        return gathered
    block = 256
    whole = gathered.transpose(1, 0, 2).reshape(columns, -1, block)
    return whole.transpose(1, 0, 2)


def body(right_side, diag_inverse, coupling, updates, update_rows, tile_counts):
    batches, halves, sources, own_rows = right_side.shape
    chain_size = lax.axis_size("chain")
    tile_size = lax.axis_size("tile")
    entries, columns = updates.shape
    tile_rows = entries // tile_counts.shape[0]
    cap = 2 * entries // tile_size
    slots = tile_size * cap
    width = -(-(columns + 1) // 128) * 128
    share = sources // CHUNKS
    vmem = pl.BlockSpec(memory_space=pltpu.VMEM)
    smem = pl.BlockSpec(memory_space=pltpu.SMEM)
    packed = pl.pallas_call(
        functools.partial(pack_kernel, own_rows, cap, tile_rows),
        in_specs=[smem, vmem, vmem],
        out_specs=vmem,
        out_shape=jax.ShapeDtypeStruct((slots, width), f32),
        compiler_params=kernel_params(),
    )(tile_counts, update_rows[None, :], updates.T)
    received = lax.all_to_all(packed.reshape(tile_size, cap, width), "tile", 0, 0, tiled=False).reshape(slots, width)
    reduced = pl.pallas_call(
        reduce_kernel,
        in_specs=[vmem, vmem],
        out_specs=[vmem] * CHUNKS,
        out_shape=[jax.ShapeDtypeStruct((columns // CHUNKS, own_rows), f32)] * CHUNKS,
        compiler_params=kernel_params(),
    )(received, right_side)
    onward = [(i, i + 1) for i in range(chain_size - 1)]
    own = [gather_blocks(chunk) for chunk in reduced]
    state = [[blocks] for blocks in own]
    for _ in range(chain_size - 1):
        for chunk in range(CHUNKS):
            carried = complex_apply(coupling, state[chunk], share)
            state[chunk] = [own[chunk], gather_blocks(lax.ppermute(carried, "chain", onward))]
    pieces = [complex_apply(diag_inverse, blocks, share).reshape(batches, halves, share, own_rows) for blocks in state]
    return jnp.concatenate(pieces, axis=2)


def solution(mesh):
    in_specs = (
        P(None, None, None, ("chain", "tile")),
        P(None, ("chain", "tile"), None),
        P(None, ("chain", "tile"), None),
        P(("chain", "tile"), None),
        P(("chain", "tile")),
        P(("chain", "tile")),
    )
    out_specs = P(None, None, None, ("chain", "tile"))
    return jax.shard_map(body, mesh=mesh, in_specs=in_specs, out_specs=out_specs, check_vma=False)
```

```python
import functools

import jax
import jax.numpy as jnp
from jax import lax
from jax.experimental import pallas as pl
from jax.experimental.pallas import tpu as pltpu
from jax.sharding import PartitionSpec as P

MIB = 1 << 20
AHEAD = 3
f32 = jnp.float32
bf16 = jnp.bfloat16
lanes_contract = (((1,), (1,)), ((), ()))


def halves_of(value):
    high = value.astype(bf16)
    return high, (value - high.astype(f32)).astype(bf16)


def thirds_of(value):
    high = value.astype(bf16)
    rest = value - high.astype(f32)
    middle = rest.astype(bf16)
    return high, middle, (rest - middle.astype(f32)).astype(bf16)


def kernel_params():
    return pltpu.CompilerParams(vmem_limit_bytes=56 * MIB)


def pack_kernel(own_rows, cap, tile_rows, counts_ref, rows_ref, updates_ref, packed_ref):
    columns, entries = updates_ref.shape
    slots, width = packed_ref.shape
    entry = lax.broadcasted_iota(jnp.int32, (1, entries), 1)
    live = jnp.zeros((1, entries), jnp.bool_)
    for tile in range(entries // tile_rows):
        start = tile * tile_rows
        live = live | ((entry >= start) & (entry < start + counts_ref[tile]))
    rows = rows_ref[...]
    owner = rows // own_rows
    lane_owner = jnp.broadcast_to(owner.astype(f32), (entries, entries))
    earlier = lax.broadcasted_iota(jnp.int32, (entries, entries), 0) < lax.broadcasted_iota(jnp.int32, (entries, entries), 1)
    rank = jnp.sum(jnp.where(earlier & (lane_owner.T == lane_owner), 1, 0), axis=0, keepdims=True)
    slot = owner * cap + rank
    choose = jnp.where(lax.broadcasted_iota(jnp.int32, (slots, entries), 0) == slot, 1.0, 0.0).astype(bf16)
    data = jnp.where(live, updates_ref[...], 0.0)
    local_row = (rows - owner * own_rows).astype(f32)
    tail = jnp.where(lax.broadcasted_iota(jnp.int32, (width - columns, entries), 0) == 0, local_row, 0.0)
    data = jnp.concatenate([data, tail], axis=0)
    packed = jnp.zeros((slots, width), f32)
    for piece in thirds_of(data):
        packed += lax.dot_general(choose, piece, lanes_contract, preferred_element_type=f32)
    packed_ref[...] = packed


def reduce_kernel(received_ref, right_ref, reduced_ref):
    slots = received_ref.shape[0]
    columns, own_rows = reduced_ref.shape
    received = received_ref[...]
    local_row = received[:, columns:columns + 1].astype(jnp.int32)
    place = jnp.where(lax.broadcasted_iota(jnp.int32, (slots, own_rows), 1) == local_row, 1.0, 0.0).astype(bf16)
    total = jnp.zeros((columns, own_rows), f32)
    for piece in thirds_of(received[:, :columns].T):
        total += jnp.dot(piece, place, preferred_element_type=f32)
    reduced_ref[...] = right_ref[...] - total


def product_kernel(sources, plain, counts, order_ref, *refs):
    sets = 1 if plain else 2
    x_refs = refs[:len(counts)]
    own_refs = refs[len(counts):-6]
    k_ref, out_ref, x_buf, k_buf, total_ref, sems = refs[-6:]
    parts, own_rows, block = k_buf.shape[1:]
    columns = out_ref.shape[0]
    count = sum(counts)
    place = [(i, j) for i in range(len(counts)) for j in range(counts[i])]

    def copies(q):
        i, j = place[q]
        tile = order_ref[q]
        made = [
            (x_refs[i].at[j], x_buf.at[0, q], sems.at[0, q]),
            (k_ref.at[:, :, pl.ds(pl.multiple_of(tile * block, block), block)], k_buf.at[q], sems.at[1, q]),
        ]
        if not plain:
            made.append((own_refs[i * len(own_refs) // len(counts)].at[tile // 2], x_buf.at[1, q], sems.at[2, q]))
        return [pltpu.make_async_copy(*each) for each in made]

    for q in range(min(count, 2 * AHEAD)):
        for copy in copies(q):
            copy.start()
    total = None
    for first in range(0, count, 2):
        pair = range(first, min(first + 2, count))
        for q in pair:
            if q + 2 * AHEAD < count:
                for copy in copies(q + 2 * AHEAD):
                    copy.start()
        for q in pair:
            for copy in copies(q):
                copy.wait()
        x = jnp.concatenate([x_buf[0, q] if plain else x_buf[1, q] - x_buf[0, q] for q in pair], axis=1)
        k = jnp.concatenate([k_buf[q].reshape(parts * own_rows, block) for q in pair], axis=1)
        x_high, x_low = halves_of(x)
        k_high, k_low = halves_of(k)
        both = lax.dot_general(jnp.concatenate([x_high, x_low], axis=0), k_high, lanes_contract, preferred_element_type=f32)
        part = both[:columns] + both[columns:] + lax.dot_general(x_high, k_low, lanes_contract, preferred_element_type=f32)
        if first == 0:
            total_ref[...] = part
        else:
            total_ref[...] += part
    for batch in range(columns // (2 * sources)):
        real = pl.ds(batch * 2 * sources, sources)
        imag = pl.ds((batch * 2 + 1) * sources, sources)
        out_ref[real, :] = total_ref[real, :own_rows] - total_ref[imag, own_rows:]
        out_ref[imag, :] = total_ref[imag, :own_rows] + total_ref[real, own_rows:]


def complex_apply(matrix, order, blocks, own, sources):
    parts, own_rows, full_rows = matrix.shape
    columns, block = blocks[0].shape[1:]
    counts = [each.shape[0] for each in blocks]
    plain = len(own) == 0
    anywhere = pl.BlockSpec(memory_space=pl.ANY)
    count = sum(counts)
    return pl.pallas_call(
        functools.partial(product_kernel, sources, plain, counts),
        in_specs=[pl.BlockSpec(memory_space=pltpu.SMEM)] + [anywhere] * (len(blocks) + len(own) + 1),
        out_specs=pl.BlockSpec(memory_space=pltpu.VMEM),
        out_shape=jax.ShapeDtypeStruct((columns, own_rows), f32),
        scratch_shapes=[
            pltpu.VMEM((1 if plain else 2, count, columns, block), f32),
            pltpu.VMEM((count, parts, own_rows, block), f32),
            pltpu.VMEM((columns, parts * own_rows), f32),
            pltpu.SemaphoreType.DMA((3, count)),
        ],
        compiler_params=kernel_params(),
        cost_estimate=pl.CostEstimate(flops=6 * columns * parts * own_rows * full_rows, bytes_accessed=4 * matrix.size, transcendentals=0),
    )(order, *blocks, *own, matrix)


def swap(value, distance, size):
    return lax.ppermute(value, "tile", [(i, i ^ distance) for i in range(size)])


def solve_paired(reduced, diag_inverse, coupling, sources):
    chain_size = lax.axis_size("chain")
    tile_size = lax.axis_size("tile")
    layers = tile_size // 4
    me = lax.axis_index("tile")
    core, row, layer = me % 2, me // 2 % 2, me // 4
    chips = tile_size // 2
    groups = [[2 * chip + side for chip in range(chips)] for side in range(2)]
    mine = lax.all_gather(reduced, "tile", axis=0, tiled=False, axis_index_groups=groups)
    own = [mine, swap(mine, 1, tile_size)]
    chip_order = 2 * jnp.arange(chips, dtype=jnp.int32)
    order = jnp.concatenate([chip_order + core, chip_order + 1 - core])
    blocks, others = own, []
    layer_order = (layer - jnp.arange(layers, dtype=jnp.int32)) % layers * 4
    near = layer_order + row * 2
    far = layer_order + (1 - row) * 2
    hop_order = jnp.concatenate([near + core, far + core, near + 1 - core, far + 1 - core])
    for _ in range(chain_size - 1):
        carried = complex_apply(coupling, order, blocks, others, sources)
        arrived = []
        for by in range(layers):
            pairs = [
                (c * tile_size + t, (c + 1) * tile_size + (t + 4 * by) % tile_size)
                for c in range(chain_size - 1)
                for t in range(tile_size)
            ]
            arrived.append(lax.ppermute(carried, ("chain", "tile"), pairs))
        line = jnp.stack(arrived)
        across = swap(line, 2, tile_size)
        blocks = [line, across, swap(line, 1, tile_size), swap(across, 1, tile_size)]
        order, others = hop_order, own
    return complex_apply(diag_inverse, order, blocks, others, sources)


def solve_flat(reduced, diag_inverse, coupling, sources):
    chain_size = lax.axis_size("chain")
    columns = reduced.shape[0]
    full_rows = diag_inverse.shape[2]
    block = min(256, full_rows)
    order = jnp.arange(full_rows // block, dtype=jnp.int32)
    onward = [(i, i + 1) for i in range(chain_size - 1)]

    def gathered(value):
        whole = lax.all_gather(value, "tile", axis=1, tiled=True)
        return [whole.reshape(columns, -1, block).transpose(1, 0, 2)]

    current = reduced
    for _ in range(chain_size - 1):
        carried = complex_apply(coupling, order, gathered(current), [], sources)
        current = reduced - lax.ppermute(carried, "chain", onward)
    return complex_apply(diag_inverse, order, gathered(current), [], sources)


def body(right_side, diag_inverse, coupling, updates, update_rows, tile_counts):
    batches, halves, sources, own_rows = right_side.shape
    tile_size = lax.axis_size("tile")
    entries, columns = updates.shape
    tile_rows = entries // tile_counts.shape[0]
    cap = 2 * entries // tile_size
    slots = tile_size * cap
    width = -(-(columns + 1) // 128) * 128
    vmem = pl.BlockSpec(memory_space=pltpu.VMEM)
    smem = pl.BlockSpec(memory_space=pltpu.SMEM)
    packed = pl.pallas_call(
        functools.partial(pack_kernel, own_rows, cap, tile_rows),
        in_specs=[smem, vmem, vmem],
        out_specs=vmem,
        out_shape=jax.ShapeDtypeStruct((slots, width), f32),
        compiler_params=kernel_params(),
    )(tile_counts, update_rows[None, :], updates.T)
    received = lax.all_to_all(packed.reshape(tile_size, cap, width), "tile", 0, 0, tiled=False).reshape(slots, width)
    reduced = pl.pallas_call(
        reduce_kernel,
        in_specs=[vmem, vmem],
        out_specs=vmem,
        out_shape=jax.ShapeDtypeStruct((columns, own_rows), f32),
        compiler_params=kernel_params(),
    )(received, right_side.reshape(columns, own_rows))
    paired = own_rows % 128 == 0 and tile_size % 8 == 0
    solve = solve_paired if paired else solve_flat
    return solve(reduced, diag_inverse, coupling, sources).reshape(right_side.shape)


def solution(mesh):
    in_specs = (
        P(None, None, None, ("chain", "tile")),
        P(None, ("chain", "tile"), None),
        P(None, ("chain", "tile"), None),
        P(("chain", "tile"), None),
        P(("chain", "tile")),
        P(("chain", "tile")),
    )
    out_specs = P(None, None, None, ("chain", "tile"))
    return jax.shard_map(body, mesh=mesh, in_specs=in_specs, out_specs=out_specs, check_vma=False)
```

```python
import functools

import jax
import jax.numpy as jnp
from jax import lax
from jax.experimental import pallas as pl
from jax.experimental.pallas import tpu as pltpu
from jax.sharding import PartitionSpec as P

MIB = 1 << 20
f32 = jnp.float32
bf16 = jnp.bfloat16
lanes_contract = (((1,), (1,)), ((), ()))


def halves_of(value):
    high = value.astype(bf16)
    return high, (value - high.astype(f32)).astype(bf16)


def thirds_of(value):
    high = value.astype(bf16)
    rest = value - high.astype(f32)
    middle = rest.astype(bf16)
    return high, middle, (rest - middle.astype(f32)).astype(bf16)


def kernel_params():
    return pltpu.CompilerParams(vmem_limit_bytes=56 * MIB)


def pack_kernel(own_rows, cap, tile_rows, counts_ref, rows_ref, updates_ref, packed_ref):
    columns, entries = updates_ref.shape
    slots, width = packed_ref.shape
    entry = lax.broadcasted_iota(jnp.int32, (1, entries), 1)
    live = jnp.zeros((1, entries), jnp.bool_)
    for tile in range(entries // tile_rows):
        start = tile * tile_rows
        live = live | ((entry >= start) & (entry < start + counts_ref[tile]))
    rows = rows_ref[...]
    owner = rows // own_rows
    lane_owner = jnp.broadcast_to(owner.astype(f32), (entries, entries))
    earlier = lax.broadcasted_iota(jnp.int32, (entries, entries), 0) < lax.broadcasted_iota(jnp.int32, (entries, entries), 1)
    rank = jnp.sum(jnp.where(earlier & (lane_owner.T == lane_owner), 1, 0), axis=0, keepdims=True)
    slot = owner * cap + rank
    choose = jnp.where(lax.broadcasted_iota(jnp.int32, (slots, entries), 0) == slot, 1.0, 0.0).astype(bf16)
    data = jnp.where(live, updates_ref[...], 0.0)
    local_row = (rows - owner * own_rows).astype(f32)
    tail = jnp.where(lax.broadcasted_iota(jnp.int32, (width - columns, entries), 0) == 0, local_row, 0.0)
    data = jnp.concatenate([data, tail], axis=0)
    packed = jnp.zeros((slots, width), f32)
    for piece in thirds_of(data):
        packed += lax.dot_general(choose, piece, lanes_contract, preferred_element_type=f32)
    packed_ref[...] = packed


def reduce_kernel(received_ref, right_ref, *reduced_refs):
    slots = received_ref.shape[0]
    columns, own_rows = right_ref.shape
    received = received_ref[...]
    local_row = received[:, columns:columns + 1].astype(jnp.int32)
    place = jnp.where(lax.broadcasted_iota(jnp.int32, (slots, own_rows), 1) == local_row, 1.0, 0.0).astype(bf16)
    total = jnp.zeros((columns, own_rows), f32)
    for piece in thirds_of(received[:, :columns].T):
        total += jnp.dot(piece, place, preferred_element_type=f32)
    reduced = right_ref[...] - total
    start = 0
    for reduced_ref in reduced_refs:
        reduced_ref[...] = reduced[start:start + reduced_ref.shape[0]]
        start += reduced_ref.shape[0]


def split_kernel(k_ref, high_ref, low_ref):
    blocks, rows, block = high_ref.shape
    for i in range(blocks):
        high, low = halves_of(k_ref[:, :, i * block:(i + 1) * block].reshape(rows, block))
        high_ref[i] = high
        low_ref[i] = low


def split_blocks(matrix, block):
    parts, own_rows, full_rows = matrix.shape
    count = full_rows // block
    per_step = 4 if count % 4 == 0 else 1
    shape = jax.ShapeDtypeStruct((count, parts * own_rows, block), bf16)
    out_spec = pl.BlockSpec((per_step, parts * own_rows, block), lambda i: (i, 0, 0))
    return pl.pallas_call(
        split_kernel,
        grid=(count // per_step,),
        in_specs=[pl.BlockSpec((parts, own_rows, per_step * block), lambda i: (0, 0, i))],
        out_specs=[out_spec, out_spec],
        out_shape=[shape, shape],
        compiler_params=pltpu.CompilerParams(vmem_limit_bytes=12 * MIB),
        cost_estimate=pl.CostEstimate(flops=3 * matrix.size, bytes_accessed=8 * matrix.size, transcendentals=0),
    )(matrix)


def product_kernel(sources, layout, inputs, sets, order_ref, *refs):
    high_ref, low_ref = refs[inputs * sets:inputs * sets + 2]
    out_refs, total_ref = refs[inputs * sets + 2:-1], refs[-1]
    count, both_rows, block = high_ref.shape
    columns, own_rows = total_ref.shape[0], both_rows // 2
    per_step = 4 if count % 4 == 0 else 1

    def block_of(q):
        pieces = []
        for group in layout:
            which, place = group[q]
            value = refs[which][place]
            if sets == 2:
                value = refs[inputs + which][place] - value
            pieces.append(value)
        return jnp.concatenate(pieces, axis=0)

    for first in range(0, count, per_step):
        tiles = [order_ref[q] for q in range(first, first + per_step)]
        x_high, x_low = halves_of(jnp.concatenate([block_of(q) for q in range(first, first + per_step)], axis=1))
        k_high = jnp.concatenate([high_ref[tile] for tile in tiles], axis=1)
        k_low = jnp.concatenate([low_ref[tile] for tile in tiles], axis=1)
        both = lax.dot_general(jnp.concatenate([x_high, x_low], axis=0), k_high, lanes_contract, preferred_element_type=f32)
        part = both[:columns] + both[columns:] + lax.dot_general(x_high, k_low, lanes_contract, preferred_element_type=f32)
        if first == 0:
            total_ref[...] = part
        else:
            total_ref[...] += part
    start = 0
    for out_ref in out_refs:
        for first in range(0, out_ref.shape[0], 2 * sources):
            real = pl.ds(start + first, sources)
            imag = pl.ds(start + first + sources, sources)
            out_ref[first:first + sources, :] = total_ref[real, :own_rows] - total_ref[imag, own_rows:]
            out_ref[first + sources:first + 2 * sources, :] = total_ref[imag, :own_rows] + total_ref[real, own_rows:]
        start += out_ref.shape[0]


def complex_apply(split, order, layout, blocks, own, sources, shares):
    count, both_rows, block = split[0].shape
    vmem = pl.BlockSpec(memory_space=pltpu.VMEM)
    sets = 2 if own else 1
    arrays = list(blocks) + list(own)
    return pl.pallas_call(
        functools.partial(product_kernel, sources, layout, len(blocks), sets),
        in_specs=[pl.BlockSpec(memory_space=pltpu.SMEM)] + [vmem] * (len(arrays) + 2),
        out_specs=[vmem] * len(shares),
        out_shape=[jax.ShapeDtypeStruct((rows, both_rows // 2), f32) for rows in shares],
        scratch_shapes=[pltpu.VMEM((sum(shares), both_rows), f32)],
        compiler_params=pltpu.CompilerParams(vmem_limit_bytes=32 * MIB),
        cost_estimate=pl.CostEstimate(flops=6 * sum(shares) * both_rows * block * count, bytes_accessed=MIB, transcendentals=0),
    )(order, *arrays, *split)


def tied(value, to):
    return lax.optimization_barrier((value, to))[0]


def solve_paired(reduced, diag_inverse, coupling, sources):
    chain_size = lax.axis_size("chain")
    tile_size = lax.axis_size("tile")
    own_rows = reduced[0].shape[1]
    shares = [each.shape[0] for each in reduced]
    layers = tile_size // 4
    me = lax.axis_index("tile")
    core, row, layer = lax.rem(me, 2), lax.rem(lax.div(me, 2), 2), lax.div(me, 4)
    order = []
    for side in range(2):
        for across in range(2):
            for by in range(layers):
                from_layer = lax.rem(layer + layers - by, layers)
                from_row = row + across - 2 * row * across
                from_core = core + side - 2 * core * side
                order.append(from_layer * 4 + from_row * 2 + from_core)
    order = jnp.stack(order).astype(jnp.int32)
    places = [(side, across, by) for side in range(2) for across in range(2) for by in range(layers)]
    layout = [
        [(2 * side + across, (by,)) for side, across, by in places],
        [(4 + side, (by, across)) for side, across, by in places],
    ]

    def send(value, hop, target):
        if not hop:
            return lax.ppermute(value, "tile", [(t, target(t)) for t in range(tile_size)])
        pairs = [(c * tile_size + t, (c + 1) * tile_size + target(t)) for c in range(chain_size - 1) for t in range(tile_size)]
        return lax.ppermute(value, ("chain", "tile"), pairs)

    def gathered(first, second, hop, matrix):
        pair = [second if across == 0 and not hop else send(second, hop, lambda t: t ^ (2 * across)) for across in range(2)]
        line = [first if by == 0 and not hop else send(first, hop, lambda t: (t + 4 * by) % tile_size) for by in range(layers)]
        split = split_blocks(tied(matrix, first), own_rows)
        pair, line, split = lax.optimization_barrier((jnp.stack(pair), jnp.stack(line), split))
        far = send(line, False, lambda t: t ^ 2)
        rest = [pair if by == 0 else send(pair, False, lambda t: (t + 4 * by) % tile_size) for by in range(layers)]
        rest = jnp.stack(rest)
        held = [line, far]
        return held + [send(each, False, lambda t: t ^ 1) for each in held] + [rest, send(rest, False, lambda t: t ^ 1)], split

    own, split = gathered(*reduced, False, coupling if chain_size > 1 else diag_inverse)
    state, others = own, []
    coupling_split = split
    for step in range(chain_size - 1):
        carried = complex_apply(coupling_split, order, layout, state, others, sources, shares)
        state, split = gathered(*carried, True, diag_inverse if step == chain_size - 2 else coupling)
        others = own
    return complex_apply(split, order, layout, state, others, sources, [sum(shares)])[0]


def solve_flat(reduced, diag_inverse, coupling, sources):
    chain_size = lax.axis_size("chain")
    reduced = reduced[0]
    columns = reduced.shape[0]
    full_rows = diag_inverse.shape[2]
    block = min(256, full_rows)
    count = full_rows // block
    order = jnp.arange(count, dtype=jnp.int32)
    layout = [[(0, (q,)) for q in range(count)]]
    onward = [(i, i + 1) for i in range(chain_size - 1)]
    diag_split = split_blocks(diag_inverse, block)
    coupling_split = split_blocks(coupling, block)

    def gathered(value):
        whole = lax.all_gather(value, "tile", axis=1, tiled=True)
        return [whole.reshape(columns, count, block).transpose(1, 0, 2)]

    current = reduced
    for _ in range(chain_size - 1):
        carried = complex_apply(coupling_split, order, layout, gathered(current), [], sources, [columns])[0]
        current = reduced - lax.ppermute(carried, "chain", onward)
    return complex_apply(diag_split, order, layout, gathered(current), [], sources, [columns])[0]


def body(right_side, diag_inverse, coupling, updates, update_rows, tile_counts):
    batches, halves, sources, own_rows = right_side.shape
    tile_size = lax.axis_size("tile")
    entries, columns = updates.shape
    tile_rows = entries // tile_counts.shape[0]
    cap = 2 * entries // tile_size
    slots = tile_size * cap
    width = -(-(columns + 1) // 128) * 128
    vmem = pl.BlockSpec(memory_space=pltpu.VMEM)
    smem = pl.BlockSpec(memory_space=pltpu.SMEM)
    packed = pl.pallas_call(
        functools.partial(pack_kernel, own_rows, cap, tile_rows),
        in_specs=[smem, vmem, vmem],
        out_specs=vmem,
        out_shape=jax.ShapeDtypeStruct((slots, width), f32),
        compiler_params=kernel_params(),
    )(tile_counts, update_rows[None, :], updates.T)
    received = lax.all_to_all(packed.reshape(tile_size, cap, width), "tile", 0, 0, tiled=False).reshape(slots, width)
    paired = own_rows % 128 == 0 and tile_size % 8 == 0 and batches > 1
    early = batches * 2 // 3 * halves * sources
    shares = [early, columns - early] if paired else [columns]
    reduced = pl.pallas_call(
        reduce_kernel,
        in_specs=[vmem, vmem],
        out_specs=[vmem] * len(shares),
        out_shape=[jax.ShapeDtypeStruct((rows, own_rows), f32) for rows in shares],
        compiler_params=kernel_params(),
    )(received, right_side.reshape(columns, own_rows))
    solve = solve_paired if paired else solve_flat
    return solve(reduced, diag_inverse, coupling, sources).reshape(right_side.shape)


def solution(mesh):
    in_specs = (
        P(None, None, None, ("chain", "tile")),
        P(None, ("chain", "tile"), None),
        P(None, ("chain", "tile"), None),
        P(("chain", "tile"), None),
        P(("chain", "tile")),
        P(("chain", "tile")),
    )
    out_specs = P(None, None, None, ("chain", "tile"))
    return jax.shard_map(body, mesh=mesh, in_specs=in_specs, out_specs=out_specs, check_vma=False)
```

```python
import functools

import jax
import jax.numpy as jnp
from jax import lax
from jax.experimental import pallas as pl
from jax.experimental.pallas import tpu as pltpu
from jax.sharding import PartitionSpec as P

MIB = 1 << 20
f32 = jnp.float32
bf16 = jnp.bfloat16
lanes_contract = (((1,), (1,)), ((), ()))


def halves_of(value):
    high = value.astype(bf16)
    return high, (value - high.astype(f32)).astype(bf16)


def thirds_of(value):
    high = value.astype(bf16)
    rest = value - high.astype(f32)
    middle = rest.astype(bf16)
    return high, middle, (rest - middle.astype(f32)).astype(bf16)


def kernel_params():
    return pltpu.CompilerParams(vmem_limit_bytes=56 * MIB)


def pack_kernel(own_rows, cap, tile_rows, counts_hbm, rows_hbm, updates_hbm, packed_ref, counts_ref, rows_ref, updates_ref, sems):
    moves = [
        pltpu.make_async_copy(counts_hbm, counts_ref, sems.at[0]),
        pltpu.make_async_copy(rows_hbm, rows_ref, sems.at[1]),
        pltpu.make_async_copy(updates_hbm, updates_ref, sems.at[2]),
    ]
    for move in moves:
        move.start()
    columns, entries = updates_ref.shape
    owners, height, width = packed_ref.shape
    slots = owners * cap
    entry = lax.broadcasted_iota(jnp.int32, (1, entries), 1)
    earlier = lax.broadcasted_iota(jnp.int32, (entries, entries), 0) < lax.broadcasted_iota(jnp.int32, (entries, entries), 1)
    for move in moves:
        move.wait()
    live = jnp.zeros((1, entries), jnp.bool_)
    for tile in range(entries // tile_rows):
        start = tile * tile_rows
        live = live | ((entry >= start) & (entry < start + counts_ref[tile]))
    rows = rows_ref[...]
    owner = rows // own_rows
    lane_owner = jnp.broadcast_to(owner.astype(f32), (entries, entries))
    rank = jnp.sum(jnp.where(earlier & (lane_owner.T == lane_owner), 1, 0), axis=0, keepdims=True)
    slot = owner * cap + rank
    choose = jnp.where(lax.broadcasted_iota(jnp.int32, (slots, entries), 0) == slot, 1.0, 0.0).astype(bf16)
    data = jnp.where(live, updates_ref[...], 0.0)
    local_row = (rows - owner * own_rows).astype(f32)
    folded = height > cap
    if not folded:
        tail = jnp.where(lax.broadcasted_iota(jnp.int32, (width - columns, entries), 0) == 0, local_row, 0.0)
        data = jnp.concatenate([data, tail], axis=0)
    packed = jnp.zeros((slots, data.shape[0]), f32)
    for piece in thirds_of(data):
        packed += lax.dot_general(choose, piece, lanes_contract, preferred_element_type=f32)
    packed = packed.reshape(owners, cap, data.shape[0])
    if not folded:
        packed_ref[...] = packed
        return
    half = cap // 2
    packed_ref[:, :cap, :] = packed[:, :, :width]
    packed_ref[:, cap:cap + half, :] = jnp.concatenate([packed[:, :half, width:], packed[:, half:, width:]], axis=2)
    first = lax.axis_index("tile") * cap
    by_owner = jnp.where(lax.broadcasted_iota(jnp.int32, (owners, entries), 0) == owner, local_row, 0.0).astype(bf16)
    by_lane = jnp.where(lax.broadcasted_iota(jnp.int32, (width, entries), 0) == first % width + rank, 1.0, 0.0).astype(bf16)
    numbers = lax.dot_general(by_owner, by_lane, lanes_contract, preferred_element_type=f32)
    line = lax.broadcasted_iota(jnp.int32, (owners, 8, width), 1)
    packed_ref[:, cap + half:, :] = jnp.where(line == first // width, numbers[:, None, :], 0.0)


def reduce_kernel(cap, received_ref, right_hbm, *refs):
    reduced_refs, right_ref, sem = refs[:-2], refs[-2], refs[-1]
    move = pltpu.make_async_copy(right_hbm, right_ref, sem)
    move.start()
    owners, height, width = received_ref.shape
    slots = owners * cap
    columns, own_rows = right_ref.shape
    if height > cap:
        half = cap // 2
        numbers = jnp.sum(received_ref[:, cap + half:, :], axis=0)
        numbers = jnp.concatenate([numbers[i:i + 1] for i in range(slots // width)], axis=1).astype(jnp.int32)
        rest = received_ref[:, cap:cap + half, :]
        rest = jnp.concatenate([rest[:, :, :width // 2], rest[:, :, width // 2:]], axis=1)
        sets = [received_ref[:, :cap, :].reshape(slots, width), rest.reshape(slots, width // 2)]
        place = jnp.where(lax.broadcasted_iota(jnp.int32, (own_rows, slots), 0) == numbers, 1.0, 0.0).astype(bf16)
        totals = []
        for value in sets:
            total = jnp.zeros((own_rows, value.shape[1]), f32)
            for piece in thirds_of(value):
                total += jnp.dot(place, piece, preferred_element_type=f32)
            totals.append(total.T)
        total = jnp.concatenate(totals, axis=0)
    else:
        received = received_ref[...].reshape(slots, width)
        local_row = received[:, columns:columns + 1].astype(jnp.int32)
        place = jnp.where(lax.broadcasted_iota(jnp.int32, (slots, own_rows), 1) == local_row, 1.0, 0.0).astype(bf16)
        total = jnp.zeros((columns, own_rows), f32)
        for piece in thirds_of(received[:, :columns].T):
            total += jnp.dot(piece, place, preferred_element_type=f32)
    move.wait()
    start = 0
    for reduced_ref in reduced_refs:
        rows = reduced_ref.shape[0]
        reduced_ref[...] = right_ref[start:start + rows, :] - total[start:start + rows]
        start += rows


def split_kernel(matrix_ref, high_ref, low_ref):
    parts, own_rows, full_rows = matrix_ref.shape
    blocks, rows, block = high_ref.shape
    height = 64
    for part in range(parts):
        for first in range(0, own_rows, height):
            for j in range(blocks):
                high, low = halves_of(matrix_ref[part, first:first + height, j * block:(j + 1) * block])
                start = part * own_rows + first
                high_ref[j, start:start + height, :] = high
                low_ref[j, start:start + height, :] = low


def split_blocks(matrix, block):
    parts, own_rows, full_rows = matrix.shape
    count = full_rows // block
    vmem = pl.BlockSpec(memory_space=pltpu.VMEM)
    shape = jax.ShapeDtypeStruct((count, parts * own_rows, block), bf16)
    return pl.pallas_call(
        split_kernel,
        in_specs=[vmem],
        out_specs=[vmem, vmem],
        out_shape=[shape, shape],
        compiler_params=pltpu.CompilerParams(vmem_limit_bytes=20 * MIB),
        cost_estimate=pl.CostEstimate(flops=3 * matrix.size, bytes_accessed=8 * matrix.size, transcendentals=0),
    )(matrix)


def tile_of(q, size):
    me = lax.axis_index("tile")
    layers = size // 4
    side, across, by = q // (2 * layers), q // layers % 2, q % layers
    layer = lax.rem(lax.div(me, 4) + (layers - by), layers)
    row = lax.rem(lax.div(me, 2) + across, 2)
    core = lax.rem(me + side, 2)
    return layer * 4 + row * 2 + core


def product_kernel(sources, layout, inputs, sets, begin, end, finish, onward, relative, *refs):
    high_ref, low_ref = refs[inputs * sets:inputs * sets + 2]
    rest = refs[inputs * sets + 2:]
    count, both_rows, block = high_ref.shape
    own_rows = both_rows // 2
    start_ref, rest = (rest[0], rest[1:]) if begin > 0 else (None, rest)
    out_refs, total_ref = (rest[:-1], rest[-1]) if finish else ((), rest[0])
    columns = total_ref.shape[0]
    per_step = 4 if (end - begin) % 4 == 0 else 1

    def block_of(q):
        pieces = []
        for group in layout:
            which, place = group[q]
            value = refs[which][place]
            if sets == 2:
                value = refs[inputs + which][place] - value
            pieces.append(value)
        return jnp.concatenate(pieces, axis=0)

    @pl.when(jnp.logical_not(onward) | (lax.axis_index("chain") < lax.axis_size("chain") - 1))
    def _():
        for first in range(begin, end, per_step):
            tiles = [tile_of(q, count) if relative else q for q in range(first, first + per_step)]
            x_high, x_low = halves_of(jnp.concatenate([block_of(q) for q in range(first, first + per_step)], axis=1))
            k_high = jnp.concatenate([high_ref[tile] for tile in tiles], axis=1)
            k_low = jnp.concatenate([low_ref[tile] for tile in tiles], axis=1)
            both = lax.dot_general(jnp.concatenate([x_high, x_low], axis=0), k_high, lanes_contract, preferred_element_type=f32)
            part = both[:columns] + both[columns:] + lax.dot_general(x_high, k_low, lanes_contract, preferred_element_type=f32)
            if first > begin:
                total_ref[...] += part
            elif start_ref is None:
                total_ref[...] = part
            else:
                total_ref[...] = start_ref[...] + part
        start = 0
        for out_ref in out_refs:
            for first in range(0, out_ref.shape[0], 2 * sources):
                real = pl.ds(start + first, sources)
                imag = pl.ds(start + first + sources, sources)
                out_ref[first:first + sources, :] = total_ref[real, :own_rows] - total_ref[imag, own_rows:]
                out_ref[first + sources:first + 2 * sources, :] = total_ref[imag, :own_rows] + total_ref[real, own_rows:]
            start += out_ref.shape[0]


def product_part(split, onward, layout, blocks, own, begin, end, started, sources, shares):
    count, both_rows, block = split[0].shape
    vmem = pl.BlockSpec(memory_space=pltpu.VMEM)
    finish = end == count
    whole = (sum(shares), both_rows)
    arrays = list(blocks) + list(own) + list(split) + ([] if started is None else [started])
    if finish:
        out_shape = [jax.ShapeDtypeStruct((rows, both_rows // 2), f32) for rows in shares]
    else:
        out_shape = jax.ShapeDtypeStruct(whole, f32)
    return pl.pallas_call(
        functools.partial(product_kernel, sources, layout, len(blocks), 2 if own else 1, begin, end, finish, onward, len(layout) > 1),
        in_specs=[vmem] * len(arrays),
        out_specs=[vmem] * len(shares) if finish else vmem,
        out_shape=out_shape,
        scratch_shapes=[pltpu.VMEM(whole, f32)] if finish else [],
        compiler_params=pltpu.CompilerParams(vmem_limit_bytes=20 * MIB),
        cost_estimate=pl.CostEstimate(flops=6 * sum(shares) * both_rows * block * (end - begin), bytes_accessed=MIB, transcendentals=0),
    )(*arrays)


def tied(value, to):
    return lax.optimization_barrier((value, to))[0]


def solve_paired(reduced, diag_inverse, coupling, sources):
    chain_size = lax.axis_size("chain")
    tile_size = lax.axis_size("tile")
    own_rows = reduced[0].shape[1]
    shares = [each.shape[0] for each in reduced]
    layers = tile_size // 4
    count = tile_size
    places = [(side, across, by) for side in range(2) for across in range(2) for by in range(layers)]

    def send(value, hop, target):
        if not hop:
            return lax.ppermute(value, "tile", [(t, target(t)) for t in range(tile_size)])
        pairs = [(c * tile_size + t, (c + 1) * tile_size + target(t)) for c in range(chain_size - 1) for t in range(tile_size)]
        return lax.ppermute(value, ("chain", "tile"), pairs)

    def first_stage(first, second, hop):
        pair = [second if across == 0 and not hop else send(second, hop, lambda t: t ^ (2 * across)) for across in range(2)]
        line = [first if by == 0 and not hop else send(first, hop, lambda t: (t + 4 * by) % tile_size) for by in range(layers)]
        return jnp.stack(pair), jnp.stack(line)

    def second_stage(pair, line):
        far = send(line, False, lambda t: t ^ 2)
        rest = [pair if by == 0 else send(pair, False, lambda t: (t + 4 * by) % tile_size) for by in range(layers)]
        return [line, far, jnp.stack(rest)]

    layout = [
        [(across, (by,)) for side, across, by in places],
        [(2, (by, across)) for side, across, by in places],
    ]

    def products(split, onward, held, own, shares):
        other = [send(each, False, lambda t: t ^ 1) for each in held]
        mine, theirs = own if own else ([], [])
        started = product_part(split, onward, layout, held, mine, 0, count // 2, None, sources, shares)
        return product_part(split, onward, layout, other, theirs, count // 2, count, started, sources, shares), other

    only = chain_size == 1
    pair, line = first_stage(*reduced, False)
    split = split_blocks(tied(diag_inverse if only else coupling, reduced[0]), own_rows)
    pair, line, split = lax.optimization_barrier((pair, line, split))
    held = second_stage(pair, line)
    if only:
        return products(split, False, held, None, [sum(shares)])[0][0]
    diag_split = split_blocks(tied(diag_inverse, line), own_rows)
    held[1], held[2], diag_split = lax.optimization_barrier((held[1], held[2], diag_split))
    carried, other = products(split, True, held, None, shares)
    own = (held, other)
    for step in range(chain_size - 1):
        held = second_stage(*lax.optimization_barrier(first_stage(*carried, True)))
        if step < chain_size - 2:
            carried = products(split, True, held, own, shares)[0]
    return products(diag_split, False, held, own, [sum(shares)])[0][0]


def solve_flat(reduced, diag_inverse, coupling, sources):
    chain_size = lax.axis_size("chain")
    reduced = reduced[0]
    columns = reduced.shape[0]
    full_rows = diag_inverse.shape[2]
    block = min(256, full_rows)
    count = full_rows // block
    layout = [[(0, (q,)) for q in range(count)]]
    onward = [(i, i + 1) for i in range(chain_size - 1)]
    diag_split = split_blocks(diag_inverse, block)
    coupling_split = split_blocks(coupling, block)

    def gathered(value):
        whole = lax.all_gather(value, "tile", axis=1, tiled=True)
        return [whole.reshape(columns, count, block).transpose(1, 0, 2)]

    current = reduced
    for _ in range(chain_size - 1):
        carried = product_part(coupling_split, True, layout, gathered(current), [], 0, count, None, sources, [columns])[0]
        current = reduced - lax.ppermute(carried, "chain", onward)
    return product_part(diag_split, False, layout, gathered(current), [], 0, count, None, sources, [columns])[0]


def body(right_side, diag_inverse, coupling, updates, update_rows, tile_counts):
    batches, halves, sources, own_rows = right_side.shape
    tile_size = lax.axis_size("tile")
    entries, columns = updates.shape
    tile_rows = entries // tile_counts.shape[0]
    cap = 2 * entries // tile_size
    slots = tile_size * cap
    vmem = pl.BlockSpec(memory_space=pltpu.VMEM)
    hbm = pl.BlockSpec(memory_space=pltpu.HBM)
    folded = cap % 16 == 0 and slots <= 1024 and columns == 192 and own_rows <= 256 and 128 % cap == 0
    width = 128 if folded else -(-(columns + 1) // 128) * 128
    height = cap + cap // 2 + 8 if folded else cap
    packed = pl.pallas_call(
        functools.partial(pack_kernel, own_rows, cap, tile_rows),
        in_specs=[hbm, hbm, hbm],
        out_specs=vmem,
        out_shape=jax.ShapeDtypeStruct((tile_size, height, width), f32),
        scratch_shapes=[
            pltpu.SMEM(tile_counts.shape, jnp.int32),
            pltpu.VMEM((1, entries), jnp.int32),
            pltpu.VMEM((columns, entries), f32),
            pltpu.SemaphoreType.DMA((3,)),
        ],
        compiler_params=kernel_params(),
    )(tile_counts, update_rows[None, :], updates.T)
    received = lax.all_to_all(packed, "tile", 0, 0, tiled=False)
    paired = own_rows % 128 == 0 and tile_size % 8 == 0 and batches > 1
    early = batches * 2 // 3 * halves * sources
    shares = [early, columns - early] if paired else [columns]
    reduced = pl.pallas_call(
        functools.partial(reduce_kernel, cap),
        in_specs=[vmem, hbm],
        out_specs=[vmem] * len(shares),
        out_shape=[jax.ShapeDtypeStruct((rows, own_rows), f32) for rows in shares],
        scratch_shapes=[pltpu.VMEM((columns, own_rows), f32), pltpu.SemaphoreType.DMA(())],
        compiler_params=kernel_params(),
    )(received, right_side.reshape(columns, own_rows))
    solve = solve_paired if paired else solve_flat
    return solve(reduced, diag_inverse, coupling, sources).reshape(right_side.shape)


def solution(mesh):
    in_specs = (
        P(None, None, None, ("chain", "tile")),
        P(None, ("chain", "tile"), None),
        P(None, ("chain", "tile"), None),
        P(("chain", "tile"), None),
        P(("chain", "tile")),
        P(("chain", "tile")),
    )
    out_specs = P(None, None, None, ("chain", "tile"))
    return jax.shard_map(body, mesh=mesh, in_specs=in_specs, out_specs=out_specs, check_vma=False)
```

```python
import functools

import jax
import jax.numpy as jnp
from jax import lax
from jax.experimental import pallas as pl
from jax.experimental.pallas import tpu as pltpu
from jax.sharding import PartitionSpec as P

MIB = 1 << 20
f32 = jnp.float32
bf16 = jnp.bfloat16
lanes_contract = (((1,), (1,)), ((), ()))


def halves_of(value):
    high = value.astype(bf16)
    return high, (value - high.astype(f32)).astype(bf16)


def thirds_of(value):
    high = value.astype(bf16)
    rest = value - high.astype(f32)
    middle = rest.astype(bf16)
    return high, middle, (rest - middle.astype(f32)).astype(bf16)


def kernel_params(size):
    return pltpu.CompilerParams(vmem_limit_bytes=size * MIB)


def pack_kernel(own_rows, cap, tile_rows, folded, counts_hbm, rows_hbm, updates_hbm, *refs):
    packed_refs, (counts_ref, rows_ref, updates_ref, sems) = refs[:-4], refs[-4:]
    moves = [
        pltpu.make_async_copy(counts_hbm, counts_ref, sems.at[0]),
        pltpu.make_async_copy(rows_hbm, rows_ref, sems.at[1]),
        pltpu.make_async_copy(updates_hbm, updates_ref, sems.at[2]),
    ]
    for move in moves:
        move.start()
    columns, entries = updates_ref.shape
    owners = lax.axis_size("tile")
    width = packed_refs[0].shape[-1]
    slots = owners * cap
    entry = lax.broadcasted_iota(jnp.int32, (1, entries), 1)
    earlier = lax.broadcasted_iota(jnp.int32, (entries, entries), 0) < lax.broadcasted_iota(jnp.int32, (entries, entries), 1)
    for move in moves:
        move.wait()
    live = jnp.zeros((1, entries), jnp.bool_)
    for tile in range(entries // tile_rows):
        start = tile * tile_rows
        live = live | ((entry >= start) & (entry < start + counts_ref[tile]))
    rows = rows_ref[...]
    owner = rows // own_rows
    local_row = (rows - owner * own_rows).astype(f32)
    if folded:
        owner = owner ^ lax.axis_index("tile")
    lane_owner = jnp.broadcast_to(owner.astype(f32), (entries, entries))
    rank = jnp.sum(jnp.where(earlier & (lane_owner.T == lane_owner), 1, 0), axis=0, keepdims=True)
    slot = owner * cap + rank
    choose = jnp.where(lax.broadcasted_iota(jnp.int32, (slots, entries), 0) == slot, 1.0, 0.0).astype(bf16)
    data = jnp.where(live, updates_ref[...], 0.0)
    if not folded:
        tail = jnp.where(lax.broadcasted_iota(jnp.int32, (width - columns, entries), 0) == 0, local_row, 0.0)
        data = jnp.concatenate([data, tail], axis=0)
    packed = jnp.zeros((slots, data.shape[0]), f32)
    for piece in thirds_of(data):
        packed += lax.dot_general(choose, piece, lanes_contract, preferred_element_type=f32)
    packed = packed.reshape(owners, cap, data.shape[0])
    if not folded:
        packed_refs[0][...] = packed
        return
    half = cap // 2
    by_owner = jnp.where(lax.broadcasted_iota(jnp.int32, (owners, entries), 0) == owner, local_row, 0.0).astype(bf16)
    by_lane = jnp.where(lax.broadcasted_iota(jnp.int32, (width, entries), 0) == lax.rem(slot, width), 1.0, 0.0).astype(bf16)
    numbers = lax.dot_general(by_owner, by_lane, lanes_contract, preferred_element_type=f32)
    line = lax.broadcasted_iota(jnp.int32, (8, width), 0)
    for i, packed_ref in enumerate(packed_refs):
        packed_ref[:cap, :] = packed[i, :, :width]
        packed_ref[cap:cap + half, :] = jnp.concatenate([packed[i, :half, width:], packed[i, half:, width:]], axis=1)
        packed_ref[cap + half:, :] = jnp.where(line == i * cap // width, numbers[i:i + 1], 0.0)


def reduce_kernel(cap, inputs, right_hbm, *refs):
    received_refs, reduced_refs, right_ref, sem = refs[:inputs], refs[inputs:-2], refs[-2], refs[-1]
    move = pltpu.make_async_copy(right_hbm, right_ref, sem)
    move.start()
    columns, own_rows = right_ref.shape
    if inputs > 1:
        slots = inputs * cap
        half = cap // 2
        width = received_refs[0].shape[1]
        numbers = received_refs[0][cap + half:, :]
        for ref in received_refs[1:]:
            numbers += ref[cap + half:, :]
        numbers = jnp.concatenate([numbers[i:i + 1] for i in range(slots // width)], axis=1).astype(jnp.int32)
        rest = []
        for ref in received_refs:
            rest += [ref[cap:cap + half, :width // 2], ref[cap:cap + half, width // 2:]]
        sets = [jnp.concatenate([ref[:cap, :] for ref in received_refs], axis=0), jnp.concatenate(rest, axis=0)]
        place = jnp.where(lax.broadcasted_iota(jnp.int32, (own_rows, slots), 0) == numbers, 1.0, 0.0).astype(bf16)
        totals = []
        for value in sets:
            total = jnp.zeros((own_rows, value.shape[1]), f32)
            for piece in thirds_of(value):
                total += jnp.dot(place, piece, preferred_element_type=f32)
            totals.append(total.T)
        total = jnp.concatenate(totals, axis=0)
    else:
        owners, height, width = received_refs[0].shape
        slots = owners * height
        received = received_refs[0][...].reshape(slots, width)
        local_row = received[:, columns:columns + 1].astype(jnp.int32)
        place = jnp.where(lax.broadcasted_iota(jnp.int32, (slots, own_rows), 1) == local_row, 1.0, 0.0).astype(bf16)
        total = jnp.zeros((columns, own_rows), f32)
        for piece in thirds_of(received[:, :columns].T):
            total += jnp.dot(piece, place, preferred_element_type=f32)
    move.wait()
    start = 0
    for reduced_ref in reduced_refs:
        rows = reduced_ref.shape[0]
        reduced_ref[...] = right_ref[start:start + rows, :] - total[start:start + rows]
        start += rows


def split_kernel(matrix_ref, high_ref, low_ref):
    parts, own_rows, full_rows = matrix_ref.shape
    blocks, rows, block = high_ref.shape
    height = 64
    for part in range(parts):
        for first in range(0, own_rows, height):
            for j in range(blocks):
                high, low = halves_of(matrix_ref[part, first:first + height, j * block:(j + 1) * block])
                start = part * own_rows + first
                high_ref[j, start:start + height, :] = high
                low_ref[j, start:start + height, :] = low


def split_blocks(matrix, block):
    parts, own_rows, full_rows = matrix.shape
    count = full_rows // block
    vmem = pl.BlockSpec(memory_space=pltpu.VMEM)
    shape = jax.ShapeDtypeStruct((count, parts * own_rows, block), bf16)
    return pl.pallas_call(
        split_kernel,
        in_specs=[vmem],
        out_specs=[vmem, vmem],
        out_shape=[shape, shape],
        compiler_params=kernel_params(20),
        cost_estimate=pl.CostEstimate(flops=3 * matrix.size, bytes_accessed=8 * matrix.size, transcendentals=0),
    )(matrix)


def tile_of(q, size):
    me = lax.axis_index("tile")
    layers = size // 4
    side, across, by = q // (2 * layers), q // layers % 2, q % layers
    layer = lax.rem(lax.div(me, 4) + (layers - by), layers)
    row = lax.rem(lax.div(me, 2) + across, 2)
    core = lax.rem(me + side, 2)
    return layer * 4 + row * 2 + core


def product_kernel(sources, layout, inputs, sets, begin, end, finish, onward, relative, *refs):
    high_ref, low_ref = refs[inputs * sets:inputs * sets + 2]
    rest = refs[inputs * sets + 2:]
    count, both_rows, block = high_ref.shape
    own_rows = both_rows // 2
    start_ref, rest = (rest[0], rest[1:]) if begin > 0 else (None, rest)
    out_refs, total_ref = (rest[:-1], rest[-1]) if finish else ((), rest[0])
    columns = total_ref.shape[0]
    per_step = 4 if (end - begin) % 4 == 0 else 1

    def block_of(q):
        pieces = []
        for group in layout:
            which, place = group[q]
            value = refs[which][place]
            if sets == 2:
                value = refs[inputs + which][place] - value
            pieces.append(value)
        return jnp.concatenate(pieces, axis=0)

    @pl.when(jnp.logical_not(onward) | (lax.axis_index("chain") < lax.axis_size("chain") - 1))
    def _():
        for first in range(begin, end, per_step):
            tiles = [tile_of(q, count) if relative else q for q in range(first, first + per_step)]
            x_high, x_low = halves_of(jnp.concatenate([block_of(q) for q in range(first, first + per_step)], axis=1))
            k_high = jnp.concatenate([high_ref[tile] for tile in tiles], axis=1)
            k_low = jnp.concatenate([low_ref[tile] for tile in tiles], axis=1)
            both = lax.dot_general(jnp.concatenate([x_high, x_low], axis=0), k_high, lanes_contract, preferred_element_type=f32)
            part = both[:columns] + both[columns:] + lax.dot_general(x_high, k_low, lanes_contract, preferred_element_type=f32)
            if first > begin:
                total_ref[...] += part
            elif start_ref is None:
                total_ref[...] = part
            else:
                total_ref[...] = start_ref[...] + part
        start = 0
        for out_ref in out_refs:
            for first in range(0, out_ref.shape[0], 2 * sources):
                real = pl.ds(start + first, sources)
                imag = pl.ds(start + first + sources, sources)
                out_ref[first:first + sources, :] = total_ref[real, :own_rows] - total_ref[imag, own_rows:]
                out_ref[first + sources:first + 2 * sources, :] = total_ref[imag, :own_rows] + total_ref[real, own_rows:]
            start += out_ref.shape[0]


def product_part(split, onward, layout, blocks, own, begin, end, started, sources, shares):
    count, both_rows, block = split[0].shape
    vmem = pl.BlockSpec(memory_space=pltpu.VMEM)
    finish = end == count
    whole = (sum(shares), both_rows)
    arrays = list(blocks) + list(own) + list(split) + ([] if started is None else [started])
    if finish:
        out_shape = [jax.ShapeDtypeStruct((rows, both_rows // 2), f32) for rows in shares]
    else:
        out_shape = jax.ShapeDtypeStruct(whole, f32)
    return pl.pallas_call(
        functools.partial(product_kernel, sources, layout, len(blocks), 2 if own else 1, begin, end, finish, onward, len(layout) > 1),
        in_specs=[vmem] * len(arrays),
        out_specs=[vmem] * len(shares) if finish else vmem,
        out_shape=out_shape,
        scratch_shapes=[pltpu.VMEM(whole, f32)] if finish else [],
        compiler_params=kernel_params(20),
        cost_estimate=pl.CostEstimate(flops=6 * sum(shares) * both_rows * block * (end - begin), bytes_accessed=MIB, transcendentals=0),
    )(*arrays)


def tied(value, to):
    return lax.optimization_barrier((value, to))[0]


def solve_paired(reduced, diag_inverse, coupling, sources):
    chain_size = lax.axis_size("chain")
    tile_size = lax.axis_size("tile")
    own_rows = reduced[0].shape[1]
    shares = [each.shape[0] for each in reduced]
    layers = tile_size // 4
    count = tile_size
    places = [(side, across, by) for side in range(2) for across in range(2) for by in range(layers)]

    def send(value, hop, target):
        if not hop:
            return lax.ppermute(value, "tile", [(t, target(t)) for t in range(tile_size)])
        pairs = [(c * tile_size + t, (c + 1) * tile_size + target(t)) for c in range(chain_size - 1) for t in range(tile_size)]
        return lax.ppermute(value, ("chain", "tile"), pairs)

    def first_stage(first, second, hop):
        pair = [second if across == 0 and not hop else send(second, hop, lambda t: t ^ (2 * across)) for across in range(2)]
        line = [first if by == 0 and not hop else send(first, hop, lambda t: (t + 4 * by) % tile_size) for by in range(layers)]
        return jnp.stack(pair), jnp.stack(line)

    def second_stage(pair, line):
        far = send(line, False, lambda t: t ^ 2)
        rest = [pair if by == 0 else send(pair, False, lambda t: (t + 4 * by) % tile_size) for by in range(layers)]
        return [line, far, jnp.stack(rest)]

    layout = [
        [(across, (by,)) for side, across, by in places],
        [(2, (by, across)) for side, across, by in places],
    ]

    def products(split, onward, held, own, shares):
        other = [send(each, False, lambda t: t ^ 1) for each in held]
        mine, theirs = own if own else ([], [])
        started = product_part(split, onward, layout, held, mine, 0, count // 2, None, sources, shares)
        return product_part(split, onward, layout, other, theirs, count // 2, count, started, sources, shares), other

    only = chain_size == 1
    pair, line = first_stage(*reduced, False)
    split = split_blocks(tied(diag_inverse if only else coupling, reduced[0]), own_rows)
    pair, line, split = lax.optimization_barrier((pair, line, split))
    held = second_stage(pair, line)
    if only:
        return products(split, False, held, None, [sum(shares)])[0][0]
    diag_split = split_blocks(tied(diag_inverse, line), own_rows)
    held[1], held[2], diag_split = lax.optimization_barrier((held[1], held[2], diag_split))
    carried, other = products(split, True, held, None, shares)
    own = (held, other)
    for step in range(chain_size - 1):
        held = second_stage(*lax.optimization_barrier(first_stage(*carried, True)))
        if step < chain_size - 2:
            carried = products(split, True, held, own, shares)[0]
    return products(diag_split, False, held, own, [sum(shares)])[0][0]


def solve_flat(reduced, diag_inverse, coupling, sources):
    chain_size = lax.axis_size("chain")
    reduced = reduced[0]
    columns = reduced.shape[0]
    full_rows = diag_inverse.shape[2]
    block = min(256, full_rows)
    count = full_rows // block
    layout = [[(0, (q,)) for q in range(count)]]
    onward = [(i, i + 1) for i in range(chain_size - 1)]
    diag_split = split_blocks(diag_inverse, block)
    coupling_split = split_blocks(coupling, block)

    def gathered(value):
        whole = lax.all_gather(value, "tile", axis=1, tiled=True)
        return [whole.reshape(columns, count, block).transpose(1, 0, 2)]

    current = reduced
    for _ in range(chain_size - 1):
        carried = product_part(coupling_split, True, layout, gathered(current), [], 0, count, None, sources, [columns])[0]
        current = reduced - lax.ppermute(carried, "chain", onward)
    return product_part(diag_split, False, layout, gathered(current), [], 0, count, None, sources, [columns])[0]


def body(right_side, diag_inverse, coupling, updates, update_rows, tile_counts):
    batches, halves, sources, own_rows = right_side.shape
    tile_size = lax.axis_size("tile")
    entries, columns = updates.shape
    tile_rows = entries // tile_counts.shape[0]
    cap = 2 * entries // tile_size
    slots = tile_size * cap
    vmem = pl.BlockSpec(memory_space=pltpu.VMEM)
    hbm = pl.BlockSpec(memory_space=pltpu.HBM)
    folded = cap % 16 == 0 and slots <= 1024 and columns == 192 and own_rows <= 256 and 128 % cap == 0
    folded = folded and tile_size & (tile_size - 1) == 0
    if folded:
        packed_shape = [jax.ShapeDtypeStruct((cap + cap // 2 + 8, 128), f32)] * tile_size
    else:
        packed_shape = [jax.ShapeDtypeStruct((tile_size, cap, -(-(columns + 1) // 128) * 128), f32)]
    packed = pl.pallas_call(
        functools.partial(pack_kernel, own_rows, cap, tile_rows, folded),
        in_specs=[hbm, hbm, hbm],
        out_specs=[vmem] * len(packed_shape),
        out_shape=packed_shape,
        scratch_shapes=[
            pltpu.SMEM(tile_counts.shape, jnp.int32),
            pltpu.VMEM((1, entries), jnp.int32),
            pltpu.VMEM((columns, entries), f32),
            pltpu.SemaphoreType.DMA((3,)),
        ],
        compiler_params=kernel_params(56),
    )(tile_counts, update_rows[None, :], updates.T)
    if folded:
        received = [packed[0]]
        for by in range(1, tile_size):
            received.append(lax.ppermute(packed[by], "tile", [(t, t ^ by) for t in range(tile_size)]))
    else:
        received = [lax.all_to_all(packed[0], "tile", 0, 0, tiled=False)]
    paired = own_rows % 128 == 0 and tile_size % 8 == 0 and batches > 1
    early = batches * 2 // 3 * halves * sources
    shares = [early, columns - early] if paired else [columns]
    reduced = pl.pallas_call(
        functools.partial(reduce_kernel, cap, len(received)),
        in_specs=[hbm] + [vmem] * len(received),
        out_specs=[vmem] * len(shares),
        out_shape=[jax.ShapeDtypeStruct((rows, own_rows), f32) for rows in shares],
        scratch_shapes=[pltpu.VMEM((columns, own_rows), f32), pltpu.SemaphoreType.DMA(())],
        compiler_params=kernel_params(20),
    )(right_side.reshape(columns, own_rows), *received)
    solve = solve_paired if paired else solve_flat
    return solve(reduced, diag_inverse, coupling, sources).reshape(right_side.shape)


def solution(mesh):
    in_specs = (
        P(None, None, None, ("chain", "tile")),
        P(None, ("chain", "tile"), None),
        P(None, ("chain", "tile"), None),
        P(("chain", "tile"), None),
        P(("chain", "tile")),
        P(("chain", "tile")),
    )
    out_specs = P(None, None, None, ("chain", "tile"))
    return jax.shard_map(body, mesh=mesh, in_specs=in_specs, out_specs=out_specs, check_vma=False)
```

```python
import functools

import jax
import jax.numpy as jnp
from jax import lax
from jax.experimental import pallas as pl
from jax.experimental.pallas import tpu as pltpu
from jax.sharding import PartitionSpec as P

MIB = 1 << 20
f32 = jnp.float32
bf16 = jnp.bfloat16
lanes_contract = (((1,), (1,)), ((), ()))


def halves_of(value):
    high = value.astype(bf16)
    return high, (value - high.astype(f32)).astype(bf16)


def thirds_of(value):
    high = value.astype(bf16)
    rest = value - high.astype(f32)
    middle = rest.astype(bf16)
    return high, middle, (rest - middle.astype(f32)).astype(bf16)


def kernel_params(size):
    return pltpu.CompilerParams(vmem_limit_bytes=int(size * MIB))


def pack_kernel(own_rows, cap, tile_rows, counts_hbm, rows_hbm, updates_hbm, packed_ref, counts_ref, rows_ref, updates_ref, sems):
    moves = [
        pltpu.make_async_copy(counts_hbm, counts_ref, sems.at[0]),
        pltpu.make_async_copy(rows_hbm, rows_ref, sems.at[1]),
        pltpu.make_async_copy(updates_hbm, updates_ref, sems.at[2]),
    ]
    for move in moves:
        move.start()
    columns, entries = updates_ref.shape
    owners, height, width = packed_ref.shape
    slots = owners * cap
    entry = lax.broadcasted_iota(jnp.int32, (1, entries), 1)
    earlier = lax.broadcasted_iota(jnp.int32, (entries, entries), 0) < lax.broadcasted_iota(jnp.int32, (entries, entries), 1)
    for move in moves:
        move.wait()
    live = jnp.zeros((1, entries), jnp.bool_)
    for tile in range(entries // tile_rows):
        start = tile * tile_rows
        live = live | ((entry >= start) & (entry < start + counts_ref[tile]))
    rows = rows_ref[...]
    owner = rows // own_rows
    lane_owner = jnp.broadcast_to(owner.astype(f32), (entries, entries))
    rank = jnp.sum(jnp.where(earlier & (lane_owner.T == lane_owner), 1, 0), axis=0, keepdims=True)
    slot = owner * cap + rank
    choose = jnp.where(lax.broadcasted_iota(jnp.int32, (slots, entries), 0) == slot, 1.0, 0.0).astype(bf16)
    data = jnp.where(live, updates_ref[...], 0.0)
    local_row = (rows - owner * own_rows).astype(f32)
    folded = height > cap
    if not folded:
        tail = jnp.where(lax.broadcasted_iota(jnp.int32, (width - columns, entries), 0) == 0, local_row, 0.0)
        data = jnp.concatenate([data, tail], axis=0)
    packed = jnp.zeros((slots, data.shape[0]), f32)
    for piece in thirds_of(data):
        packed += lax.dot_general(choose, piece, lanes_contract, preferred_element_type=f32)
    packed = packed.reshape(owners, cap, data.shape[0])
    if not folded:
        packed_ref[...] = packed
        return
    half = cap // 2
    packed_ref[:, :cap, :] = packed[:, :, :width]
    packed_ref[:, cap:cap + half, :] = jnp.concatenate([packed[:, :half, width:], packed[:, half:, width:]], axis=2)
    first = lax.axis_index("tile") * cap
    by_owner = jnp.where(lax.broadcasted_iota(jnp.int32, (owners, entries), 0) == owner, local_row, 0.0).astype(bf16)
    by_lane = jnp.where(lax.broadcasted_iota(jnp.int32, (width, entries), 0) == first % width + rank, 1.0, 0.0).astype(bf16)
    numbers = lax.dot_general(by_owner, by_lane, lanes_contract, preferred_element_type=f32)
    line = lax.broadcasted_iota(jnp.int32, (owners, 8, width), 1)
    packed_ref[:, cap + half:, :] = jnp.where(line == first // width, numbers[:, None, :], 0.0)


def reduce_kernel(cap, received_ref, right_hbm, *refs):
    reduced_refs, right_ref, sem = refs[:-2], refs[-2], refs[-1]
    move = pltpu.make_async_copy(right_hbm, right_ref, sem)
    move.start()
    owners, height, width = received_ref.shape
    slots = owners * cap
    columns, own_rows = right_ref.shape
    if height > cap:
        half = cap // 2
        numbers = jnp.sum(received_ref[:, cap + half:, :], axis=0)
        numbers = jnp.concatenate([numbers[i:i + 1] for i in range(slots // width)], axis=1).astype(jnp.int32)
        rest = received_ref[:, cap:cap + half, :]
        rest = jnp.concatenate([rest[:, :, :width // 2], rest[:, :, width // 2:]], axis=1)
        sets = [received_ref[:, :cap, :].reshape(slots, width), rest.reshape(slots, width // 2)]
        place = jnp.where(lax.broadcasted_iota(jnp.int32, (own_rows, slots), 0) == numbers, 1.0, 0.0).astype(bf16)
        totals = []
        for value in sets:
            total = jnp.zeros((own_rows, value.shape[1]), f32)
            for piece in thirds_of(value):
                total += jnp.dot(place, piece, preferred_element_type=f32)
            totals.append(total.T)
        total = jnp.concatenate(totals, axis=0)
    else:
        received = received_ref[...].reshape(slots, width)
        local_row = received[:, columns:columns + 1].astype(jnp.int32)
        place = jnp.where(lax.broadcasted_iota(jnp.int32, (slots, own_rows), 1) == local_row, 1.0, 0.0).astype(bf16)
        total = jnp.zeros((columns, own_rows), f32)
        for piece in thirds_of(received[:, :columns].T):
            total += jnp.dot(piece, place, preferred_element_type=f32)
    move.wait()
    start = 0
    for reduced_ref in reduced_refs:
        rows = reduced_ref.shape[0]
        reduced_ref[...] = right_ref[start:start + rows, :] - total[start:start + rows]
        start += rows


def split_kernel(matrix_ref, high_ref, low_ref):
    parts, own_rows, full_rows = matrix_ref.shape
    blocks, rows, block = high_ref.shape
    height = 64
    for part in range(parts):
        for first in range(0, own_rows, height):
            for j in range(blocks):
                high, low = halves_of(matrix_ref[part, first:first + height, j * block:(j + 1) * block])
                start = part * own_rows + first
                high_ref[j, start:start + height, :] = high
                low_ref[j, start:start + height, :] = low


def split_blocks(matrix, block):
    parts, own_rows, full_rows = matrix.shape
    count = full_rows // block
    vmem = pl.BlockSpec(memory_space=pltpu.VMEM)
    shape = jax.ShapeDtypeStruct((count, parts * own_rows, block), bf16)
    return pl.pallas_call(
        split_kernel,
        in_specs=[vmem],
        out_specs=[vmem, vmem],
        out_shape=[shape, shape],
        compiler_params=kernel_params(20),
        cost_estimate=pl.CostEstimate(flops=3 * matrix.size, bytes_accessed=8 * matrix.size, transcendentals=0),
    )(matrix)


def tile_of(q, size):
    me = lax.axis_index("tile")
    layers = size // 4
    side, across, by = q // (2 * layers), q // layers % 2, q % layers
    layer = lax.rem(lax.div(me, 4) + (layers - by), layers)
    row = lax.rem(lax.div(me, 2) + across, 2)
    core = lax.rem(me + side, 2)
    return layer * 4 + row * 2 + core


def product_kernel(sources, layout, inputs, sets, begin, end, finish, onward, relative, *refs):
    high_ref, low_ref = refs[inputs * sets:inputs * sets + 2]
    rest = refs[inputs * sets + 2:]
    count, both_rows, block = high_ref.shape
    own_rows = both_rows // 2
    start_ref, rest = (rest[0], rest[1:]) if begin > 0 else (None, rest)
    out_refs, total_ref = (rest[:-1], rest[-1]) if finish else ((), rest[0])
    columns = total_ref.shape[0]
    per_step = 4 if (end - begin) % 4 == 0 else 1

    def block_of(q):
        pieces = []
        for group in layout:
            which, place = group[q]
            value = refs[which][place]
            if sets == 2:
                value = refs[inputs + which][place] - value
            pieces.append(value)
        return jnp.concatenate(pieces, axis=0)

    @pl.when(jnp.logical_not(onward) | (lax.axis_index("chain") < lax.axis_size("chain") - 1))
    def _():
        for first in range(begin, end, per_step):
            tiles = [tile_of(q, count) if relative else q for q in range(first, first + per_step)]
            x_high, x_low = halves_of(jnp.concatenate([block_of(q) for q in range(first, first + per_step)], axis=1))
            k_high = jnp.concatenate([high_ref[tile] for tile in tiles], axis=1)
            k_low = jnp.concatenate([low_ref[tile] for tile in tiles], axis=1)
            both = lax.dot_general(jnp.concatenate([x_high, x_low], axis=0), k_high, lanes_contract, preferred_element_type=f32)
            part = both[:columns] + both[columns:] + lax.dot_general(x_high, k_low, lanes_contract, preferred_element_type=f32)
            if first > begin:
                total_ref[...] += part
            elif start_ref is None:
                total_ref[...] = part
            else:
                total_ref[...] = start_ref[...] + part
        start = 0
        for out_ref in out_refs:
            for first in range(0, out_ref.shape[0], 2 * sources):
                real = pl.ds(start + first, sources)
                imag = pl.ds(start + first + sources, sources)
                out_ref[first:first + sources, :] = total_ref[real, :own_rows] - total_ref[imag, own_rows:]
                out_ref[first + sources:first + 2 * sources, :] = total_ref[imag, :own_rows] + total_ref[real, own_rows:]
            start += out_ref.shape[0]


def product_part(split, onward, layout, blocks, own, begin, end, started, sources, shares):
    count, both_rows, block = split[0].shape
    vmem = pl.BlockSpec(memory_space=pltpu.VMEM)
    finish = end == count
    whole = (sum(shares), both_rows)
    arrays = list(blocks) + list(own) + list(split) + ([] if started is None else [started])
    if finish:
        out_shape = [jax.ShapeDtypeStruct((rows, both_rows // 2), f32) for rows in shares]
    else:
        out_shape = jax.ShapeDtypeStruct(whole, f32)
    return pl.pallas_call(
        functools.partial(product_kernel, sources, layout, len(blocks), 2 if own else 1, begin, end, finish, onward, len(layout) > 1),
        in_specs=[vmem] * len(arrays),
        out_specs=[vmem] * len(shares) if finish else vmem,
        out_shape=out_shape,
        scratch_shapes=[pltpu.VMEM(whole, f32)] if finish else [],
        compiler_params=kernel_params(20),
        cost_estimate=pl.CostEstimate(flops=6 * sum(shares) * both_rows * block * (end - begin), bytes_accessed=MIB, transcendentals=0),
    )(*arrays)


def tied(value, to):
    return lax.optimization_barrier((value, to))[0]


def solve_paired(reduced, diag_inverse, coupling, sources):
    chain_size = lax.axis_size("chain")
    tile_size = lax.axis_size("tile")
    own_rows = reduced[0].shape[1]
    shares = [each.shape[0] for each in reduced]
    layers = tile_size // 4
    count = tile_size
    places = [(side, across, by) for side in range(2) for across in range(2) for by in range(layers)]

    def send(value, hop, target):
        if not hop:
            return lax.ppermute(value, "tile", [(t, target(t)) for t in range(tile_size)])
        pairs = [(c * tile_size + t, (c + 1) * tile_size + target(t)) for c in range(chain_size - 1) for t in range(tile_size)]
        return lax.ppermute(value, ("chain", "tile"), pairs)

    def first_stage(first, second, hop):
        second = send(second, True, lambda t: t) if hop else second
        pair = [second, send(second, False, lambda t: t ^ 2)]
        line = [first if by == 0 and not hop else send(first, hop, lambda t: (t + 4 * by) % tile_size) for by in range(layers)]
        return jnp.stack(pair), jnp.stack(line)

    def second_stage(pair, line):
        far = send(line, False, lambda t: t ^ 2)
        rest = [pair if by == 0 else send(pair, False, lambda t: (t + 4 * by) % tile_size) for by in range(layers)]
        return [line, far, jnp.stack(rest)]

    layout = [
        [(across, (by,)) for side, across, by in places],
        [(2, (by, across)) for side, across, by in places],
    ]

    def products(split, onward, held, own, shares):
        other = [send(each, False, lambda t: t ^ 1) for each in held]
        mine, theirs = own if own else ([], [])
        started = product_part(split, onward, layout, held, mine, 0, count // 2, None, sources, shares)
        return product_part(split, onward, layout, other, theirs, count // 2, count, started, sources, shares), other

    only = chain_size == 1
    pair, line = first_stage(*reduced, False)
    split = split_blocks(tied(diag_inverse if only else coupling, reduced[0]), own_rows)
    pair, line, split = lax.optimization_barrier((pair, line, split))
    held = second_stage(pair, line)
    if only:
        return products(split, False, held, None, [sum(shares)])[0][0]
    diag_split = split_blocks(tied(diag_inverse, line), own_rows)
    held[1], held[2], diag_split = lax.optimization_barrier((held[1], held[2], diag_split))
    carried, other = products(split, True, held, None, shares)
    own = (held, other)
    for step in range(chain_size - 1):
        held = second_stage(*lax.optimization_barrier(first_stage(*carried, True)))
        if step < chain_size - 2:
            carried = products(split, True, held, own, shares)[0]
    return products(diag_split, False, held, own, [sum(shares)])[0][0]


def solve_flat(reduced, diag_inverse, coupling, sources):
    chain_size = lax.axis_size("chain")
    reduced = reduced[0]
    columns = reduced.shape[0]
    full_rows = diag_inverse.shape[2]
    block = min(256, full_rows)
    count = full_rows // block
    layout = [[(0, (q,)) for q in range(count)]]
    onward = [(i, i + 1) for i in range(chain_size - 1)]
    diag_split = split_blocks(diag_inverse, block)
    coupling_split = split_blocks(coupling, block)

    def gathered(value):
        whole = lax.all_gather(value, "tile", axis=1, tiled=True)
        return [whole.reshape(columns, count, block).transpose(1, 0, 2)]

    current = reduced
    for _ in range(chain_size - 1):
        carried = product_part(coupling_split, True, layout, gathered(current), [], 0, count, None, sources, [columns])[0]
        current = reduced - lax.ppermute(carried, "chain", onward)
    return product_part(diag_split, False, layout, gathered(current), [], 0, count, None, sources, [columns])[0]


def body(right_side, diag_inverse, coupling, updates, update_rows, tile_counts):
    batches, halves, sources, own_rows = right_side.shape
    tile_size = lax.axis_size("tile")
    entries, columns = updates.shape
    tile_rows = entries // tile_counts.shape[0]
    cap = 2 * entries // tile_size
    slots = tile_size * cap
    vmem = pl.BlockSpec(memory_space=pltpu.VMEM)
    hbm = pl.BlockSpec(memory_space=pltpu.HBM)
    folded = cap % 16 == 0 and slots <= 1024 and columns == 192 and own_rows <= 256 and 128 % cap == 0
    width = 128 if folded else -(-(columns + 1) // 128) * 128
    height = cap + cap // 2 + 8 if folded else cap
    packed = pl.pallas_call(
        functools.partial(pack_kernel, own_rows, cap, tile_rows),
        in_specs=[hbm, hbm, hbm],
        out_specs=vmem,
        out_shape=jax.ShapeDtypeStruct((tile_size, height, width), f32),
        scratch_shapes=[
            pltpu.SMEM(tile_counts.shape, jnp.int32),
            pltpu.VMEM((1, entries), jnp.int32),
            pltpu.VMEM((columns, entries), f32),
            pltpu.SemaphoreType.DMA((3,)),
        ],
        compiler_params=kernel_params(56),
    )(tile_counts, update_rows[None, :], updates.T)
    received = lax.all_to_all(packed, "tile", 0, 0, tiled=False)
    paired = own_rows % 128 == 0 and tile_size % 8 == 0 and batches > 1
    early = batches * 2 // 3 * halves * sources
    shares = [early, columns - early] if paired else [columns]
    reduced = pl.pallas_call(
        functools.partial(reduce_kernel, cap),
        in_specs=[vmem, hbm],
        out_specs=[vmem] * len(shares),
        out_shape=[jax.ShapeDtypeStruct((rows, own_rows), f32) for rows in shares],
        scratch_shapes=[pltpu.VMEM((columns, own_rows), f32), pltpu.SemaphoreType.DMA(())],
        compiler_params=kernel_params(20),
    )(received, right_side.reshape(columns, own_rows))
    solve = solve_paired if paired else solve_flat
    return solve(reduced, diag_inverse, coupling, sources).reshape(right_side.shape)


def solution(mesh):
    in_specs = (
        P(None, None, None, ("chain", "tile")),
        P(None, ("chain", "tile"), None),
        P(None, ("chain", "tile"), None),
        P(("chain", "tile"), None),
        P(("chain", "tile")),
        P(("chain", "tile")),
    )
    out_specs = P(None, None, None, ("chain", "tile"))
    return jax.shard_map(body, mesh=mesh, in_specs=in_specs, out_specs=out_specs, check_vma=False)
```

```python
import functools

import jax
import jax.numpy as jnp
from jax import lax
from jax.experimental import pallas as pl
from jax.experimental.pallas import tpu as pltpu
from jax.sharding import PartitionSpec as P

MIB = 1 << 20
f32 = jnp.float32
bf16 = jnp.bfloat16
lanes_contract = (((1,), (1,)), ((), ()))


def halves_of(value):
    high = value.astype(bf16)
    return high, (value - high.astype(f32)).astype(bf16)


def thirds_of(value):
    high = value.astype(bf16)
    rest = value - high.astype(f32)
    middle = rest.astype(bf16)
    return high, middle, (rest - middle.astype(f32)).astype(bf16)


def kernel_params(size):
    return pltpu.CompilerParams(vmem_limit_bytes=int(size * MIB))


def pack_kernel(own_rows, cap, tile_rows, counts_hbm, rows_hbm, updates_hbm, packed_ref, counts_ref, rows_ref, updates_ref, sems):
    moves = [
        pltpu.make_async_copy(counts_hbm, counts_ref, sems.at[0]),
        pltpu.make_async_copy(rows_hbm, rows_ref, sems.at[1]),
        pltpu.make_async_copy(updates_hbm, updates_ref, sems.at[2]),
    ]
    for move in moves:
        move.start()
    columns, entries = updates_ref.shape
    owners, height, width = packed_ref.shape
    slots = owners * cap
    entry = lax.broadcasted_iota(jnp.int32, (1, entries), 1)
    earlier = lax.broadcasted_iota(jnp.int32, (entries, entries), 0) < lax.broadcasted_iota(jnp.int32, (entries, entries), 1)
    for move in moves:
        move.wait()
    live = jnp.zeros((1, entries), jnp.bool_)
    for tile in range(entries // tile_rows):
        start = tile * tile_rows
        live = live | ((entry >= start) & (entry < start + counts_ref[tile]))
    rows = rows_ref[...]
    owner = rows // own_rows
    lane_owner = jnp.broadcast_to(owner.astype(f32), (entries, entries))
    rank = jnp.sum(jnp.where(earlier & (lane_owner.T == lane_owner), 1, 0), axis=0, keepdims=True)
    slot = owner * cap + rank
    choose = jnp.where(lax.broadcasted_iota(jnp.int32, (slots, entries), 0) == slot, 1.0, 0.0).astype(bf16)
    data = jnp.where(live, updates_ref[...], 0.0)
    local_row = (rows - owner * own_rows).astype(f32)
    folded = height > cap
    if not folded:
        tail = jnp.where(lax.broadcasted_iota(jnp.int32, (width - columns, entries), 0) == 0, local_row, 0.0)
        data = jnp.concatenate([data, tail], axis=0)
    packed = jnp.zeros((slots, data.shape[0]), f32)
    for piece in thirds_of(data):
        packed += lax.dot_general(choose, piece, lanes_contract, preferred_element_type=f32)
    packed = packed.reshape(owners, cap, data.shape[0])
    if not folded:
        packed_ref[...] = packed
        return
    half = cap // 2
    packed_ref[:, :cap, :] = packed[:, :, :width]
    packed_ref[:, cap:cap + half, :] = jnp.concatenate([packed[:, :half, width:], packed[:, half:, width:]], axis=2)
    first = lax.axis_index("tile") * cap
    by_owner = jnp.where(lax.broadcasted_iota(jnp.int32, (owners, entries), 0) == owner, local_row, 0.0).astype(bf16)
    by_lane = jnp.where(lax.broadcasted_iota(jnp.int32, (width, entries), 0) == first % width + rank, 1.0, 0.0).astype(bf16)
    numbers = lax.dot_general(by_owner, by_lane, lanes_contract, preferred_element_type=f32)
    line = lax.broadcasted_iota(jnp.int32, (owners, 8, width), 1)
    packed_ref[:, cap + half:, :] = jnp.where(line == first // width, numbers[:, None, :], 0.0)


def reduce_kernel(cap, received_ref, right_hbm, *refs):
    reduced_refs, right_ref, sem = refs[:-2], refs[-2], refs[-1]
    move = pltpu.make_async_copy(right_hbm, right_ref, sem)
    move.start()
    owners, height, width = received_ref.shape
    slots = owners * cap
    columns, own_rows = right_ref.shape
    if height > cap:
        half = cap // 2
        numbers = jnp.sum(received_ref[:, cap + half:, :], axis=0)
        numbers = jnp.concatenate([numbers[i:i + 1] for i in range(slots // width)], axis=1).astype(jnp.int32)
        rest = received_ref[:, cap:cap + half, :]
        rest = jnp.concatenate([rest[:, :, :width // 2], rest[:, :, width // 2:]], axis=1)
        sets = [received_ref[:, :cap, :].reshape(slots, width), rest.reshape(slots, width // 2)]
        place = jnp.where(lax.broadcasted_iota(jnp.int32, (own_rows, slots), 0) == numbers, 1.0, 0.0).astype(bf16)
        totals = []
        for value in sets:
            total = jnp.zeros((own_rows, value.shape[1]), f32)
            for piece in thirds_of(value):
                total += jnp.dot(place, piece, preferred_element_type=f32)
            totals.append(total.T)
        total = jnp.concatenate(totals, axis=0)
    else:
        received = received_ref[...].reshape(slots, width)
        local_row = received[:, columns:columns + 1].astype(jnp.int32)
        place = jnp.where(lax.broadcasted_iota(jnp.int32, (slots, own_rows), 1) == local_row, 1.0, 0.0).astype(bf16)
        total = jnp.zeros((columns, own_rows), f32)
        for piece in thirds_of(received[:, :columns].T):
            total += jnp.dot(piece, place, preferred_element_type=f32)
    move.wait()
    start = 0
    for reduced_ref in reduced_refs:
        rows = reduced_ref.shape[0]
        reduced_ref[...] = right_ref[start:start + rows, :] - total[start:start + rows]
        start += rows


def split_kernel(block, relative, matrix_ref, high_ref, low_ref):
    parts, own_rows, full_rows = matrix_ref.shape
    groups, rows, width = high_ref.shape
    layers = width // block
    height = 64
    for part in range(parts):
        for first in range(0, own_rows, height):
            start = part * own_rows + first
            for group in range(groups):
                for layer in range(layers):
                    column = (layer * groups + group if relative else group * layers + layer) * block
                    high, low = halves_of(matrix_ref[part, first:first + height, column:column + block])
                    high_ref[group, start:start + height, layer * block:(layer + 1) * block] = high
                    low_ref[group, start:start + height, layer * block:(layer + 1) * block] = low


def split_blocks(matrix, block, relative):
    parts, own_rows, full_rows = matrix.shape
    groups = 4 if full_rows % (4 * block) == 0 else 1
    vmem = pl.BlockSpec(memory_space=pltpu.VMEM)
    shape = jax.ShapeDtypeStruct((groups, parts * own_rows, full_rows // groups), bf16)
    return pl.pallas_call(
        functools.partial(split_kernel, block, relative),
        in_specs=[vmem],
        out_specs=[vmem, vmem],
        out_shape=[shape, shape],
        compiler_params=kernel_params(20),
        cost_estimate=pl.CostEstimate(flops=3 * matrix.size, bytes_accessed=8 * matrix.size, transcendentals=0),
    )(matrix)


def product_kernel(sources, layout, inputs, sets, block, begin, end, onward, relative, *refs):
    high_ref, low_ref = refs[inputs * sets:inputs * sets + 2]
    rest = refs[inputs * sets + 2:]
    groups, both_rows, width = high_ref.shape
    layers = width // block
    own_rows = both_rows // 2
    start_ref, rest = (rest[0], rest[1:]) if begin > 0 else (None, rest)
    out_refs, total_ref = (rest[:-1], rest[-1]) if end == groups else ((), rest[0])
    columns = total_ref.shape[0]
    me = lax.axis_index("tile")

    def block_of(step, layer):
        held = lax.rem(lax.div(me, 4) + (layers - layer), layers) if relative else layer
        pieces = []
        for group in layout:
            which, place = group(step, held)
            value = refs[which][place]
            if sets == 2:
                value = refs[inputs + which][place] - value
            pieces.append(value)
        return jnp.concatenate(pieces, axis=0)

    @pl.when(jnp.logical_not(onward) | (lax.axis_index("chain") < lax.axis_size("chain") - 1))
    def _():
        for step in range(begin, end):
            group = step
            if relative:
                group = lax.rem(lax.div(me, 2) + step % 2, 2) * 2 + lax.rem(me + step // 2, 2)
            x_high, x_low = halves_of(jnp.concatenate([block_of(step, layer) for layer in range(layers)], axis=1))
            lhs = jnp.concatenate([x_high, x_low], axis=0)
            both = lax.dot_general(lhs, high_ref[group], lanes_contract, preferred_element_type=f32)
            part = both[:columns] + both[columns:]
            part += lax.dot_general(x_high, low_ref[group], lanes_contract, preferred_element_type=f32)
            if step > begin:
                total_ref[...] += part
            elif start_ref is None:
                total_ref[...] = part
            else:
                total_ref[...] = start_ref[...] + part
        start = 0
        for out_ref in out_refs:
            for first in range(0, out_ref.shape[0], 2 * sources):
                real = pl.ds(start + first, sources)
                imag = pl.ds(start + first + sources, sources)
                out_ref[first:first + sources, :] = total_ref[real, :own_rows] - total_ref[imag, own_rows:]
                out_ref[first + sources:first + 2 * sources, :] = total_ref[imag, :own_rows] + total_ref[real, own_rows:]
            start += out_ref.shape[0]


def product_part(split, onward, layout, blocks, own, begin, end, started, sources, shares, relative):
    groups, both_rows, width = split[0].shape
    block = blocks[0].shape[-1]
    vmem = pl.BlockSpec(memory_space=pltpu.VMEM)
    finish = end == groups
    whole = (sum(shares), both_rows)
    arrays = list(blocks) + list(own) + list(split) + ([] if started is None else [started])
    if finish:
        out_shape = [jax.ShapeDtypeStruct((rows, both_rows // 2), f32) for rows in shares]
    else:
        out_shape = jax.ShapeDtypeStruct(whole, f32)
    return pl.pallas_call(
        functools.partial(product_kernel, sources, layout, len(blocks), 2 if own else 1, block, begin, end, onward, relative),
        in_specs=[vmem] * len(arrays),
        out_specs=[vmem] * len(shares) if finish else vmem,
        out_shape=out_shape,
        scratch_shapes=[pltpu.VMEM(whole, f32)] if finish else [],
        compiler_params=kernel_params(20),
        cost_estimate=pl.CostEstimate(flops=6 * sum(shares) * both_rows * width * (end - begin), bytes_accessed=MIB, transcendentals=0),
    )(*arrays)


def tied(value, to):
    return lax.optimization_barrier((value, to))[0]


def solve_paired(reduced, diag_inverse, coupling, sources):
    chain_size = lax.axis_size("chain")
    tile_size = lax.axis_size("tile")
    own_rows = reduced[0].shape[1]
    shares = [each.shape[0] for each in reduced]
    layers = tile_size // 4

    def send(value, hop, target):
        if not hop:
            return lax.ppermute(value, "tile", [(t, target(t)) for t in range(tile_size)])
        pairs = [(c * tile_size + t, (c + 1) * tile_size + target(t)) for c in range(chain_size - 1) for t in range(tile_size)]
        return lax.ppermute(value, ("chain", "tile"), pairs)

    def first_stage(first, second, hop):
        pair = [second if across == 0 and not hop else send(second, hop, lambda t: t ^ (2 * across)) for across in range(2)]
        line = [first if by == 0 and not hop else send(first, hop, lambda t: (t + 4 * by) % tile_size) for by in range(layers)]
        return jnp.stack(pair), jnp.stack(line)

    def second_stage(pair, line):
        far = send(line, False, lambda t: t ^ 2)
        rest = [pair if by == 0 else send(pair, False, lambda t: (t + 4 * by) % tile_size) for by in range(layers)]
        return [line, far, jnp.stack(rest)]

    layout = [lambda step, held: (step % 2, (held,)), lambda step, held: (2, (held, step % 2))]

    def products(split, onward, held, own, shares):
        other = [send(each, False, lambda t: t ^ 1) for each in held]
        mine, theirs = own if own else ([], [])
        started = product_part(split, onward, layout, held, mine, 0, 2, None, sources, shares, True)
        return product_part(split, onward, layout, other, theirs, 2, 4, started, sources, shares, True), other

    only = chain_size == 1
    pair, line = first_stage(*reduced, False)
    split = split_blocks(tied(diag_inverse if only else coupling, reduced[0]), own_rows, True)
    pair, line, split = lax.optimization_barrier((pair, line, split))
    held = second_stage(pair, line)
    if only:
        return products(split, False, held, None, [sum(shares)])[0][0]
    diag_split = split_blocks(tied(diag_inverse, line), own_rows, True)
    held[1], held[2], diag_split = lax.optimization_barrier((held[1], held[2], diag_split))
    carried, other = products(split, True, held, None, shares)
    own = (held, other)
    for step in range(chain_size - 1):
        held = second_stage(*lax.optimization_barrier(first_stage(*carried, True)))
        if step < chain_size - 2:
            carried = products(split, True, held, own, shares)[0]
    return products(diag_split, False, held, own, [sum(shares)])[0][0]


def solve_flat(reduced, diag_inverse, coupling, sources):
    chain_size = lax.axis_size("chain")
    reduced = reduced[0]
    columns = reduced.shape[0]
    full_rows = diag_inverse.shape[2]
    block = min(256, full_rows)
    count = full_rows // block
    layout = [lambda step, held: (0, (step * layers + held,))]
    onward = [(i, i + 1) for i in range(chain_size - 1)]
    diag_split = split_blocks(diag_inverse, block, False)
    coupling_split = split_blocks(coupling, block, False)
    groups = diag_split[0].shape[0]
    layers = count // groups

    def gathered(value):
        whole = lax.all_gather(value, "tile", axis=1, tiled=True)
        return [whole.reshape(columns, count, block).transpose(1, 0, 2)]

    current = reduced
    for _ in range(chain_size - 1):
        carried = product_part(coupling_split, True, layout, gathered(current), [], 0, groups, None, sources, [columns], False)[0]
        current = reduced - lax.ppermute(carried, "chain", onward)
    return product_part(diag_split, False, layout, gathered(current), [], 0, groups, None, sources, [columns], False)[0]


def body(right_side, diag_inverse, coupling, updates, update_rows, tile_counts):
    batches, halves, sources, own_rows = right_side.shape
    tile_size = lax.axis_size("tile")
    entries, columns = updates.shape
    tile_rows = entries // tile_counts.shape[0]
    cap = 2 * entries // tile_size
    slots = tile_size * cap
    vmem = pl.BlockSpec(memory_space=pltpu.VMEM)
    hbm = pl.BlockSpec(memory_space=pltpu.HBM)
    folded = cap % 16 == 0 and slots <= 1024 and columns == 192 and own_rows <= 256 and 128 % cap == 0
    width = 128 if folded else -(-(columns + 1) // 128) * 128
    height = cap + cap // 2 + 8 if folded else cap
    packed = pl.pallas_call(
        functools.partial(pack_kernel, own_rows, cap, tile_rows),
        in_specs=[hbm, hbm, hbm],
        out_specs=vmem,
        out_shape=jax.ShapeDtypeStruct((tile_size, height, width), f32),
        scratch_shapes=[
            pltpu.SMEM(tile_counts.shape, jnp.int32),
            pltpu.VMEM((1, entries), jnp.int32),
            pltpu.VMEM((columns, entries), f32),
            pltpu.SemaphoreType.DMA((3,)),
        ],
        compiler_params=kernel_params(56),
    )(tile_counts, update_rows[None, :], updates.T)
    received = lax.all_to_all(packed, "tile", 0, 0, tiled=False)
    paired = own_rows % 128 == 0 and tile_size % 8 == 0 and batches > 1
    early = batches * 2 // 3 * halves * sources
    shares = [early, columns - early] if paired else [columns]
    reduced = pl.pallas_call(
        functools.partial(reduce_kernel, cap),
        in_specs=[vmem, hbm],
        out_specs=[vmem] * len(shares),
        out_shape=[jax.ShapeDtypeStruct((rows, own_rows), f32) for rows in shares],
        scratch_shapes=[pltpu.VMEM((columns, own_rows), f32), pltpu.SemaphoreType.DMA(())],
        compiler_params=kernel_params(20),
    )(received, right_side.reshape(columns, own_rows))
    solve = solve_paired if paired else solve_flat
    return solve(reduced, diag_inverse, coupling, sources).reshape(right_side.shape)


def solution(mesh):
    in_specs = (
        P(None, None, None, ("chain", "tile")),
        P(None, ("chain", "tile"), None),
        P(None, ("chain", "tile"), None),
        P(("chain", "tile"), None),
        P(("chain", "tile")),
        P(("chain", "tile")),
    )
    out_specs = P(None, None, None, ("chain", "tile"))
    return jax.shard_map(body, mesh=mesh, in_specs=in_specs, out_specs=out_specs, check_vma=False)
```

```python
import functools

import jax
import jax.numpy as jnp
from jax import lax
from jax.experimental import pallas as pl
from jax.experimental.pallas import tpu as pltpu
from jax.sharding import PartitionSpec as P

MIB = 1 << 20
f32 = jnp.float32
bf16 = jnp.bfloat16
lanes_contract = (((1,), (1,)), ((), ()))


def halves_of(value):
    high = value.astype(bf16)
    return high, (value - high.astype(f32)).astype(bf16)


def kernel_params(size):
    return pltpu.CompilerParams(vmem_limit_bytes=int(size * MIB))


def pack_kernel(own_rows, cap, tile_rows, counts_hbm, rows_hbm, updates_hbm, packed_ref, counts_ref, rows_ref, updates_ref, sems):
    moves = [
        pltpu.make_async_copy(counts_hbm, counts_ref, sems.at[0]),
        pltpu.make_async_copy(rows_hbm, rows_ref, sems.at[1]),
        pltpu.make_async_copy(updates_hbm, updates_ref, sems.at[2]),
    ]
    for move in moves:
        move.start()
    columns, entries = updates_ref.shape
    owners, height, width = packed_ref.shape
    slots = owners * cap
    entry = lax.broadcasted_iota(jnp.int32, (1, entries), 1)
    earlier = lax.broadcasted_iota(jnp.int32, (entries, entries), 0) < lax.broadcasted_iota(jnp.int32, (entries, entries), 1)
    for move in moves:
        move.wait()
    live = jnp.zeros((1, entries), jnp.bool_)
    for tile in range(entries // tile_rows):
        start = tile * tile_rows
        live = live | ((entry >= start) & (entry < start + counts_ref[tile]))
    rows = rows_ref[...]
    owner = rows // own_rows
    lane_owner = jnp.broadcast_to(owner.astype(f32), (entries, entries))
    rank = jnp.sum(jnp.where(earlier & (lane_owner.T == lane_owner), 1, 0), axis=0, keepdims=True)
    slot = owner * cap + rank
    choose = jnp.where(lax.broadcasted_iota(jnp.int32, (slots, entries), 0) == slot, 1.0, 0.0).astype(bf16)
    data = jnp.where(live, updates_ref[...], 0.0)
    local_row = (rows - owner * own_rows).astype(f32)
    folded = height > cap
    if not folded:
        tail = jnp.where(lax.broadcasted_iota(jnp.int32, (width - columns, entries), 0) == 0, local_row, 0.0)
        data = jnp.concatenate([data, tail], axis=0)
    packed = jnp.zeros((slots, data.shape[0]), f32)
    for piece in halves_of(data):
        packed += lax.dot_general(choose, piece, lanes_contract, preferred_element_type=f32)
    packed = packed.reshape(owners, cap, data.shape[0])
    if not folded:
        packed_ref[...] = packed
        return
    half = cap // 2
    packed_ref[:, :cap, :] = packed[:, :, :width]
    packed_ref[:, cap:cap + half, :] = jnp.concatenate([packed[:, :half, width:], packed[:, half:, width:]], axis=2)
    first = lax.axis_index("tile") * cap
    by_owner = jnp.where(lax.broadcasted_iota(jnp.int32, (owners, entries), 0) == owner, local_row, 0.0).astype(bf16)
    by_lane = jnp.where(lax.broadcasted_iota(jnp.int32, (width, entries), 0) == first % width + rank, 1.0, 0.0).astype(bf16)
    numbers = lax.dot_general(by_owner, by_lane, lanes_contract, preferred_element_type=f32)
    line = lax.broadcasted_iota(jnp.int32, (owners, 8, width), 1)
    packed_ref[:, cap + half:, :] = jnp.where(line == first // width, numbers[:, None, :], 0.0)


def reduce_kernel(cap, received_ref, right_hbm, *refs):
    reduced_refs, right_ref, sem = refs[:-2], refs[-2], refs[-1]
    move = pltpu.make_async_copy(right_hbm, right_ref, sem)
    move.start()
    owners, height, width = received_ref.shape
    slots = owners * cap
    columns, own_rows = right_ref.shape
    if height > cap:
        half = cap // 2
        numbers = jnp.sum(received_ref[:, cap + half:, :], axis=0)
        numbers = jnp.concatenate([numbers[i:i + 1] for i in range(slots // width)], axis=1).astype(jnp.int32)
        rest = received_ref[:, cap:cap + half, :]
        rest = jnp.concatenate([rest[:, :, :width // 2], rest[:, :, width // 2:]], axis=1)
        sets = [received_ref[:, :cap, :].reshape(slots, width), rest.reshape(slots, width // 2)]
        place = jnp.where(lax.broadcasted_iota(jnp.int32, (own_rows, slots), 0) == numbers, 1.0, 0.0).astype(bf16)
        totals = []
        for value in sets:
            total = jnp.zeros((own_rows, value.shape[1]), f32)
            for piece in halves_of(value):
                total += jnp.dot(place, piece, preferred_element_type=f32)
            totals.append(total.T)
        total = jnp.concatenate(totals, axis=0)
    else:
        received = received_ref[...].reshape(slots, width)
        local_row = received[:, columns:columns + 1].astype(jnp.int32)
        place = jnp.where(lax.broadcasted_iota(jnp.int32, (slots, own_rows), 1) == local_row, 1.0, 0.0).astype(bf16)
        total = jnp.zeros((columns, own_rows), f32)
        for piece in halves_of(received[:, :columns].T):
            total += jnp.dot(piece, place, preferred_element_type=f32)
    move.wait()
    start = 0
    for reduced_ref in reduced_refs:
        rows = reduced_ref.shape[0]
        reduced_ref[...] = right_ref[start:start + rows, :] - total[start:start + rows]
        start += rows


def split_kernel(block, relative, matrix_ref, high_ref, low_ref):
    parts, own_rows, full_rows = matrix_ref.shape
    groups, rows, width = high_ref.shape
    layers = width // block
    height = 64
    for part in range(parts):
        for first in range(0, own_rows, height):
            start = part * own_rows + first
            for group in range(groups):
                for layer in range(layers):
                    column = (layer * groups + group if relative else group * layers + layer) * block
                    high, low = halves_of(matrix_ref[part, first:first + height, column:column + block])
                    high_ref[group, start:start + height, layer * block:(layer + 1) * block] = high
                    low_ref[group, start:start + height, layer * block:(layer + 1) * block] = low


def split_blocks(matrix, block, relative):
    parts, own_rows, full_rows = matrix.shape
    groups = 4 if full_rows % (4 * block) == 0 else 1
    vmem = pl.BlockSpec(memory_space=pltpu.VMEM)
    shape = jax.ShapeDtypeStruct((groups, parts * own_rows, full_rows // groups), bf16)
    return pl.pallas_call(
        functools.partial(split_kernel, block, relative),
        in_specs=[vmem],
        out_specs=[vmem, vmem],
        out_shape=[shape, shape],
        compiler_params=kernel_params(20),
        cost_estimate=pl.CostEstimate(flops=3 * matrix.size, bytes_accessed=8 * matrix.size, transcendentals=0),
    )(matrix)


def product_kernel(sources, layout, inputs, sets, block, begin, end, onward, relative, *refs):
    high_ref, low_ref = refs[inputs * sets:inputs * sets + 2]
    rest = refs[inputs * sets + 2:]
    groups, both_rows, width = high_ref.shape
    layers = width // block
    own_rows = both_rows // 2
    start_ref, rest = (rest[0], rest[1:]) if begin > 0 else (None, rest)
    out_refs, total_ref = (rest[:-1], rest[-1]) if end == groups else ((), rest[0])
    columns = total_ref.shape[0]
    me = lax.axis_index("tile")

    def block_of(step, layer):
        held = lax.rem(lax.div(me, 4) + (layers - layer), layers) if relative else layer
        pieces = []
        for group in layout:
            which, place = group(step, held)
            value = refs[which][place]
            if sets == 2:
                own = refs[inputs + which][place]
                value = jnp.where(lax.axis_index("chain") == 0, own, own - value)
            pieces.append(value)
        return jnp.concatenate(pieces, axis=0)

    active = jnp.logical_not(onward) | (lax.axis_index("chain") < lax.axis_size("chain") - 1)

    @pl.when(jnp.logical_not(active))
    def _():
        for out_ref in out_refs:
            out_ref[...] = jnp.zeros_like(out_ref)

    @pl.when(active)
    def _():
        for step in range(begin, end):
            group = step
            if relative:
                group = lax.rem(lax.div(me, 2) + step % 2, 2) * 2 + lax.rem(me + step // 2, 2)
            x_high, x_low = halves_of(jnp.concatenate([block_of(step, layer) for layer in range(layers)], axis=1))
            lhs = jnp.concatenate([x_high, x_low], axis=0)
            both = lax.dot_general(lhs, high_ref[group], lanes_contract, preferred_element_type=f32)
            part = both[:columns] + both[columns:]
            part += lax.dot_general(x_high, low_ref[group], lanes_contract, preferred_element_type=f32)
            if step > begin:
                total_ref[...] += part
            elif start_ref is None:
                total_ref[...] = part
            else:
                total_ref[...] = start_ref[...] + part
        start = 0
        for out_ref in out_refs:
            for first in range(0, out_ref.shape[0], 2 * sources):
                real = pl.ds(start + first, sources)
                imag = pl.ds(start + first + sources, sources)
                out_ref[first:first + sources, :] = total_ref[real, :own_rows] - total_ref[imag, own_rows:]
                out_ref[first + sources:first + 2 * sources, :] = total_ref[imag, :own_rows] + total_ref[real, own_rows:]
            start += out_ref.shape[0]


def product_part(split, onward, layout, blocks, own, begin, end, started, sources, shares, relative):
    groups, both_rows, width = split[0].shape
    block = blocks[0].shape[-1]
    vmem = pl.BlockSpec(memory_space=pltpu.VMEM)
    finish = end == groups
    whole = (sum(shares), both_rows)
    arrays = list(blocks) + list(own) + list(split) + ([] if started is None else [started])
    if finish:
        out_shape = [jax.ShapeDtypeStruct((rows, both_rows // 2), f32) for rows in shares]
    else:
        out_shape = jax.ShapeDtypeStruct(whole, f32)
    return pl.pallas_call(
        functools.partial(product_kernel, sources, layout, len(blocks), 2 if own else 1, block, begin, end, onward, relative),
        in_specs=[vmem] * len(arrays),
        out_specs=[vmem] * len(shares) if finish else vmem,
        out_shape=out_shape,
        scratch_shapes=[pltpu.VMEM(whole, f32)] if finish else [],
        compiler_params=kernel_params(20),
        cost_estimate=pl.CostEstimate(flops=6 * sum(shares) * both_rows * width * (end - begin), bytes_accessed=MIB, transcendentals=0),
    )(*arrays)


def tied(value, to):
    return lax.optimization_barrier((value, to))[0]


def solve_paired(reduced, diag_inverse, coupling, sources):
    chain_size = lax.axis_size("chain")
    tile_size = lax.axis_size("tile")
    own_rows = reduced[0].shape[1]
    shares = [each.shape[0] for each in reduced]
    layers = tile_size // 4

    def send(value, hop, target):
        if not hop:
            return lax.ppermute(value, "tile", [(t, target(t)) for t in range(tile_size)])
        pairs = [(c * tile_size + t, (c + 1) % chain_size * tile_size + target(t)) for c in range(chain_size) for t in range(tile_size)]
        return lax.ppermute(value, ("chain", "tile"), pairs)

    def first_stage(first, second, hop):
        line = [first if by == 0 and not hop else send(first, hop, lambda t: (t + 4 * by) % tile_size) for by in range(layers)]
        if hop:
            second, line[-1] = lax.optimization_barrier((send(second, True, lambda t: t), line[-1]))
        pair = [second, send(second, False, lambda t: t ^ 2)]
        return jnp.stack(pair), jnp.stack(line)

    def second_stage(pair, line):
        far = send(line, False, lambda t: t ^ 2)
        rest = [pair if by == 0 else send(pair, False, lambda t: (t + 4 * by) % tile_size) for by in range(layers)]
        return [line, far, jnp.stack(rest)]

    layout = [lambda step, held: (step % 2, (held,)), lambda step, held: (2, (held, step % 2))]

    def products(split, onward, held, own, shares):
        other = [send(each, False, lambda t: t ^ 1) for each in held]
        mine, theirs = own if own else ([], [])
        started = product_part(split, onward, layout, held, mine, 0, 2, None, sources, shares, True)
        return product_part(split, onward, layout, other, theirs, 2, 4, started, sources, shares, True), other

    only = chain_size == 1
    pair, line = first_stage(*reduced, False)
    split = split_blocks(tied(diag_inverse if only else coupling, reduced[0]), own_rows, True)
    pair, line, split = lax.optimization_barrier((pair, line, split))
    held = second_stage(pair, line)
    if only:
        return products(split, False, held, None, [sum(shares)])[0][0]
    diag_split = split_blocks(tied(diag_inverse, line), own_rows, True)
    held[1], held[2], diag_split = lax.optimization_barrier((held[1], held[2], diag_split))
    carried, other = products(split, True, held, None, shares)
    own = (held, other)
    for step in range(chain_size - 1):
        held = second_stage(*lax.optimization_barrier(first_stage(*carried, True)))
        if step < chain_size - 2:
            carried = products(split, True, held, own, shares)[0]
    return products(diag_split, False, held, own, [sum(shares)])[0][0]


def solve_flat(reduced, diag_inverse, coupling, sources):
    chain_size = lax.axis_size("chain")
    reduced = reduced[0]
    columns = reduced.shape[0]
    full_rows = diag_inverse.shape[2]
    block = min(256, full_rows)
    count = full_rows // block
    layout = [lambda step, held: (0, (step * layers + held,))]
    onward = [(i, i + 1) for i in range(chain_size - 1)]
    diag_split = split_blocks(diag_inverse, block, False)
    coupling_split = split_blocks(coupling, block, False)
    groups = diag_split[0].shape[0]
    layers = count // groups

    def gathered(value):
        whole = lax.all_gather(value, "tile", axis=1, tiled=True)
        return [whole.reshape(columns, count, block).transpose(1, 0, 2)]

    current = reduced
    for _ in range(chain_size - 1):
        carried = product_part(coupling_split, True, layout, gathered(current), [], 0, groups, None, sources, [columns], False)[0]
        current = reduced - lax.ppermute(carried, "chain", onward)
    return product_part(diag_split, False, layout, gathered(current), [], 0, groups, None, sources, [columns], False)[0]


def body(right_side, diag_inverse, coupling, updates, update_rows, tile_counts):
    batches, halves, sources, own_rows = right_side.shape
    tile_size = lax.axis_size("tile")
    entries, columns = updates.shape
    tile_rows = entries // tile_counts.shape[0]
    cap = 2 * entries // tile_size
    slots = tile_size * cap
    vmem = pl.BlockSpec(memory_space=pltpu.VMEM)
    hbm = pl.BlockSpec(memory_space=pltpu.HBM)
    folded = cap % 16 == 0 and slots <= 1024 and columns == 192 and own_rows <= 256 and 128 % cap == 0
    width = 128 if folded else -(-(columns + 1) // 128) * 128
    height = cap + cap // 2 + 8 if folded else cap
    packed = pl.pallas_call(
        functools.partial(pack_kernel, own_rows, cap, tile_rows),
        in_specs=[hbm, hbm, hbm],
        out_specs=vmem,
        out_shape=jax.ShapeDtypeStruct((tile_size, height, width), f32),
        scratch_shapes=[
            pltpu.SMEM(tile_counts.shape, jnp.int32),
            pltpu.VMEM((1, entries), jnp.int32),
            pltpu.VMEM((columns, entries), f32),
            pltpu.SemaphoreType.DMA((3,)),
        ],
        compiler_params=kernel_params(56),
    )(tile_counts, update_rows[None, :], updates.T)
    received = lax.all_to_all(packed, "tile", 0, 0, tiled=False)
    paired = own_rows % 128 == 0 and tile_size % 8 == 0 and batches > 1
    early = batches * 2 // 3 * halves * sources
    shares = [early, columns - early] if paired else [columns]
    reduced = pl.pallas_call(
        functools.partial(reduce_kernel, cap),
        in_specs=[vmem, hbm],
        out_specs=[vmem] * len(shares),
        out_shape=[jax.ShapeDtypeStruct((rows, own_rows), f32) for rows in shares],
        scratch_shapes=[pltpu.VMEM((columns, own_rows), f32), pltpu.SemaphoreType.DMA(())],
        compiler_params=kernel_params(20),
    )(received, right_side.reshape(columns, own_rows))
    solve = solve_paired if paired else solve_flat
    return solve(reduced, diag_inverse, coupling, sources).reshape(right_side.shape)


def solution(mesh):
    in_specs = (
        P(None, None, None, ("chain", "tile")),
        P(None, ("chain", "tile"), None),
        P(None, ("chain", "tile"), None),
        P(("chain", "tile"), None),
        P(("chain", "tile")),
        P(("chain", "tile")),
    )
    out_specs = P(None, None, None, ("chain", "tile"))
    return jax.shard_map(body, mesh=mesh, in_specs=in_specs, out_specs=out_specs, check_vma=False)
```

```python
import functools

import jax
import jax.numpy as jnp
from jax import lax
from jax.experimental import pallas as pl
from jax.experimental.pallas import tpu as pltpu
from jax.sharding import PartitionSpec as P

MIB = 1 << 20
CHAINS = 2
f32 = jnp.float32
bf16 = jnp.bfloat16
lanes_contract = (((1,), (1,)), ((), ()))


def halves_of(value):
    high = value.astype(bf16)
    return high, (value - high.astype(f32)).astype(bf16)


def kernel_params(size):
    return pltpu.CompilerParams(vmem_limit_bytes=int(size * MIB))


def pack_kernel(own_rows, cap, tile_rows, counts_hbm, rows_hbm, updates_hbm, packed_ref, counts_ref, rows_ref, updates_ref, sems):
    moves = [
        pltpu.make_async_copy(counts_hbm, counts_ref, sems.at[0]),
        pltpu.make_async_copy(rows_hbm, rows_ref, sems.at[1]),
        pltpu.make_async_copy(updates_hbm, updates_ref, sems.at[2]),
    ]
    for move in moves:
        move.start()
    columns, entries = updates_ref.shape
    owners, height, width = packed_ref.shape
    slots = owners * cap
    entry = lax.broadcasted_iota(jnp.int32, (1, entries), 1)
    earlier = lax.broadcasted_iota(jnp.int32, (entries, entries), 0) < lax.broadcasted_iota(jnp.int32, (entries, entries), 1)
    for move in moves:
        move.wait()
    live = jnp.zeros((1, entries), jnp.bool_)
    for tile in range(entries // tile_rows):
        start = tile * tile_rows
        live = live | ((entry >= start) & (entry < start + counts_ref[tile]))
    rows = rows_ref[...]
    owner = rows // own_rows
    lane_owner = jnp.broadcast_to(owner.astype(f32), (entries, entries))
    rank = jnp.sum(jnp.where(earlier & (lane_owner.T == lane_owner), 1, 0), axis=0, keepdims=True)
    slot = owner * cap + rank
    choose = jnp.where(lax.broadcasted_iota(jnp.int32, (slots, entries), 0) == slot, 1.0, 0.0).astype(bf16)
    data = jnp.where(live, updates_ref[...], 0.0)
    local_row = (rows - owner * own_rows).astype(f32)
    folded = height > cap
    if not folded:
        tail = jnp.where(lax.broadcasted_iota(jnp.int32, (width - columns, entries), 0) == 0, local_row, 0.0)
        data = jnp.concatenate([data, tail], axis=0)
    packed = jnp.zeros((slots, data.shape[0]), f32)
    for piece in halves_of(data):
        packed += lax.dot_general(choose, piece, lanes_contract, preferred_element_type=f32)
    packed = packed.reshape(owners, cap, data.shape[0])
    if not folded:
        packed_ref[...] = packed
        return
    half = cap // 2
    packed_ref[:, :cap, :] = packed[:, :, :width]
    packed_ref[:, cap:cap + half, :] = jnp.concatenate([packed[:, :half, width:], packed[:, half:, width:]], axis=2)
    first = lax.axis_index("tile") * cap
    by_owner = jnp.where(lax.broadcasted_iota(jnp.int32, (owners, entries), 0) == owner, local_row, 0.0).astype(bf16)
    by_lane = jnp.where(lax.broadcasted_iota(jnp.int32, (width, entries), 0) == first % width + rank, 1.0, 0.0).astype(bf16)
    numbers = lax.dot_general(by_owner, by_lane, lanes_contract, preferred_element_type=f32)
    line = lax.broadcasted_iota(jnp.int32, (owners, 8, width), 1)
    packed_ref[:, cap + half:, :] = jnp.where(line == first // width, numbers[:, None, :], 0.0)


def reduce_kernel(cap, sources, received_ref, right_hbm, *refs):
    reduced_refs, right_ref, sem = refs[:-2], refs[-2], refs[-1]
    move = pltpu.make_async_copy(right_hbm, right_ref, sem)
    move.start()
    owners, height, width = received_ref.shape
    slots = owners * cap
    columns, own_rows = right_ref.shape
    if height > cap:
        half = cap // 2
        numbers = jnp.sum(received_ref[:, cap + half:, :], axis=0)
        numbers = jnp.concatenate([numbers[i:i + 1] for i in range(slots // width)], axis=1).astype(jnp.int32)
        rest = received_ref[:, cap:cap + half, :]
        rest = jnp.concatenate([rest[:, :, :width // 2], rest[:, :, width // 2:]], axis=1)
        sets = [received_ref[:, :cap, :].reshape(slots, width), rest.reshape(slots, width // 2)]
        place = jnp.where(lax.broadcasted_iota(jnp.int32, (own_rows, slots), 0) == numbers, 1.0, 0.0).astype(bf16)
        totals = []
        for value in sets:
            total = jnp.zeros((own_rows, value.shape[1]), f32)
            for piece in halves_of(value):
                total += jnp.dot(place, piece, preferred_element_type=f32)
            totals.append(total.T)
        total = jnp.concatenate(totals, axis=0)
    else:
        received = received_ref[...].reshape(slots, width)
        local_row = received[:, columns:columns + 1].astype(jnp.int32)
        place = jnp.where(lax.broadcasted_iota(jnp.int32, (slots, own_rows), 1) == local_row, 1.0, 0.0).astype(bf16)
        total = jnp.zeros((columns, own_rows), f32)
        for piece in halves_of(received[:, :columns].T):
            total += jnp.dot(piece, place, preferred_element_type=f32)
    move.wait()
    reduced = right_ref[...] - total
    share = sources // len(reduced_refs)
    for group in range(columns // sources):
        for chain, reduced_ref in enumerate(reduced_refs):
            start = group * sources + chain * share
            reduced_ref[group * share:(group + 1) * share, :] = reduced[start:start + share]


def split_kernel(block, relative, matrix_ref, high_ref, low_ref):
    parts, own_rows, full_rows = matrix_ref.shape
    groups, rows, width = high_ref.shape
    layers = width // block
    height = 64
    for part in range(parts):
        for first in range(0, own_rows, height):
            start = part * own_rows + first
            for group in range(groups):
                for layer in range(layers):
                    column = (layer * groups + group if relative else group * layers + layer) * block
                    high, low = halves_of(matrix_ref[part, first:first + height, column:column + block])
                    high_ref[group, start:start + height, layer * block:(layer + 1) * block] = high
                    low_ref[group, start:start + height, layer * block:(layer + 1) * block] = low


def split_blocks(matrix, block, relative):
    parts, own_rows, full_rows = matrix.shape
    groups = 4 if full_rows % (4 * block) == 0 else 1
    vmem = pl.BlockSpec(memory_space=pltpu.VMEM)
    shape = jax.ShapeDtypeStruct((groups, parts * own_rows, full_rows // groups), bf16)
    return pl.pallas_call(
        functools.partial(split_kernel, block, relative),
        in_specs=[vmem],
        out_specs=[vmem, vmem],
        out_shape=[shape, shape],
        compiler_params=kernel_params(20),
        cost_estimate=pl.CostEstimate(flops=3 * matrix.size, bytes_accessed=8 * matrix.size, transcendentals=0),
    )(matrix)


def product_kernel(share, layout, inputs, sets, block, begin, end, onward, relative, merged, *refs):
    high_ref, low_ref = refs[inputs * sets:inputs * sets + 2]
    rest = refs[inputs * sets + 2:]
    groups, both_rows, width = high_ref.shape
    layers = width // block
    own_rows = both_rows // 2
    start_ref, rest = (rest[0], rest[1:]) if begin > 0 else (None, rest)
    earlier_refs, rest = rest[:merged], rest[merged:]
    out_ref, total_ref = rest if end == groups else (None, rest[0])
    columns = total_ref.shape[0]
    me = lax.axis_index("tile")

    def block_of(step, layer):
        held = lax.rem(lax.div(me, 4) + (layers - layer), layers) if relative else layer
        which, place = layout(step, held)
        value = refs[which][place]
        return refs[inputs + which][place] - value if sets == 2 else value

    @pl.when(jnp.logical_not(onward) | (lax.axis_index("chain") < lax.axis_size("chain") - 1))
    def _():
        for step in range(begin, end):
            group = step
            if relative:
                group = lax.rem(lax.div(me, 2) + step % 2, 2) * 2 + lax.rem(me + step // 2, 2)
            x_high, x_low = halves_of(jnp.concatenate([block_of(step, layer) for layer in range(layers)], axis=1))
            lhs = jnp.concatenate([x_high, x_low], axis=0)
            both = lax.dot_general(lhs, high_ref[group], lanes_contract, preferred_element_type=f32)
            part = both[:columns] + both[columns:]
            part += lax.dot_general(x_high, low_ref[group], lanes_contract, preferred_element_type=f32)
            if step > begin:
                total_ref[...] += part
            elif start_ref is None:
                total_ref[...] = part
            else:
                total_ref[...] = start_ref[...] + part
        if out_ref is None:
            return
        for first in range(0, columns, 2 * share):
            real = pl.ds(first, share)
            imag = pl.ds(first + share, share)
            results = [
                total_ref[real, :own_rows] - total_ref[imag, own_rows:],
                total_ref[imag, :own_rows] + total_ref[real, own_rows:],
            ]
            for half, result in enumerate(results):
                row = first + half * share
                place = row * (merged + 1)
                for chain, earlier_ref in enumerate(earlier_refs):
                    out_ref[place + chain * share:place + (chain + 1) * share, :] = earlier_ref[row:row + share, :]
                out_ref[place + merged * share:place + (merged + 1) * share, :] = result


def product_part(split, onward, layout, blocks, own, begin, end, started, share, relative, earlier=()):
    groups, both_rows, width = split[0].shape
    columns, block = blocks[0].shape[-2:]
    vmem = pl.BlockSpec(memory_space=pltpu.VMEM)
    finish = end == groups
    arrays = list(blocks) + list(own) + list(split) + ([] if started is None else [started]) + list(earlier)
    out_rows = columns * (len(earlier) + 1)
    sets = 2 if own else 1
    return pl.pallas_call(
        functools.partial(product_kernel, share, layout, len(blocks), sets, block, begin, end, onward, relative, len(earlier)),
        in_specs=[vmem] * len(arrays),
        out_specs=vmem,
        out_shape=jax.ShapeDtypeStruct((out_rows, both_rows // 2) if finish else (columns, both_rows), f32),
        scratch_shapes=[pltpu.VMEM((columns, both_rows), f32)] if finish else [],
        compiler_params=kernel_params(20),
        cost_estimate=pl.CostEstimate(flops=6 * columns * both_rows * width * (end - begin), bytes_accessed=MIB, transcendentals=0),
    )(*arrays)


def tied(value, to):
    return lax.optimization_barrier((value, to))[0]


def solve_paired(reduced, diag_inverse, coupling, share):
    chain_size = lax.axis_size("chain")
    tile_size = lax.axis_size("tile")
    own_rows = reduced[0].shape[1]
    layers = tile_size // 4

    def send(value, hop, target):
        if not hop:
            return lax.ppermute(value, "tile", [(t, target(t)) for t in range(tile_size)])
        pairs = [(c * tile_size + t, (c + 1) * tile_size + target(t)) for c in range(chain_size - 1) for t in range(tile_size)]
        return lax.ppermute(value, ("chain", "tile"), pairs)

    def along(value, hop):
        return [value if by == 0 and not hop else send(value, hop, lambda t: (t + 4 * by) % tile_size) for by in range(layers)]

    def finished(line, after):
        far = send(line, False, lambda t: t ^ 2)
        held = [line, far if after is None else tied(far, after)]
        return held, [send(each, False, lambda t: t ^ 1) for each in held]

    def layout(step, held):
        return step % 2, (held,)

    def products(split, onward, held, other, own, earlier=()):
        mine, theirs = own if own else ([], [])
        started = product_part(split, onward, layout, held, mine, 0, 2, None, share, True)
        return product_part(split, onward, layout, other, theirs, 2, 4, started, share, True, earlier)

    only = chain_size == 1
    first = along(reduced[0], False)
    split = split_blocks(tied(diag_inverse if only else coupling, reduced[0]), own_rows, True)
    lines = [tied(jnp.stack(first), split)]
    lines += [jnp.stack(along(tied(value, split), False)) for value in reduced[1:]]
    after = None
    if not only:
        after = diag_split = split_blocks(tied(diag_inverse, lines[0]), own_rows, True)
    own, carried, pieces = [], [], []
    for chain in range(CHAINS):
        own.append(finished(lines[chain], after))
        carried.append(products(split, not only, *own[chain], None, tuple(carried) if only else ()))
        pieces.append(along(carried[chain], not only))
        after = carried[chain]
    for step in range(1, chain_size):
        last = step == chain_size - 1
        lines = [jnp.stack(each) for each in pieces]
        lines[0] = tied(lines[0], carried[-1])
        carried, pieces, after = [], [], None
        for chain in range(CHAINS):
            arrived = finished(lines[chain], after)
            matrix = diag_split if last else split
            carried.append(products(matrix, not last, *arrived, own[chain], tuple(carried) if last else ()))
            after = carried[chain]
            if not last:
                pieces.append(along(carried[chain], True))
    return carried[-1]


def solve_flat(reduced, diag_inverse, coupling, sources):
    chain_size = lax.axis_size("chain")
    reduced = reduced[0]
    columns = reduced.shape[0]
    full_rows = diag_inverse.shape[2]
    block = min(256, full_rows)
    count = full_rows // block

    def layout(step, held):
        return 0, (step * layers + held,)

    onward = [(i, i + 1) for i in range(chain_size - 1)]
    diag_split = split_blocks(diag_inverse, block, False)
    coupling_split = split_blocks(coupling, block, False)
    groups = diag_split[0].shape[0]
    layers = count // groups

    def gathered(value):
        whole = lax.all_gather(value, "tile", axis=1, tiled=True)
        return [whole.reshape(columns, count, block).transpose(1, 0, 2)]

    current = reduced
    for _ in range(chain_size - 1):
        carried = product_part(coupling_split, True, layout, gathered(current), [], 0, groups, None, sources, False)
        current = reduced - lax.ppermute(carried, "chain", onward)
    return product_part(diag_split, False, layout, gathered(current), [], 0, groups, None, sources, False)


def body(right_side, diag_inverse, coupling, updates, update_rows, tile_counts):
    batches, halves, sources, own_rows = right_side.shape
    tile_size = lax.axis_size("tile")
    entries, columns = updates.shape
    tile_rows = entries // tile_counts.shape[0]
    cap = 2 * entries // tile_size
    slots = tile_size * cap
    vmem = pl.BlockSpec(memory_space=pltpu.VMEM)
    hbm = pl.BlockSpec(memory_space=pltpu.HBM)
    folded = cap % 16 == 0 and slots <= 1024 and columns == 192 and own_rows <= 256 and 128 % cap == 0
    width = 128 if folded else -(-(columns + 1) // 128) * 128
    height = cap + cap // 2 + 8 if folded else cap
    packed = pl.pallas_call(
        functools.partial(pack_kernel, own_rows, cap, tile_rows),
        in_specs=[hbm, hbm, hbm],
        out_specs=vmem,
        out_shape=jax.ShapeDtypeStruct((tile_size, height, width), f32),
        scratch_shapes=[
            pltpu.SMEM(tile_counts.shape, jnp.int32),
            pltpu.VMEM((1, entries), jnp.int32),
            pltpu.VMEM((columns, entries), f32),
            pltpu.SemaphoreType.DMA((3,)),
        ],
        compiler_params=kernel_params(56),
    )(tile_counts, update_rows[None, :], updates.T)
    received = lax.all_to_all(packed, "tile", 0, 0, tiled=False)
    paired = own_rows % 128 == 0 and tile_size % 8 == 0 and sources % (8 * CHAINS) == 0
    shares = [columns // CHAINS] * CHAINS if paired else [columns]
    reduced = pl.pallas_call(
        functools.partial(reduce_kernel, cap, sources),
        in_specs=[vmem, hbm],
        out_specs=[vmem] * len(shares),
        out_shape=[jax.ShapeDtypeStruct((rows, own_rows), f32) for rows in shares],
        scratch_shapes=[pltpu.VMEM((columns, own_rows), f32), pltpu.SemaphoreType.DMA(())],
        compiler_params=kernel_params(20),
    )(received, right_side.reshape(columns, own_rows))
    if paired:
        return solve_paired(reduced, diag_inverse, coupling, sources // CHAINS).reshape(right_side.shape)
    return solve_flat(reduced, diag_inverse, coupling, sources).reshape(right_side.shape)


def solution(mesh):
    in_specs = (
        P(None, None, None, ("chain", "tile")),
        P(None, ("chain", "tile"), None),
        P(None, ("chain", "tile"), None),
        P(("chain", "tile"), None),
        P(("chain", "tile")),
        P(("chain", "tile")),
    )
    out_specs = P(None, None, None, ("chain", "tile"))
    return jax.shard_map(body, mesh=mesh, in_specs=in_specs, out_specs=out_specs, check_vma=False)
```

```python
import functools

import jax
import jax.numpy as jnp
from jax import lax
from jax.experimental import pallas as pl
from jax.experimental.pallas import tpu as pltpu
from jax.sharding import PartitionSpec as P

MIB = 1 << 20
f32 = jnp.float32
bf16 = jnp.bfloat16
lanes_contract = (((1,), (1,)), ((), ()))


def halves_of(value):
    high = value.astype(bf16)
    return high, (value - high.astype(f32)).astype(bf16)


def kernel_params(size):
    return pltpu.CompilerParams(vmem_limit_bytes=int(size * MIB))


def pack_kernel(own_rows, cap, tile_rows, counts_hbm, rows_hbm, updates_hbm, packed_ref, counts_ref, rows_ref, updates_ref, sems):
    moves = [
        pltpu.make_async_copy(counts_hbm, counts_ref, sems.at[0]),
        pltpu.make_async_copy(rows_hbm, rows_ref, sems.at[1]),
        pltpu.make_async_copy(updates_hbm, updates_ref, sems.at[2]),
    ]
    for move in moves:
        move.start()
    columns, entries = updates_ref.shape
    owners, height, width = packed_ref.shape
    slots = owners * cap
    entry = lax.broadcasted_iota(jnp.int32, (1, entries), 1)
    earlier = lax.broadcasted_iota(jnp.int32, (entries, entries), 0) < lax.broadcasted_iota(jnp.int32, (entries, entries), 1)
    for move in moves:
        move.wait()
    live = jnp.zeros((1, entries), jnp.bool_)
    for tile in range(entries // tile_rows):
        start = tile * tile_rows
        live = live | ((entry >= start) & (entry < start + counts_ref[tile]))
    rows = rows_ref[...]
    owner = rows // own_rows
    lane_owner = jnp.broadcast_to(owner.astype(f32), (entries, entries))
    rank = jnp.sum(jnp.where(earlier & (lane_owner.T == lane_owner), 1, 0), axis=0, keepdims=True)
    slot = owner * cap + rank
    choose = jnp.where(lax.broadcasted_iota(jnp.int32, (slots, entries), 0) == slot, 1.0, 0.0).astype(bf16)
    data = jnp.where(live, updates_ref[...], 0.0)
    local_row = (rows - owner * own_rows).astype(f32)
    folded = height > cap
    if not folded:
        tail = jnp.where(lax.broadcasted_iota(jnp.int32, (width - columns, entries), 0) == 0, local_row, 0.0)
        data = jnp.concatenate([data, tail], axis=0)
    packed = jnp.zeros((slots, data.shape[0]), f32)
    for piece in halves_of(data):
        packed += lax.dot_general(choose, piece, lanes_contract, preferred_element_type=f32)
    packed = packed.reshape(owners, cap, data.shape[0])
    if not folded:
        packed_ref[...] = packed
        return
    half = cap // 2
    packed_ref[:, :cap, :] = packed[:, :, :width]
    packed_ref[:, cap:cap + half, :] = jnp.concatenate([packed[:, :half, width:], packed[:, half:, width:]], axis=2)
    first = lax.axis_index("tile") * cap
    by_owner = jnp.where(lax.broadcasted_iota(jnp.int32, (owners, entries), 0) == owner, local_row, 0.0).astype(bf16)
    by_lane = jnp.where(lax.broadcasted_iota(jnp.int32, (width, entries), 0) == first % width + rank, 1.0, 0.0).astype(bf16)
    numbers = lax.dot_general(by_owner, by_lane, lanes_contract, preferred_element_type=f32)
    line = lax.broadcasted_iota(jnp.int32, (owners, 8, width), 1)
    packed_ref[:, cap + half:, :] = jnp.where(line == first // width, numbers[:, None, :], 0.0)


def reduce_kernel(cap, received_ref, right_hbm, *refs):
    reduced_refs, right_ref, sem = refs[:-2], refs[-2], refs[-1]
    move = pltpu.make_async_copy(right_hbm, right_ref, sem)
    move.start()
    owners, height, width = received_ref.shape
    slots = owners * cap
    columns, own_rows = right_ref.shape
    if height > cap:
        half = cap // 2
        numbers = jnp.sum(received_ref[:, cap + half:, :], axis=0)
        numbers = jnp.concatenate([numbers[i:i + 1] for i in range(slots // width)], axis=1).astype(jnp.int32)
        rest = received_ref[:, cap:cap + half, :]
        rest = jnp.concatenate([rest[:, :, :width // 2], rest[:, :, width // 2:]], axis=1)
        sets = [received_ref[:, :cap, :].reshape(slots, width), rest.reshape(slots, width // 2)]
        place = jnp.where(lax.broadcasted_iota(jnp.int32, (own_rows, slots), 0) == numbers, 1.0, 0.0).astype(bf16)
        totals = []
        for value in sets:
            total = jnp.zeros((own_rows, value.shape[1]), f32)
            for piece in halves_of(value):
                total += jnp.dot(place, piece, preferred_element_type=f32)
            totals.append(total.T)
        total = jnp.concatenate(totals, axis=0)
    else:
        received = received_ref[...].reshape(slots, width)
        local_row = received[:, columns:columns + 1].astype(jnp.int32)
        place = jnp.where(lax.broadcasted_iota(jnp.int32, (slots, own_rows), 1) == local_row, 1.0, 0.0).astype(bf16)
        total = jnp.zeros((columns, own_rows), f32)
        for piece in halves_of(received[:, :columns].T):
            total += jnp.dot(piece, place, preferred_element_type=f32)
    move.wait()
    start = 0
    for reduced_ref in reduced_refs:
        rows = reduced_ref.shape[0]
        reduced_ref[...] = right_ref[start:start + rows, :] - total[start:start + rows]
        start += rows


def split_kernel(block, relative, matrix_ref, high_ref, low_ref):
    parts, own_rows, full_rows = matrix_ref.shape
    groups, rows, width = high_ref.shape
    layers = width // block
    height = 64
    for part in range(parts):
        for first in range(0, own_rows, height):
            start = part * own_rows + first
            for group in range(groups):
                for layer in range(layers):
                    column = (layer * groups + group if relative else group * layers + layer) * block
                    high, low = halves_of(matrix_ref[part, first:first + height, column:column + block])
                    high_ref[group, start:start + height, layer * block:(layer + 1) * block] = high
                    low_ref[group, start:start + height, layer * block:(layer + 1) * block] = low


def split_blocks(matrix, block, relative):
    parts, own_rows, full_rows = matrix.shape
    groups = 4 if full_rows % (4 * block) == 0 else 1
    vmem = pl.BlockSpec(memory_space=pltpu.VMEM)
    shape = jax.ShapeDtypeStruct((groups, parts * own_rows, full_rows // groups), bf16)
    return pl.pallas_call(
        functools.partial(split_kernel, block, relative),
        in_specs=[vmem],
        out_specs=[vmem, vmem],
        out_shape=[shape, shape],
        compiler_params=kernel_params(20),
        cost_estimate=pl.CostEstimate(flops=3 * matrix.size, bytes_accessed=8 * matrix.size, transcendentals=0),
    )(matrix)


def product_kernel(sources, layout, inputs, sets, block, begin, end, onward, relative, *refs):
    high_ref, low_ref = refs[inputs * sets:inputs * sets + 2]
    rest = refs[inputs * sets + 2:]
    groups, both_rows, width = high_ref.shape
    layers = width // block
    own_rows = both_rows // 2
    start_ref, rest = (rest[0], rest[1:]) if begin > 0 else (None, rest)
    out_refs, total_ref = (rest[:-1], rest[-1]) if end == groups else ((), rest[0])
    columns = total_ref.shape[0]
    me = lax.axis_index("tile")

    def block_of(step, layer):
        held = lax.rem(lax.div(me, 4) + (layers - layer), layers) if relative else layer
        pieces = []
        for group in layout:
            which, place = group(step, held)
            value = refs[which][place]
            if sets == 2:
                own = refs[inputs + which][place]
                value = jnp.where(lax.axis_index("chain") == 0, own, own - value)
            pieces.append(value)
        return jnp.concatenate(pieces, axis=0)

    active = jnp.logical_not(onward) | (lax.axis_index("chain") < lax.axis_size("chain") - 1)

    @pl.when(jnp.logical_not(active))
    def _():
        for out_ref in out_refs:
            out_ref[...] = jnp.zeros_like(out_ref)

    @pl.when(active)
    def _():
        for step in range(begin, end):
            group = step
            if relative:
                group = lax.rem(lax.div(me, 2) + step % 2, 2) * 2 + lax.rem(me + step // 2, 2)
            x_high, x_low = halves_of(jnp.concatenate([block_of(step, layer) for layer in range(layers)], axis=1))
            lhs = jnp.concatenate([x_high, x_low], axis=0)
            both = lax.dot_general(lhs, high_ref[group], lanes_contract, preferred_element_type=f32)
            part = both[:columns] + both[columns:]
            part += lax.dot_general(x_high, low_ref[group], lanes_contract, preferred_element_type=f32)
            if step > begin:
                total_ref[...] += part
            elif start_ref is None:
                total_ref[...] = part
            else:
                total_ref[...] = start_ref[...] + part
        start = 0
        for out_ref in out_refs:
            for first in range(0, out_ref.shape[0], 2 * sources):
                real = pl.ds(start + first, sources)
                imag = pl.ds(start + first + sources, sources)
                out_ref[first:first + sources, :] = total_ref[real, :own_rows] - total_ref[imag, own_rows:]
                out_ref[first + sources:first + 2 * sources, :] = total_ref[imag, :own_rows] + total_ref[real, own_rows:]
            start += out_ref.shape[0]


def product_part(split, onward, layout, blocks, own, begin, end, started, sources, shares, relative):
    groups, both_rows, width = split[0].shape
    block = blocks[0].shape[-1]
    vmem = pl.BlockSpec(memory_space=pltpu.VMEM)
    finish = end == groups
    whole = (sum(shares), both_rows)
    arrays = list(blocks) + list(own) + list(split) + ([] if started is None else [started])
    if finish:
        out_shape = [jax.ShapeDtypeStruct((rows, both_rows // 2), f32) for rows in shares]
    else:
        out_shape = jax.ShapeDtypeStruct(whole, f32)
    return pl.pallas_call(
        functools.partial(product_kernel, sources, layout, len(blocks), 2 if own else 1, block, begin, end, onward, relative),
        in_specs=[vmem] * len(arrays),
        out_specs=[vmem] * len(shares) if finish else vmem,
        out_shape=out_shape,
        scratch_shapes=[pltpu.VMEM(whole, f32)] if finish else [],
        compiler_params=kernel_params(20),
        cost_estimate=pl.CostEstimate(flops=6 * sum(shares) * both_rows * width * (end - begin), bytes_accessed=MIB, transcendentals=0),
    )(*arrays)


def tied(value, to):
    return lax.optimization_barrier((value, to))[0]


def solve_paired(reduced, diag_inverse, coupling, sources):
    chain_size = lax.axis_size("chain")
    tile_size = lax.axis_size("tile")
    own_rows = reduced[0].shape[1]
    shares = [each.shape[0] for each in reduced]
    layers = tile_size // 4

    def send(value, hop, target):
        if not hop:
            return lax.ppermute(value, "tile", [(t, target(t)) for t in range(tile_size)])
        pairs = [(c * tile_size + t, (c + 1) % chain_size * tile_size + target(t)) for c in range(chain_size) for t in range(tile_size)]
        return lax.ppermute(value, ("chain", "tile"), pairs)

    def first_stage(first, second, hop):
        pair = [second if across == 0 and not hop else send(second, hop, lambda t: t ^ (2 * across)) for across in range(2)]
        line = [first if by == 0 and not hop else send(first, hop, lambda t: (t + 4 * by) % tile_size) for by in range(layers)]
        return jnp.stack(pair), jnp.stack(line)

    def second_stage(pair, line):
        far = send(line, False, lambda t: t ^ 2)
        rest = [pair if by == 0 else send(pair, False, lambda t: (t + 4 * by) % tile_size) for by in range(layers)]
        return [line, far, jnp.stack(rest)]

    layout = [lambda step, held: (step % 2, (held,)), lambda step, held: (2, (held, step % 2))]

    def products(split, onward, held, own, shares):
        other = [send(each, False, lambda t: t ^ 1) for each in held]
        mine, theirs = own if own else ([], [])
        started = product_part(split, onward, layout, held, mine, 0, 2, None, sources, shares, True)
        return product_part(split, onward, layout, other, theirs, 2, 4, started, sources, shares, True), other

    only = chain_size == 1
    pair, line = first_stage(*reduced, False)
    split = split_blocks(tied(diag_inverse if only else coupling, reduced[0]), own_rows, True)
    pair, line, split = lax.optimization_barrier((pair, line, split))
    held = second_stage(pair, line)
    if only:
        return products(split, False, held, None, [sum(shares)])[0][0]
    diag_split = split_blocks(tied(diag_inverse, line), own_rows, True)
    held[1], held[2], diag_split = lax.optimization_barrier((held[1], held[2], diag_split))
    carried, other = products(split, True, held, None, shares)
    own = (held, other)
    for step in range(chain_size - 1):
        held = second_stage(*lax.optimization_barrier(first_stage(*carried, True)))
        if step < chain_size - 2:
            carried = products(split, True, held, own, shares)[0]
    return products(diag_split, False, held, own, [sum(shares)])[0][0]


def solve_flat(reduced, diag_inverse, coupling, sources):
    chain_size = lax.axis_size("chain")
    reduced = reduced[0]
    columns = reduced.shape[0]
    full_rows = diag_inverse.shape[2]
    block = min(256, full_rows)
    count = full_rows // block
    layout = [lambda step, held: (0, (step * layers + held,))]
    onward = [(i, i + 1) for i in range(chain_size - 1)]
    diag_split = split_blocks(diag_inverse, block, False)
    coupling_split = split_blocks(coupling, block, False)
    groups = diag_split[0].shape[0]
    layers = count // groups

    def gathered(value):
        whole = lax.all_gather(value, "tile", axis=1, tiled=True)
        return [whole.reshape(columns, count, block).transpose(1, 0, 2)]

    current = reduced
    for _ in range(chain_size - 1):
        carried = product_part(coupling_split, True, layout, gathered(current), [], 0, groups, None, sources, [columns], False)[0]
        current = reduced - lax.ppermute(carried, "chain", onward)
    return product_part(diag_split, False, layout, gathered(current), [], 0, groups, None, sources, [columns], False)[0]


def body(right_side, diag_inverse, coupling, updates, update_rows, tile_counts):
    batches, halves, sources, own_rows = right_side.shape
    tile_size = lax.axis_size("tile")
    entries, columns = updates.shape
    tile_rows = entries // tile_counts.shape[0]
    cap = 2 * entries // tile_size
    slots = tile_size * cap
    vmem = pl.BlockSpec(memory_space=pltpu.VMEM)
    hbm = pl.BlockSpec(memory_space=pltpu.HBM)
    folded = cap % 16 == 0 and slots <= 1024 and columns == 192 and own_rows <= 256 and 128 % cap == 0
    width = 128 if folded else -(-(columns + 1) // 128) * 128
    height = cap + cap // 2 + 8 if folded else cap
    packed = pl.pallas_call(
        functools.partial(pack_kernel, own_rows, cap, tile_rows),
        in_specs=[hbm, hbm, hbm],
        out_specs=vmem,
        out_shape=jax.ShapeDtypeStruct((tile_size, height, width), f32),
        scratch_shapes=[
            pltpu.SMEM(tile_counts.shape, jnp.int32),
            pltpu.VMEM((1, entries), jnp.int32),
            pltpu.VMEM((columns, entries), f32),
            pltpu.SemaphoreType.DMA((3,)),
        ],
        compiler_params=kernel_params(56),
    )(tile_counts, update_rows[None, :], updates.T)
    received = lax.all_to_all(packed, "tile", 0, 0, tiled=False)
    paired = own_rows % 128 == 0 and tile_size % 8 == 0 and batches > 1
    early = batches * 2 // 3 * halves * sources
    shares = [early, columns - early] if paired else [columns]
    reduced = pl.pallas_call(
        functools.partial(reduce_kernel, cap),
        in_specs=[vmem, hbm],
        out_specs=[vmem] * len(shares),
        out_shape=[jax.ShapeDtypeStruct((rows, own_rows), f32) for rows in shares],
        scratch_shapes=[pltpu.VMEM((columns, own_rows), f32), pltpu.SemaphoreType.DMA(())],
        compiler_params=kernel_params(20),
    )(received, right_side.reshape(columns, own_rows))
    solve = solve_paired if paired else solve_flat
    return solve(reduced, diag_inverse, coupling, sources).reshape(right_side.shape)


def solution(mesh):
    in_specs = (
        P(None, None, None, ("chain", "tile")),
        P(None, ("chain", "tile"), None),
        P(None, ("chain", "tile"), None),
        P(("chain", "tile"), None),
        P(("chain", "tile")),
        P(("chain", "tile")),
    )
    out_specs = P(None, None, None, ("chain", "tile"))
    return jax.shard_map(body, mesh=mesh, in_specs=in_specs, out_specs=out_specs, check_vma=False)
```

```python
import functools

import jax
import jax.numpy as jnp
from jax import lax
from jax.experimental import pallas as pl
from jax.experimental.pallas import tpu as pltpu
from jax.sharding import PartitionSpec as P

MIB = 1 << 20
f32 = jnp.float32
bf16 = jnp.bfloat16
lanes_contract = (((1,), (1,)), ((), ()))


def halves_of(value):
    high = value.astype(bf16)
    return high, (value - high.astype(f32)).astype(bf16)


def kernel_params(size):
    return pltpu.CompilerParams(vmem_limit_bytes=int(size * MIB))


def pack_kernel(own_rows, cap, tile_rows, counts_hbm, rows_hbm, updates_hbm, packed_ref, counts_ref, rows_ref, updates_ref, sems):
    moves = [
        pltpu.make_async_copy(counts_hbm, counts_ref, sems.at[0]),
        pltpu.make_async_copy(rows_hbm, rows_ref, sems.at[1]),
        pltpu.make_async_copy(updates_hbm, updates_ref, sems.at[2]),
    ]
    for move in moves:
        move.start()
    columns, entries = updates_ref.shape
    owners, height, width = packed_ref.shape
    slots = owners * cap
    entry = lax.broadcasted_iota(jnp.int32, (1, entries), 1)
    earlier = lax.broadcasted_iota(jnp.int32, (entries, entries), 0) < lax.broadcasted_iota(jnp.int32, (entries, entries), 1)
    for move in moves:
        move.wait()
    live = jnp.zeros((1, entries), jnp.bool_)
    for tile in range(entries // tile_rows):
        start = tile * tile_rows
        live = live | ((entry >= start) & (entry < start + counts_ref[tile]))
    rows = rows_ref[...]
    owner = rows // own_rows
    lane_owner = jnp.broadcast_to(owner.astype(f32), (entries, entries))
    rank = jnp.sum(jnp.where(earlier & (lane_owner.T == lane_owner), 1, 0), axis=0, keepdims=True)
    slot = owner * cap + rank
    choose = jnp.where(lax.broadcasted_iota(jnp.int32, (slots, entries), 0) == slot, 1.0, 0.0).astype(bf16)
    data = jnp.where(live, updates_ref[...], 0.0)
    local_row = (rows - owner * own_rows).astype(f32)
    folded = height > cap
    if not folded:
        tail = jnp.where(lax.broadcasted_iota(jnp.int32, (width - columns, entries), 0) == 0, local_row, 0.0)
        data = jnp.concatenate([data, tail], axis=0)
    packed = jnp.zeros((slots, data.shape[0]), f32)
    for piece in halves_of(data):
        packed += lax.dot_general(choose, piece, lanes_contract, preferred_element_type=f32)
    packed = packed.reshape(owners, cap, data.shape[0])
    if not folded:
        packed_ref[...] = packed
        return
    half = cap // 2
    packed_ref[:, :cap, :] = packed[:, :, :width]
    packed_ref[:, cap:cap + half, :] = jnp.concatenate([packed[:, :half, width:], packed[:, half:, width:]], axis=2)
    first = lax.axis_index("tile") * cap
    by_owner = jnp.where(lax.broadcasted_iota(jnp.int32, (owners, entries), 0) == owner, local_row, 0.0).astype(bf16)
    by_lane = jnp.where(lax.broadcasted_iota(jnp.int32, (width, entries), 0) == first % width + rank, 1.0, 0.0).astype(bf16)
    numbers = lax.dot_general(by_owner, by_lane, lanes_contract, preferred_element_type=f32)
    line = lax.broadcasted_iota(jnp.int32, (owners, 8, width), 1)
    packed_ref[:, cap + half:, :] = jnp.where(line == first // width, numbers[:, None, :], 0.0)


def reduce_kernel(cap, received_ref, right_hbm, *refs):
    reduced_refs, right_ref, sem = refs[:-2], refs[-2], refs[-1]
    move = pltpu.make_async_copy(right_hbm, right_ref, sem)
    move.start()
    owners, height, width = received_ref.shape
    slots = owners * cap
    columns, own_rows = right_ref.shape
    if height > cap:
        half = cap // 2
        numbers = jnp.sum(received_ref[:, cap + half:, :], axis=0)
        numbers = jnp.concatenate([numbers[i:i + 1] for i in range(slots // width)], axis=1).astype(jnp.int32)
        rest = received_ref[:, cap:cap + half, :]
        rest = jnp.concatenate([rest[:, :, :width // 2], rest[:, :, width // 2:]], axis=1)
        sets = [received_ref[:, :cap, :].reshape(slots, width), rest.reshape(slots, width // 2)]
        place = jnp.where(lax.broadcasted_iota(jnp.int32, (own_rows, slots), 0) == numbers, 1.0, 0.0).astype(bf16)
        totals = []
        for value in sets:
            total = jnp.zeros((own_rows, value.shape[1]), f32)
            for piece in halves_of(value):
                total += jnp.dot(place, piece, preferred_element_type=f32)
            totals.append(total.T)
        total = jnp.concatenate(totals, axis=0)
    else:
        received = received_ref[...].reshape(slots, width)
        local_row = received[:, columns:columns + 1].astype(jnp.int32)
        place = jnp.where(lax.broadcasted_iota(jnp.int32, (slots, own_rows), 1) == local_row, 1.0, 0.0).astype(bf16)
        total = jnp.zeros((columns, own_rows), f32)
        for piece in halves_of(received[:, :columns].T):
            total += jnp.dot(piece, place, preferred_element_type=f32)
    move.wait()
    start = 0
    for reduced_ref in reduced_refs:
        rows = reduced_ref.shape[0]
        reduced_ref[...] = right_ref[start:start + rows, :] - total[start:start + rows]
        start += rows


def split_kernel(block, relative, matrix_ref, high_ref, low_ref):
    parts, own_rows, full_rows = matrix_ref.shape
    groups, rows, width = high_ref.shape
    layers = width // block
    height = 64
    for part in range(parts):
        for first in range(0, own_rows, height):
            start = part * own_rows + first
            for group in range(groups):
                for layer in range(layers):
                    column = (layer * groups + group if relative else group * layers + layer) * block
                    high, low = halves_of(matrix_ref[part, first:first + height, column:column + block])
                    high_ref[group, start:start + height, layer * block:(layer + 1) * block] = high
                    low_ref[group, start:start + height, layer * block:(layer + 1) * block] = low


def split_blocks(matrix, block, relative):
    parts, own_rows, full_rows = matrix.shape
    groups = 4 if full_rows % (4 * block) == 0 else 1
    vmem = pl.BlockSpec(memory_space=pltpu.VMEM)
    shape = jax.ShapeDtypeStruct((groups, parts * own_rows, full_rows // groups), bf16)
    return pl.pallas_call(
        functools.partial(split_kernel, block, relative),
        in_specs=[vmem],
        out_specs=[vmem, vmem],
        out_shape=[shape, shape],
        compiler_params=kernel_params(20),
        cost_estimate=pl.CostEstimate(flops=3 * matrix.size, bytes_accessed=8 * matrix.size, transcendentals=0),
    )(matrix)


def put(out_refs, first, value):
    start = 0
    for out_ref in out_refs:
        low = max(first, start)
        high = min(first + value.shape[0], start + out_ref.shape[0])
        if low < high:
            out_ref[low - start:high - start, :] = value[low - first:high - first]
        start += out_ref.shape[0]


def product_kernel(sources, layout, inputs, sets, block, begin, end, onward, relative, *refs):
    high_ref, low_ref = refs[inputs * sets:inputs * sets + 2]
    rest = refs[inputs * sets + 2:]
    groups, both_rows, width = high_ref.shape
    layers = width // block
    own_rows = both_rows // 2
    start_ref, rest = (rest[0], rest[1:]) if begin > 0 else (None, rest)
    out_refs, total_ref = (rest[:-1], rest[-1]) if end == groups else ((), rest[0])
    columns = total_ref.shape[0]
    me = lax.axis_index("tile")

    def block_of(step, layer):
        held = lax.rem(lax.div(me, 4) + (layers - layer), layers) if relative else layer
        pieces = []
        for group in layout:
            which, place = group(step, held)
            value = refs[which][place]
            if sets == 2:
                own = refs[inputs + which][place]
                value = jnp.where(lax.axis_index("chain") == 0, own, own - value)
            pieces.append(value)
        return jnp.concatenate(pieces, axis=0)

    active = jnp.logical_not(onward) | (lax.axis_index("chain") < lax.axis_size("chain") - 1)

    @pl.when(jnp.logical_not(active))
    def _():
        for out_ref in out_refs:
            out_ref[...] = jnp.zeros_like(out_ref)

    @pl.when(active)
    def _():
        for step in range(begin, end):
            group = step
            if relative:
                group = lax.rem(lax.div(me, 2) + step % 2, 2) * 2 + lax.rem(me + step // 2, 2)
            x_high, x_low = halves_of(jnp.concatenate([block_of(step, layer) for layer in range(layers)], axis=1))
            lhs = jnp.concatenate([x_high, x_low], axis=0)
            both = lax.dot_general(lhs, high_ref[group], lanes_contract, preferred_element_type=f32)
            part = both[:columns] + both[columns:]
            part += lax.dot_general(x_high, low_ref[group], lanes_contract, preferred_element_type=f32)
            if step > begin:
                total_ref[...] += part
            elif start_ref is None:
                total_ref[...] = part
            else:
                total_ref[...] = start_ref[...] + part
        for first in range(0, columns, 2 * sources if out_refs else columns):
            real = pl.ds(first, sources)
            imag = pl.ds(first + sources, sources)
            if out_refs:
                put(out_refs, first, total_ref[real, :own_rows] - total_ref[imag, own_rows:])
                put(out_refs, first + sources, total_ref[imag, :own_rows] + total_ref[real, own_rows:])


def product_part(split, onward, layout, blocks, own, begin, end, started, sources, shares, relative):
    groups, both_rows, width = split[0].shape
    block = blocks[0].shape[-1]
    vmem = pl.BlockSpec(memory_space=pltpu.VMEM)
    finish = end == groups
    whole = (sum(shares), both_rows)
    arrays = list(blocks) + list(own) + list(split) + ([] if started is None else [started])
    if finish:
        out_shape = [jax.ShapeDtypeStruct((rows, both_rows // 2), f32) for rows in shares]
    else:
        out_shape = jax.ShapeDtypeStruct(whole, f32)
    return pl.pallas_call(
        functools.partial(product_kernel, sources, layout, len(blocks), 2 if own else 1, block, begin, end, onward, relative),
        in_specs=[vmem] * len(arrays),
        out_specs=[vmem] * len(shares) if finish else vmem,
        out_shape=out_shape,
        scratch_shapes=[pltpu.VMEM(whole, f32)] if finish else [],
        compiler_params=kernel_params(20),
        cost_estimate=pl.CostEstimate(flops=6 * sum(shares) * both_rows * width * (end - begin), bytes_accessed=MIB, transcendentals=0),
    )(*arrays)


def tied(value, to):
    return lax.optimization_barrier((value, to))[0]


def solve_paired(reduced, diag_inverse, coupling, sources):
    chain_size = lax.axis_size("chain")
    tile_size = lax.axis_size("tile")
    own_rows = reduced[0].shape[1]
    shares = [each.shape[0] for each in reduced]
    layers = tile_size // 4

    def send(value, hop, target):
        if not hop:
            return lax.ppermute(value, "tile", [(t, target(t)) for t in range(tile_size)])
        pairs = [(c * tile_size + t, (c + 1) % chain_size * tile_size + target(t)) for c in range(chain_size) for t in range(tile_size)]
        return lax.ppermute(value, ("chain", "tile"), pairs)

    def first_stage(first, second, hop):
        pair = [second if across == 0 and not hop else send(second, hop, lambda t: t ^ (2 * across)) for across in range(2)]
        line = [first if by == 0 and not hop else send(first, hop, lambda t: (t + 4 * by) % tile_size) for by in range(layers)]
        return jnp.stack(pair), jnp.stack(line)

    def second_stage(pair, line):
        far = send(line, False, lambda t: t ^ 2)
        rest = [pair if by == 0 else send(pair, False, lambda t: (t + 4 * by) % tile_size) for by in range(layers)]
        return [line, far, jnp.stack(rest)]

    layout = [lambda step, held: (step % 2, (held,)), lambda step, held: (2, (held, step % 2))]

    def products(split, onward, held, own, shares):
        other = [send(each, False, lambda t: t ^ 1) for each in held]
        mine, theirs = own if own else ([], [])
        started = product_part(split, onward, layout, held, mine, 0, 2, None, sources, shares, True)
        return product_part(split, onward, layout, other, theirs, 2, 4, started, sources, shares, True), other

    only = chain_size == 1
    pair, line = first_stage(*reduced, False)
    split = split_blocks(tied(diag_inverse if only else coupling, reduced[0]), own_rows, True)
    pair, line, split = lax.optimization_barrier((pair, line, split))
    held = second_stage(pair, line)
    if only:
        return products(split, False, held, None, [sum(shares)])[0][0]
    diag_split = split_blocks(tied(diag_inverse, line), own_rows, True)
    held[1], held[2], diag_split = lax.optimization_barrier((held[1], held[2], diag_split))
    carried, other = products(split, True, held, None, shares)
    own = (held, other)
    for step in range(chain_size - 1):
        held = second_stage(*lax.optimization_barrier(first_stage(*carried, True)))
        if step < chain_size - 2:
            carried = products(split, True, held, own, shares)[0]
    return products(diag_split, False, held, own, [sum(shares)])[0][0]


def solve_flat(reduced, diag_inverse, coupling, sources):
    chain_size = lax.axis_size("chain")
    reduced = reduced[0]
    columns = reduced.shape[0]
    full_rows = diag_inverse.shape[2]
    block = min(256, full_rows)
    count = full_rows // block
    layout = [lambda step, held: (0, (step * layers + held,))]
    onward = [(i, i + 1) for i in range(chain_size - 1)]
    diag_split = split_blocks(diag_inverse, block, False)
    coupling_split = split_blocks(coupling, block, False)
    groups = diag_split[0].shape[0]
    layers = count // groups

    def gathered(value):
        whole = lax.all_gather(value, "tile", axis=1, tiled=True)
        return [whole.reshape(columns, count, block).transpose(1, 0, 2)]

    current = reduced
    for _ in range(chain_size - 1):
        carried = product_part(coupling_split, True, layout, gathered(current), [], 0, groups, None, sources, [columns], False)[0]
        current = reduced - lax.ppermute(carried, "chain", onward)
    return product_part(diag_split, False, layout, gathered(current), [], 0, groups, None, sources, [columns], False)[0]


def body(right_side, diag_inverse, coupling, updates, update_rows, tile_counts):
    batches, halves, sources, own_rows = right_side.shape
    tile_size = lax.axis_size("tile")
    entries, columns = updates.shape
    tile_rows = entries // tile_counts.shape[0]
    cap = 2 * entries // tile_size
    slots = tile_size * cap
    vmem = pl.BlockSpec(memory_space=pltpu.VMEM)
    hbm = pl.BlockSpec(memory_space=pltpu.HBM)
    folded = cap % 16 == 0 and slots <= 1024 and columns == 192 and own_rows <= 256 and 128 % cap == 0
    width = 128 if folded else -(-(columns + 1) // 128) * 128
    height = cap + cap // 2 + 8 if folded else cap
    packed = pl.pallas_call(
        functools.partial(pack_kernel, own_rows, cap, tile_rows),
        in_specs=[hbm, hbm, hbm],
        out_specs=vmem,
        out_shape=jax.ShapeDtypeStruct((tile_size, height, width), f32),
        scratch_shapes=[
            pltpu.SMEM(tile_counts.shape, jnp.int32),
            pltpu.VMEM((1, entries), jnp.int32),
            pltpu.VMEM((columns, entries), f32),
            pltpu.SemaphoreType.DMA((3,)),
        ],
        compiler_params=kernel_params(56),
    )(tile_counts, update_rows[None, :], updates.T)
    received = lax.all_to_all(packed, "tile", 0, 0, tiled=False)
    paired = own_rows % 128 == 0 and tile_size % 8 == 0 and columns % 8 == 0 and columns >= 24
    early = columns * 17 // 24 // 8 * 8
    shares = [early, columns - early] if paired else [columns]
    reduced = pl.pallas_call(
        functools.partial(reduce_kernel, cap),
        in_specs=[vmem, hbm],
        out_specs=[vmem] * len(shares),
        out_shape=[jax.ShapeDtypeStruct((rows, own_rows), f32) for rows in shares],
        scratch_shapes=[pltpu.VMEM((columns, own_rows), f32), pltpu.SemaphoreType.DMA(())],
        compiler_params=kernel_params(20),
    )(received, right_side.reshape(columns, own_rows))
    solve = solve_paired if paired else solve_flat
    return solve(reduced, diag_inverse, coupling, sources).reshape(right_side.shape)


def solution(mesh):
    in_specs = (
        P(None, None, None, ("chain", "tile")),
        P(None, ("chain", "tile"), None),
        P(None, ("chain", "tile"), None),
        P(("chain", "tile"), None),
        P(("chain", "tile")),
        P(("chain", "tile")),
    )
    out_specs = P(None, None, None, ("chain", "tile"))
    return jax.shard_map(body, mesh=mesh, in_specs=in_specs, out_specs=out_specs, check_vma=False)
```

```python
import functools

import jax
import jax.numpy as jnp
from jax import lax
from jax.experimental import pallas as pl
from jax.experimental.pallas import tpu as pltpu
from jax.sharding import PartitionSpec as P

MIB = 1 << 20
f32 = jnp.float32
bf16 = jnp.bfloat16
lanes_contract = (((1,), (1,)), ((), ()))


def halves_of(value):
    high = value.astype(bf16)
    return high, (value - high.astype(f32)).astype(bf16)


def kernel_params(size):
    return pltpu.CompilerParams(vmem_limit_bytes=int(size * MIB))


def pack_kernel(own_rows, cap, tile_rows, counts_hbm, rows_hbm, updates_hbm, packed_ref, counts_ref, rows_ref, updates_ref, sems):
    moves = [
        pltpu.make_async_copy(counts_hbm, counts_ref, sems.at[0]),
        pltpu.make_async_copy(rows_hbm, rows_ref, sems.at[1]),
        pltpu.make_async_copy(updates_hbm, updates_ref, sems.at[2]),
    ]
    for move in moves:
        move.start()
    columns, entries = updates_ref.shape
    owners, height, width = packed_ref.shape
    slots = owners * cap
    entry = lax.broadcasted_iota(jnp.int32, (1, entries), 1)
    earlier = lax.broadcasted_iota(jnp.int32, (entries, entries), 0) < lax.broadcasted_iota(jnp.int32, (entries, entries), 1)
    for move in moves:
        move.wait()
    live = jnp.zeros((1, entries), jnp.bool_)
    for tile in range(entries // tile_rows):
        start = tile * tile_rows
        live = live | ((entry >= start) & (entry < start + counts_ref[tile]))
    rows = rows_ref[...]
    owner = rows // own_rows
    me = lax.axis_index("tile")
    local_row = (rows - owner * own_rows).astype(f32)
    if height > cap:
        owner = owner ^ lax.rem(me, 2)
    lane_owner = jnp.broadcast_to(owner.astype(f32), (entries, entries))
    rank = jnp.sum(jnp.where(earlier & (lane_owner.T == lane_owner), 1, 0), axis=0, keepdims=True)
    slot = owner * cap + rank
    choose = jnp.where(lax.broadcasted_iota(jnp.int32, (slots, entries), 0) == slot, 1.0, 0.0).astype(bf16)
    data = jnp.where(live, updates_ref[...], 0.0)
    folded = height > cap
    if not folded:
        tail = jnp.where(lax.broadcasted_iota(jnp.int32, (width - columns, entries), 0) == 0, local_row, 0.0)
        data = jnp.concatenate([data, tail], axis=0)
    packed = jnp.zeros((slots, data.shape[0]), f32)
    for piece in halves_of(data):
        packed += lax.dot_general(choose, piece, lanes_contract, preferred_element_type=f32)
    packed = packed.reshape(owners, cap, data.shape[0])
    if not folded:
        packed_ref[...] = packed
        return
    half = cap // 2
    packed_ref[:, :cap, :] = packed[:, :, :width]
    packed_ref[:, cap:cap + half, :] = jnp.concatenate([packed[:, :half, width:], packed[:, half:, width:]], axis=2)
    first = lax.div(me, 2) * cap
    by_owner = jnp.where(lax.broadcasted_iota(jnp.int32, (owners, entries), 0) == owner, local_row, 0.0).astype(bf16)
    by_lane = jnp.where(lax.broadcasted_iota(jnp.int32, (width, entries), 0) == lax.rem(first, width) + rank, 1.0, 0.0).astype(bf16)
    numbers = lax.dot_general(by_owner, by_lane, lanes_contract, preferred_element_type=f32)
    line = lax.broadcasted_iota(jnp.int32, (owners, 8, width), 1)
    other = lax.broadcasted_iota(jnp.int32, (owners, 8, width), 0) % 2
    target = lax.div(first, width) + other * (owners // 2 * cap // width)
    packed_ref[:, cap + half:, :] = jnp.where(line == target, numbers[:, None, :], 0.0)


def reduce_kernel(cap, inputs, right_hbm, *refs):
    received_refs, reduced_refs, right_ref, sem = refs[:inputs], refs[inputs:-2], refs[-2], refs[-1]
    move = pltpu.make_async_copy(right_hbm, right_ref, sem)
    move.start()
    owners, height, width = received_refs[-1].shape
    slots = owners * cap * inputs
    columns, own_rows = right_ref.shape
    if height > cap:
        half = cap // 2
        numbers = sum(jnp.sum(ref[:, cap + half:height, :], axis=0) for ref in received_refs)
        numbers = jnp.concatenate([numbers[i:i + 1] for i in range(slots // width)], axis=1).astype(jnp.int32)
        wide, rest = [], []
        for ref in received_refs:
            wide.append(ref[:, :cap, :].reshape(owners * cap, width))
            folds = ref[:, cap:cap + half, :]
            folds = jnp.concatenate([folds[:, :, :width // 2], folds[:, :, width // 2:]], axis=1)
            rest.append(folds.reshape(owners * cap, width // 2))
        sets = [jnp.concatenate(wide, axis=0), jnp.concatenate(rest, axis=0)]
        place = jnp.where(lax.broadcasted_iota(jnp.int32, (own_rows, slots), 0) == numbers, 1.0, 0.0).astype(bf16)
        totals = []
        for value in sets:
            total = jnp.zeros((own_rows, value.shape[1]), f32)
            for piece in halves_of(value):
                total += jnp.dot(place, piece, preferred_element_type=f32)
            totals.append(total.T)
        total = jnp.concatenate(totals, axis=0)
    else:
        received = received_refs[0][...].reshape(slots, width)
        local_row = received[:, columns:columns + 1].astype(jnp.int32)
        place = jnp.where(lax.broadcasted_iota(jnp.int32, (slots, own_rows), 1) == local_row, 1.0, 0.0).astype(bf16)
        total = jnp.zeros((columns, own_rows), f32)
        for piece in halves_of(received[:, :columns].T):
            total += jnp.dot(piece, place, preferred_element_type=f32)
    move.wait()
    start = 0
    for reduced_ref in reduced_refs:
        rows = reduced_ref.shape[0]
        reduced_ref[...] = right_ref[start:start + rows, :] - total[start:start + rows]
        start += rows


def split_kernel(block, relative, matrix_ref, high_ref, low_ref):
    parts, own_rows, full_rows = matrix_ref.shape
    groups, rows, width = high_ref.shape
    layers = width // block
    height = 64
    for part in range(parts):
        for first in range(0, own_rows, height):
            start = part * own_rows + first
            for group in range(groups):
                for layer in range(layers):
                    column = (layer * groups + group if relative else group * layers + layer) * block
                    high, low = halves_of(matrix_ref[part, first:first + height, column:column + block])
                    high_ref[group, start:start + height, layer * block:(layer + 1) * block] = high
                    low_ref[group, start:start + height, layer * block:(layer + 1) * block] = low


def split_blocks(matrix, block, relative):
    parts, own_rows, full_rows = matrix.shape
    groups = 4 if full_rows % (4 * block) == 0 else 1
    vmem = pl.BlockSpec(memory_space=pltpu.VMEM)
    shape = jax.ShapeDtypeStruct((groups, parts * own_rows, full_rows // groups), bf16)
    return pl.pallas_call(
        functools.partial(split_kernel, block, relative),
        in_specs=[vmem],
        out_specs=[vmem, vmem],
        out_shape=[shape, shape],
        compiler_params=kernel_params(20),
        cost_estimate=pl.CostEstimate(flops=3 * matrix.size, bytes_accessed=8 * matrix.size, transcendentals=0),
    )(matrix)


def product_kernel(sources, layout, inputs, sets, block, begin, end, onward, relative, *refs):
    high_ref, low_ref = refs[inputs * sets:inputs * sets + 2]
    rest = refs[inputs * sets + 2:]
    groups, both_rows, width = high_ref.shape
    layers = width // block
    own_rows = both_rows // 2
    start_ref, rest = (rest[0], rest[1:]) if begin > 0 else (None, rest)
    out_refs, total_ref = (rest[:-1], rest[-1]) if end == groups else ((), rest[0])
    columns = total_ref.shape[0]
    me = lax.axis_index("tile")

    def block_of(step, layer):
        held = lax.rem(lax.div(me, 4) + (layers - layer), layers) if relative else layer
        pieces = []
        for group in layout:
            which, place = group(step, held)
            value = refs[which][place]
            if sets == 2:
                own = refs[inputs + which][place]
                value = jnp.where(lax.axis_index("chain") == 0, own, own - value)
            pieces.append(value)
        return jnp.concatenate(pieces, axis=0)

    active = jnp.logical_not(onward) | (lax.axis_index("chain") < lax.axis_size("chain") - 1)

    @pl.when(jnp.logical_not(active))
    def _():
        for out_ref in out_refs:
            out_ref[...] = jnp.zeros_like(out_ref)

    @pl.when(active)
    def _():
        for step in range(begin, end):
            group = step
            if relative:
                group = lax.rem(lax.div(me, 2) + step % 2, 2) * 2 + lax.rem(me + step // 2, 2)
            x_high, x_low = halves_of(jnp.concatenate([block_of(step, layer) for layer in range(layers)], axis=1))
            lhs = jnp.concatenate([x_high, x_low], axis=0)
            both = lax.dot_general(lhs, high_ref[group], lanes_contract, preferred_element_type=f32)
            part = both[:columns] + both[columns:]
            part += lax.dot_general(x_high, low_ref[group], lanes_contract, preferred_element_type=f32)
            if step > begin:
                total_ref[...] += part
            elif start_ref is None:
                total_ref[...] = part
            else:
                total_ref[...] = start_ref[...] + part
        start = 0
        for out_ref in out_refs:
            for first in range(0, out_ref.shape[0], 2 * sources):
                real = pl.ds(start + first, sources)
                imag = pl.ds(start + first + sources, sources)
                out_ref[first:first + sources, :] = total_ref[real, :own_rows] - total_ref[imag, own_rows:]
                out_ref[first + sources:first + 2 * sources, :] = total_ref[imag, :own_rows] + total_ref[real, own_rows:]
            start += out_ref.shape[0]


def product_part(split, onward, layout, blocks, own, begin, end, started, sources, shares, relative):
    groups, both_rows, width = split[0].shape
    block = blocks[0].shape[-1]
    vmem = pl.BlockSpec(memory_space=pltpu.VMEM)
    finish = end == groups
    whole = (sum(shares), both_rows)
    arrays = list(blocks) + list(own) + list(split) + ([] if started is None else [started])
    if finish:
        out_shape = [jax.ShapeDtypeStruct((rows, both_rows // 2), f32) for rows in shares]
    else:
        out_shape = jax.ShapeDtypeStruct(whole, f32)
    return pl.pallas_call(
        functools.partial(product_kernel, sources, layout, len(blocks), 2 if own else 1, block, begin, end, onward, relative),
        in_specs=[vmem] * len(arrays),
        out_specs=[vmem] * len(shares) if finish else vmem,
        out_shape=out_shape,
        scratch_shapes=[pltpu.VMEM(whole, f32)] if finish else [],
        compiler_params=kernel_params(20),
        cost_estimate=pl.CostEstimate(flops=6 * sum(shares) * both_rows * width * (end - begin), bytes_accessed=MIB, transcendentals=0),
    )(*arrays)


def tied(value, to):
    return lax.optimization_barrier((value, to))[0]


def solve_paired(reduced, diag_inverse, coupling, sources):
    chain_size = lax.axis_size("chain")
    tile_size = lax.axis_size("tile")
    own_rows = reduced[0].shape[1]
    shares = [each.shape[0] for each in reduced]
    layers = tile_size // 4

    def send(value, hop, target):
        if not hop:
            return lax.ppermute(value, "tile", [(t, target(t)) for t in range(tile_size)])
        pairs = [(c * tile_size + t, (c + 1) % chain_size * tile_size + target(t)) for c in range(chain_size) for t in range(tile_size)]
        return lax.ppermute(value, ("chain", "tile"), pairs)

    def first_stage(first, second, hop):
        pair = [second if across == 0 and not hop else send(second, hop, lambda t: t ^ (2 * across)) for across in range(2)]
        line = [first if by == 0 and not hop else send(first, hop, lambda t: (t + 4 * by) % tile_size) for by in range(layers)]
        return jnp.stack(pair), jnp.stack(line)

    def second_stage(pair, line):
        far = send(line, False, lambda t: t ^ 2)
        rest = [pair if by == 0 else send(pair, False, lambda t: (t + 4 * by) % tile_size) for by in range(layers)]
        return [line, far, jnp.stack(rest)]

    layout = [lambda step, held: (step % 2, (held,)), lambda step, held: (2, (held, step % 2))]

    def products(split, onward, held, own, shares):
        other = [send(each, False, lambda t: t ^ 1) for each in held]
        mine, theirs = own if own else ([], [])
        started = product_part(split, onward, layout, held, mine, 0, 2, None, sources, shares, True)
        return product_part(split, onward, layout, other, theirs, 2, 4, started, sources, shares, True), other

    only = chain_size == 1
    pair, line = first_stage(*reduced, False)
    split = split_blocks(tied(diag_inverse if only else coupling, reduced[0]), own_rows, True)
    pair, line, split = lax.optimization_barrier((pair, line, split))
    held = second_stage(pair, line)
    if only:
        return products(split, False, held, None, [sum(shares)])[0][0]
    diag_split = split_blocks(tied(diag_inverse, line), own_rows, True)
    held[1], held[2], diag_split = lax.optimization_barrier((held[1], held[2], diag_split))
    carried, other = products(split, True, held, None, shares)
    own = (held, other)
    for step in range(chain_size - 1):
        held = second_stage(*lax.optimization_barrier(first_stage(*carried, True)))
        if step < chain_size - 2:
            carried = products(split, True, held, own, shares)[0]
    return products(diag_split, False, held, own, [sum(shares)])[0][0]


def solve_flat(reduced, diag_inverse, coupling, sources):
    chain_size = lax.axis_size("chain")
    reduced = reduced[0]
    columns = reduced.shape[0]
    full_rows = diag_inverse.shape[2]
    block = min(256, full_rows)
    count = full_rows // block
    layout = [lambda step, held: (0, (step * layers + held,))]
    onward = [(i, i + 1) for i in range(chain_size - 1)]
    diag_split = split_blocks(diag_inverse, block, False)
    coupling_split = split_blocks(coupling, block, False)
    groups = diag_split[0].shape[0]
    layers = count // groups

    def gathered(value):
        whole = lax.all_gather(value, "tile", axis=1, tiled=True)
        return [whole.reshape(columns, count, block).transpose(1, 0, 2)]

    current = reduced
    for _ in range(chain_size - 1):
        carried = product_part(coupling_split, True, layout, gathered(current), [], 0, groups, None, sources, [columns], False)[0]
        current = reduced - lax.ppermute(carried, "chain", onward)
    return product_part(diag_split, False, layout, gathered(current), [], 0, groups, None, sources, [columns], False)[0]


def body(right_side, diag_inverse, coupling, updates, update_rows, tile_counts):
    batches, halves, sources, own_rows = right_side.shape
    tile_size = lax.axis_size("tile")
    entries, columns = updates.shape
    tile_rows = entries // tile_counts.shape[0]
    cap = 2 * entries // tile_size
    slots = tile_size * cap
    vmem = pl.BlockSpec(memory_space=pltpu.VMEM)
    hbm = pl.BlockSpec(memory_space=pltpu.HBM)
    folded = cap % 16 == 0 and slots <= 1024 and columns == 192 and own_rows <= 256 and 128 % cap == 0
    folded = folded and tile_size % 2 == 0 and tile_size // 2 * cap % 128 == 0
    width = 128 if folded else -(-(columns + 1) // 128) * 128
    height = cap + cap // 2 + 8 if folded else cap
    packed = pl.pallas_call(
        functools.partial(pack_kernel, own_rows, cap, tile_rows),
        in_specs=[hbm, hbm, hbm],
        out_specs=vmem,
        out_shape=jax.ShapeDtypeStruct((tile_size, height, width), f32),
        scratch_shapes=[
            pltpu.SMEM(tile_counts.shape, jnp.int32),
            pltpu.VMEM((1, entries), jnp.int32),
            pltpu.VMEM((columns, entries), f32),
            pltpu.SemaphoreType.DMA((3,)),
        ],
        compiler_params=kernel_params(56),
    )(tile_counts, update_rows[None, :], updates.T)
    if folded:
        chips = tile_size // 2
        groups = [[2 * chip + core for chip in range(chips)] for core in range(2)]
        packed = packed.reshape(chips, 2 * height, width)
        arrived = lax.all_to_all(packed, "tile", 0, 0, tiled=False, axis_index_groups=groups)
        received = [arrived, lax.ppermute(arrived[:, height:, :], "tile", [(t, t ^ 1) for t in range(tile_size)])]
    else:
        received = [lax.all_to_all(packed, "tile", 0, 0, tiled=False)]
    paired = own_rows % 128 == 0 and tile_size % 8 == 0 and batches > 1
    early = batches * 2 // 3 * halves * sources
    shares = [early, columns - early] if paired else [columns]
    reduced = pl.pallas_call(
        functools.partial(reduce_kernel, cap, len(received)),
        in_specs=[hbm] + [vmem] * len(received),
        out_specs=[vmem] * len(shares),
        out_shape=[jax.ShapeDtypeStruct((rows, own_rows), f32) for rows in shares],
        scratch_shapes=[pltpu.VMEM((columns, own_rows), f32), pltpu.SemaphoreType.DMA(())],
        compiler_params=kernel_params(20),
    )(right_side.reshape(columns, own_rows), *received)
    solve = solve_paired if paired else solve_flat
    return solve(reduced, diag_inverse, coupling, sources).reshape(right_side.shape)


def solution(mesh):
    in_specs = (
        P(None, None, None, ("chain", "tile")),
        P(None, ("chain", "tile"), None),
        P(None, ("chain", "tile"), None),
        P(("chain", "tile"), None),
        P(("chain", "tile")),
        P(("chain", "tile")),
    )
    out_specs = P(None, None, None, ("chain", "tile"))
    return jax.shard_map(body, mesh=mesh, in_specs=in_specs, out_specs=out_specs, check_vma=False)
```

```python
import functools

import jax
import jax.numpy as jnp
from jax import lax
from jax.experimental import pallas as pl
from jax.experimental.pallas import tpu as pltpu
from jax.sharding import PartitionSpec as P

MIB = 1 << 20
f32 = jnp.float32
bf16 = jnp.bfloat16
lanes_contract = (((1,), (1,)), ((), ()))


def halves_of(value):
    high = value.astype(bf16)
    return high, (value - high.astype(f32)).astype(bf16)


def kernel_params(size):
    return pltpu.CompilerParams(vmem_limit_bytes=int(size * MIB))


def pack_kernel(own_rows, cap, tile_rows, counts_hbm, rows_hbm, updates_hbm, packed_ref, counts_ref, rows_ref, updates_ref, sems):
    moves = [
        pltpu.make_async_copy(counts_hbm, counts_ref, sems.at[0]),
        pltpu.make_async_copy(rows_hbm, rows_ref, sems.at[1]),
        pltpu.make_async_copy(updates_hbm, updates_ref, sems.at[2]),
    ]
    for move in moves:
        move.start()
    columns, entries = updates_ref.shape
    owners, height, width = packed_ref.shape
    slots = owners * cap
    entry = lax.broadcasted_iota(jnp.int32, (1, entries), 1)
    earlier = lax.broadcasted_iota(jnp.int32, (entries, entries), 0) < lax.broadcasted_iota(jnp.int32, (entries, entries), 1)
    for move in moves:
        move.wait()
    live = jnp.zeros((1, entries), jnp.bool_)
    for tile in range(entries // tile_rows):
        start = tile * tile_rows
        live = live | ((entry >= start) & (entry < start + counts_ref[tile]))
    rows = rows_ref[...]
    owner = rows // own_rows
    lane_owner = jnp.broadcast_to(owner.astype(f32), (entries, entries))
    rank = jnp.sum(jnp.where(earlier & (lane_owner.T == lane_owner), 1, 0), axis=0, keepdims=True)
    slot = owner * cap + rank
    choose = jnp.where(lax.broadcasted_iota(jnp.int32, (slots, entries), 0) == slot, 1.0, 0.0).astype(bf16)
    data = jnp.where(live, updates_ref[...], 0.0)
    local_row = (rows - owner * own_rows).astype(f32)
    folded = height > cap
    if not folded:
        tail = jnp.where(lax.broadcasted_iota(jnp.int32, (width - columns, entries), 0) == 0, local_row, 0.0)
        data = jnp.concatenate([data, tail], axis=0)
    packed = jnp.zeros((slots, data.shape[0]), f32)
    for piece in halves_of(data):
        packed += lax.dot_general(choose, piece, lanes_contract, preferred_element_type=f32)
    packed = packed.reshape(owners, cap, data.shape[0])
    if not folded:
        packed_ref[...] = packed
        return
    half = cap // 2
    packed_ref[:, :cap, :] = packed[:, :, :width]
    packed_ref[:, cap:cap + half, :] = jnp.concatenate([packed[:, :half, width:], packed[:, half:, width:]], axis=2)
    first = lax.axis_index("tile") * cap
    by_owner = jnp.where(lax.broadcasted_iota(jnp.int32, (owners, entries), 0) == owner, local_row, 0.0).astype(bf16)
    by_lane = jnp.where(lax.broadcasted_iota(jnp.int32, (width, entries), 0) == first % width + rank, 1.0, 0.0).astype(bf16)
    numbers = lax.dot_general(by_owner, by_lane, lanes_contract, preferred_element_type=f32)
    line = lax.broadcasted_iota(jnp.int32, (owners, 8, width), 1)
    packed_ref[:, cap + half:, :] = jnp.where(line == first // width, numbers[:, None, :], 0.0)


def reduce_kernel(cap, received_ref, right_hbm, *refs):
    reduced_refs, right_ref, sem = refs[:-2], refs[-2], refs[-1]
    move = pltpu.make_async_copy(right_hbm, right_ref, sem)
    move.start()
    owners, height, width = received_ref.shape
    slots = owners * cap
    columns, own_rows = right_ref.shape
    if height > cap:
        half = cap // 2
        numbers = jnp.sum(received_ref[:, cap + half:, :], axis=0)
        numbers = jnp.concatenate([numbers[i:i + 1] for i in range(slots // width)], axis=1).astype(jnp.int32)
        rest = received_ref[:, cap:cap + half, :]
        rest = jnp.concatenate([rest[:, :, :width // 2], rest[:, :, width // 2:]], axis=1)
        sets = [received_ref[:, :cap, :].reshape(slots, width), rest.reshape(slots, width // 2)]
        place = jnp.where(lax.broadcasted_iota(jnp.int32, (own_rows, slots), 0) == numbers, 1.0, 0.0).astype(bf16)
        totals = []
        for value in sets:
            total = jnp.zeros((own_rows, value.shape[1]), f32)
            for piece in halves_of(value):
                total += jnp.dot(place, piece, preferred_element_type=f32)
            totals.append(total.T)
        total = jnp.concatenate(totals, axis=0)
    else:
        received = received_ref[...].reshape(slots, width)
        local_row = received[:, columns:columns + 1].astype(jnp.int32)
        place = jnp.where(lax.broadcasted_iota(jnp.int32, (slots, own_rows), 1) == local_row, 1.0, 0.0).astype(bf16)
        total = jnp.zeros((columns, own_rows), f32)
        for piece in halves_of(received[:, :columns].T):
            total += jnp.dot(piece, place, preferred_element_type=f32)
    move.wait()
    start = 0
    for reduced_ref in reduced_refs:
        rows = reduced_ref.shape[0]
        reduced_ref[...] = right_ref[start:start + rows, :] - total[start:start + rows]
        start += rows


def split_kernel(block, relative, matrix_ref, high_ref, low_ref):
    parts, own_rows, full_rows = matrix_ref.shape
    groups, rows, width = high_ref.shape
    layers = width // block
    height = 64
    for part in range(parts):
        for first in range(0, own_rows, height):
            start = part * own_rows + first
            for group in range(groups):
                for layer in range(layers):
                    column = (layer * groups + group if relative else group * layers + layer) * block
                    high, low = halves_of(matrix_ref[part, first:first + height, column:column + block])
                    high_ref[group, start:start + height, layer * block:(layer + 1) * block] = high
                    low_ref[group, start:start + height, layer * block:(layer + 1) * block] = low


def split_blocks(matrix, block, relative):
    parts, own_rows, full_rows = matrix.shape
    groups = 4 if full_rows % (4 * block) == 0 else 1
    vmem = pl.BlockSpec(memory_space=pltpu.VMEM)
    shape = jax.ShapeDtypeStruct((groups, parts * own_rows, full_rows // groups), bf16)
    return pl.pallas_call(
        functools.partial(split_kernel, block, relative),
        in_specs=[vmem],
        out_specs=[vmem, vmem],
        out_shape=[shape, shape],
        compiler_params=kernel_params(20),
        cost_estimate=pl.CostEstimate(flops=3 * matrix.size, bytes_accessed=8 * matrix.size, transcendentals=0),
    )(matrix)


def product_kernel(sources, layout, inputs, sets, block, begin, end, onward, relative, *refs):
    high_ref, low_ref = refs[inputs * sets:inputs * sets + 2]
    rest = refs[inputs * sets + 2:]
    groups, both_rows, width = high_ref.shape
    layers = width // block
    own_rows = both_rows // 2
    start_ref, rest = (rest[0], rest[1:]) if begin > 0 else (None, rest)
    out_refs, total_ref = (rest[:-1], rest[-1]) if end == groups else ((), rest[0])
    columns = total_ref.shape[0]
    me = lax.axis_index("tile")

    def block_of(step, layer):
        held = lax.div(me, 4) ^ layer if relative else layer
        pieces = []
        for group in layout:
            which, place = group(step, held)
            value = refs[which][place]
            if sets == 2:
                own = refs[inputs + which][place]
                value = jnp.where(lax.axis_index("chain") == 0, own, own - value)
            pieces.append(value)
        return jnp.concatenate(pieces, axis=0)

    active = jnp.logical_not(onward) | (lax.axis_index("chain") < lax.axis_size("chain") - 1)

    @pl.when(jnp.logical_not(active))
    def _():
        for out_ref in out_refs:
            out_ref[...] = jnp.zeros_like(out_ref)

    @pl.when(active)
    def _():
        for step in range(begin, end):
            group = step
            if relative:
                group = lax.rem(lax.div(me, 2) + step % 2, 2) * 2 + lax.rem(me + step // 2, 2)
            x_high, x_low = halves_of(jnp.concatenate([block_of(step, layer) for layer in range(layers)], axis=1))
            lhs = jnp.concatenate([x_high, x_low], axis=0)
            both = lax.dot_general(lhs, high_ref[group], lanes_contract, preferred_element_type=f32)
            part = both[:columns] + both[columns:]
            part += lax.dot_general(x_high, low_ref[group], lanes_contract, preferred_element_type=f32)
            if step > begin:
                total_ref[...] += part
            elif start_ref is None:
                total_ref[...] = part
            else:
                total_ref[...] = start_ref[...] + part
        start = 0
        for out_ref in out_refs:
            for first in range(0, out_ref.shape[0], 2 * sources):
                real = pl.ds(start + first, sources)
                imag = pl.ds(start + first + sources, sources)
                out_ref[first:first + sources, :] = total_ref[real, :own_rows] - total_ref[imag, own_rows:]
                out_ref[first + sources:first + 2 * sources, :] = total_ref[imag, :own_rows] + total_ref[real, own_rows:]
            start += out_ref.shape[0]


def product_part(split, onward, layout, blocks, own, begin, end, started, sources, shares, relative):
    groups, both_rows, width = split[0].shape
    block = blocks[0].shape[-1]
    vmem = pl.BlockSpec(memory_space=pltpu.VMEM)
    finish = end == groups
    whole = (sum(shares), both_rows)
    arrays = list(blocks) + list(own) + list(split) + ([] if started is None else [started])
    if finish:
        out_shape = [jax.ShapeDtypeStruct((rows, both_rows // 2), f32) for rows in shares]
    else:
        out_shape = jax.ShapeDtypeStruct(whole, f32)
    return pl.pallas_call(
        functools.partial(product_kernel, sources, layout, len(blocks), 2 if own else 1, block, begin, end, onward, relative),
        in_specs=[vmem] * len(arrays),
        out_specs=[vmem] * len(shares) if finish else vmem,
        out_shape=out_shape,
        scratch_shapes=[pltpu.VMEM(whole, f32)] if finish else [],
        compiler_params=kernel_params(20),
        cost_estimate=pl.CostEstimate(flops=6 * sum(shares) * both_rows * width * (end - begin), bytes_accessed=MIB, transcendentals=0),
    )(*arrays)


def tied(value, to):
    return lax.optimization_barrier((value, to))[0]


def solve_paired(reduced, diag_inverse, coupling, sources):
    chain_size = lax.axis_size("chain")
    tile_size = lax.axis_size("tile")
    own_rows = reduced[0].shape[1]
    shares = [each.shape[0] for each in reduced]
    layers = tile_size // 4

    def send(value, hop, target):
        if not hop:
            return lax.ppermute(value, "tile", [(t, target(t)) for t in range(tile_size)])
        pairs = [(c * tile_size + t, (c + 1) % chain_size * tile_size + target(t)) for c in range(chain_size) for t in range(tile_size)]
        return lax.ppermute(value, ("chain", "tile"), pairs)

    def first_stage(first, second, hop):
        pair = [second if across == 0 and not hop else send(second, hop, lambda t: t ^ (2 * across)) for across in range(2)]
        line = [first if by == 0 and not hop else send(first, hop, lambda t: t ^ (4 * by)) for by in range(layers)]
        return jnp.stack(pair), jnp.stack(line)

    def second_stage(pair, line):
        far = send(line, False, lambda t: t ^ 2)
        rest = [pair if by == 0 else send(pair, False, lambda t: t ^ (4 * by)) for by in range(layers)]
        return [line, far, jnp.stack(rest)]

    layout = [lambda step, held: (step % 2, (held,)), lambda step, held: (2, (held, step % 2))]

    def products(split, onward, held, own, shares):
        other = [send(each, False, lambda t: t ^ 1) for each in held]
        mine, theirs = own if own else ([], [])
        started = product_part(split, onward, layout, held, mine, 0, 2, None, sources, shares, True)
        return product_part(split, onward, layout, other, theirs, 2, 4, started, sources, shares, True), other

    only = chain_size == 1
    pair, line = first_stage(*reduced, False)
    split = split_blocks(tied(diag_inverse if only else coupling, reduced[0]), own_rows, True)
    pair, line, split = lax.optimization_barrier((pair, line, split))
    held = second_stage(pair, line)
    if only:
        return products(split, False, held, None, [sum(shares)])[0][0]
    diag_split = split_blocks(tied(diag_inverse, line), own_rows, True)
    held[1], held[2], diag_split = lax.optimization_barrier((held[1], held[2], diag_split))
    carried, other = products(split, True, held, None, shares)
    own = (held, other)
    for step in range(chain_size - 1):
        held = second_stage(*lax.optimization_barrier(first_stage(*carried, True)))
        if step < chain_size - 2:
            carried = products(split, True, held, own, shares)[0]
    return products(diag_split, False, held, own, [sum(shares)])[0][0]


def solve_flat(reduced, diag_inverse, coupling, sources):
    chain_size = lax.axis_size("chain")
    reduced = reduced[0]
    columns = reduced.shape[0]
    full_rows = diag_inverse.shape[2]
    block = min(256, full_rows)
    count = full_rows // block
    layout = [lambda step, held: (0, (step * layers + held,))]
    onward = [(i, i + 1) for i in range(chain_size - 1)]
    diag_split = split_blocks(diag_inverse, block, False)
    coupling_split = split_blocks(coupling, block, False)
    groups = diag_split[0].shape[0]
    layers = count // groups

    def gathered(value):
        whole = lax.all_gather(value, "tile", axis=1, tiled=True)
        return [whole.reshape(columns, count, block).transpose(1, 0, 2)]

    current = reduced
    for _ in range(chain_size - 1):
        carried = product_part(coupling_split, True, layout, gathered(current), [], 0, groups, None, sources, [columns], False)[0]
        current = reduced - lax.ppermute(carried, "chain", onward)
    return product_part(diag_split, False, layout, gathered(current), [], 0, groups, None, sources, [columns], False)[0]


def body(right_side, diag_inverse, coupling, updates, update_rows, tile_counts):
    batches, halves, sources, own_rows = right_side.shape
    tile_size = lax.axis_size("tile")
    entries, columns = updates.shape
    tile_rows = entries // tile_counts.shape[0]
    cap = 2 * entries // tile_size
    slots = tile_size * cap
    vmem = pl.BlockSpec(memory_space=pltpu.VMEM)
    hbm = pl.BlockSpec(memory_space=pltpu.HBM)
    folded = cap % 16 == 0 and slots <= 1024 and columns == 192 and own_rows <= 256 and 128 % cap == 0
    width = 128 if folded else -(-(columns + 1) // 128) * 128
    height = cap + cap // 2 + 8 if folded else cap
    packed = pl.pallas_call(
        functools.partial(pack_kernel, own_rows, cap, tile_rows),
        in_specs=[hbm, hbm, hbm],
        out_specs=vmem,
        out_shape=jax.ShapeDtypeStruct((tile_size, height, width), f32),
        scratch_shapes=[
            pltpu.SMEM(tile_counts.shape, jnp.int32),
            pltpu.VMEM((1, entries), jnp.int32),
            pltpu.VMEM((columns, entries), f32),
            pltpu.SemaphoreType.DMA((3,)),
        ],
        compiler_params=kernel_params(56),
    )(tile_counts, update_rows[None, :], updates.T)
    received = lax.all_to_all(packed, "tile", 0, 0, tiled=False)
    paired = own_rows % 128 == 0 and tile_size >= 8 and tile_size & (tile_size - 1) == 0 and batches > 1
    early = batches * 2 // 3 * halves * sources
    shares = [early, columns - early] if paired else [columns]
    reduced = pl.pallas_call(
        functools.partial(reduce_kernel, cap),
        in_specs=[vmem, hbm],
        out_specs=[vmem] * len(shares),
        out_shape=[jax.ShapeDtypeStruct((rows, own_rows), f32) for rows in shares],
        scratch_shapes=[pltpu.VMEM((columns, own_rows), f32), pltpu.SemaphoreType.DMA(())],
        compiler_params=kernel_params(20),
    )(received, right_side.reshape(columns, own_rows))
    solve = solve_paired if paired else solve_flat
    return solve(reduced, diag_inverse, coupling, sources).reshape(right_side.shape)


def solution(mesh):
    in_specs = (
        P(None, None, None, ("chain", "tile")),
        P(None, ("chain", "tile"), None),
        P(None, ("chain", "tile"), None),
        P(("chain", "tile"), None),
        P(("chain", "tile")),
        P(("chain", "tile")),
    )
    out_specs = P(None, None, None, ("chain", "tile"))
    return jax.shard_map(body, mesh=mesh, in_specs=in_specs, out_specs=out_specs, check_vma=False)
```

```python
import functools

import jax
import jax.numpy as jnp
from jax import lax
from jax.experimental import pallas as pl
from jax.experimental.pallas import tpu as pltpu
from jax.sharding import PartitionSpec as P

MIB = 1 << 20
f32 = jnp.float32
bf16 = jnp.bfloat16
lanes_contract = (((1,), (1,)), ((), ()))


def halves_of(value):
    high = value.astype(bf16)
    return high, (value - high.astype(f32)).astype(bf16)


def kernel_params(size):
    return pltpu.CompilerParams(vmem_limit_bytes=int(size * MIB))


def pack_kernel(own_rows, cap, tile_rows, counts_hbm, rows_hbm, updates_hbm, packed_ref, counts_ref, rows_ref, updates_ref, sems):
    moves = [
        pltpu.make_async_copy(counts_hbm, counts_ref, sems.at[0]),
        pltpu.make_async_copy(rows_hbm, rows_ref, sems.at[1]),
        pltpu.make_async_copy(updates_hbm, updates_ref, sems.at[2]),
    ]
    for move in moves:
        move.start()
    columns, entries = updates_ref.shape
    owners, height, width = packed_ref.shape
    slots = owners * cap
    entry = lax.broadcasted_iota(jnp.int32, (1, entries), 1)
    earlier = lax.broadcasted_iota(jnp.int32, (entries, entries), 0) < lax.broadcasted_iota(jnp.int32, (entries, entries), 1)
    for move in moves:
        move.wait()
    live = jnp.zeros((1, entries), jnp.bool_)
    for tile in range(entries // tile_rows):
        start = tile * tile_rows
        live = live | ((entry >= start) & (entry < start + counts_ref[tile]))
    rows = rows_ref[...]
    owner = rows // own_rows
    lane_owner = jnp.broadcast_to(owner.astype(f32), (entries, entries))
    rank = jnp.sum(jnp.where(earlier & (lane_owner.T == lane_owner), 1, 0), axis=0, keepdims=True)
    slot = owner * cap + rank
    choose = jnp.where(lax.broadcasted_iota(jnp.int32, (slots, entries), 0) == slot, 1.0, 0.0).astype(bf16)
    data = jnp.where(live, updates_ref[...], 0.0)
    local_row = (rows - owner * own_rows).astype(f32)
    folded = height > cap
    if not folded:
        tail = jnp.where(lax.broadcasted_iota(jnp.int32, (width - columns, entries), 0) == 0, local_row, 0.0)
        data = jnp.concatenate([data, tail], axis=0)
    packed = jnp.zeros((slots, data.shape[0]), f32)
    for piece in halves_of(data):
        packed += lax.dot_general(choose, piece, lanes_contract, preferred_element_type=f32)
    packed = packed.reshape(owners, cap, data.shape[0])
    if not folded:
        packed_ref[...] = packed
        return
    half = cap // 2
    packed_ref[:, :cap, :] = packed[:, :, :width]
    packed_ref[:, cap:cap + half, :] = jnp.concatenate([packed[:, :half, width:], packed[:, half:, width:]], axis=2)
    first = lax.axis_index("tile") * cap
    by_owner = jnp.where(lax.broadcasted_iota(jnp.int32, (owners, entries), 0) == owner, local_row, 0.0).astype(bf16)
    by_lane = jnp.where(lax.broadcasted_iota(jnp.int32, (width, entries), 0) == first % width + rank, 1.0, 0.0).astype(bf16)
    numbers = lax.dot_general(by_owner, by_lane, lanes_contract, preferred_element_type=f32)
    line = lax.broadcasted_iota(jnp.int32, (owners, 8, width), 1)
    packed_ref[:, cap + half:, :] = jnp.where(line == first // width, numbers[:, None, :], 0.0)


def reduce_kernel(cap, received_ref, right_hbm, *refs):
    reduced_refs, right_ref, sem = refs[:-2], refs[-2], refs[-1]
    move = pltpu.make_async_copy(right_hbm, right_ref, sem)
    move.start()
    owners, height, width = received_ref.shape
    slots = owners * cap
    columns, own_rows = right_ref.shape
    if height > cap:
        half = cap // 2
        numbers = jnp.sum(received_ref[:, cap + half:, :], axis=0)
        numbers = jnp.concatenate([numbers[i:i + 1] for i in range(slots // width)], axis=1).astype(jnp.int32)
        rest = received_ref[:, cap:cap + half, :]
        rest = jnp.concatenate([rest[:, :, :width // 2], rest[:, :, width // 2:]], axis=1)
        sets = [received_ref[:, :cap, :].reshape(slots, width), rest.reshape(slots, width // 2)]
        place = jnp.where(lax.broadcasted_iota(jnp.int32, (own_rows, slots), 0) == numbers, 1.0, 0.0).astype(bf16)
        totals = []
        for value in sets:
            total = jnp.zeros((own_rows, value.shape[1]), f32)
            for piece in halves_of(value):
                total += jnp.dot(place, piece, preferred_element_type=f32)
            totals.append(total.T)
        total = jnp.concatenate(totals, axis=0)
    else:
        received = received_ref[...].reshape(slots, width)
        local_row = received[:, columns:columns + 1].astype(jnp.int32)
        place = jnp.where(lax.broadcasted_iota(jnp.int32, (slots, own_rows), 1) == local_row, 1.0, 0.0).astype(bf16)
        total = jnp.zeros((columns, own_rows), f32)
        for piece in halves_of(received[:, :columns].T):
            total += jnp.dot(piece, place, preferred_element_type=f32)
    move.wait()
    start = 0
    for reduced_ref in reduced_refs:
        rows = reduced_ref.shape[0]
        reduced_ref[...] = right_ref[start:start + rows, :] - total[start:start + rows]
        start += rows


def split_kernel(block, relative, matrix_ref, high_ref, low_ref):
    parts, own_rows, full_rows = matrix_ref.shape
    groups, rows, width = high_ref.shape
    layers = width // block
    height = 64
    for part in range(parts):
        for first in range(0, own_rows, height):
            start = part * own_rows + first
            for group in range(groups):
                for layer in range(layers):
                    column = (layer * groups + group if relative else group * layers + layer) * block
                    high, low = halves_of(matrix_ref[part, first:first + height, column:column + block])
                    high_ref[group, start:start + height, layer * block:(layer + 1) * block] = high
                    low_ref[group, start:start + height, layer * block:(layer + 1) * block] = low


def split_blocks(matrix, block, relative):
    parts, own_rows, full_rows = matrix.shape
    groups = 4 if full_rows % (4 * block) == 0 else 1
    vmem = pl.BlockSpec(memory_space=pltpu.VMEM)
    shape = jax.ShapeDtypeStruct((groups, parts * own_rows, full_rows // groups), bf16)
    return pl.pallas_call(
        functools.partial(split_kernel, block, relative),
        in_specs=[vmem],
        out_specs=[vmem, vmem],
        out_shape=[shape, shape],
        compiler_params=kernel_params(20),
        cost_estimate=pl.CostEstimate(flops=3 * matrix.size, bytes_accessed=8 * matrix.size, transcendentals=0),
    )(matrix)


def product_kernel(sources, layout, inputs, sets, block, begin, end, onward, relative, *refs):
    high_ref, low_ref = refs[inputs * sets:inputs * sets + 2]
    rest = refs[inputs * sets + 2:]
    groups, both_rows, width = high_ref.shape
    layers = width // block
    own_rows = both_rows // 2
    start_ref, rest = (rest[0], rest[1:]) if begin > 0 else (None, rest)
    out_refs, total_ref = (rest[:-1], rest[-1]) if end == groups else ((), rest[0])
    columns = total_ref.shape[0]
    me = lax.axis_index("tile")

    def block_of(step, layer):
        held = lax.div(me, 4) ^ layer if relative else layer
        hopped = lax.rem(lax.div(me, 4) + (layers - layer), layers)
        pieces = []
        for group in layout:
            which, place = group(step, held, held if sets == 1 else hopped)
            value = refs[which][place]
            if sets == 2:
                which, place = group(step, held, held)
                own = refs[inputs + which][place]
                value = jnp.where(lax.axis_index("chain") == 0, own, own - value)
            pieces.append(value)
        return jnp.concatenate(pieces, axis=0)

    active = jnp.logical_not(onward) | (lax.axis_index("chain") < lax.axis_size("chain") - 1)

    @pl.when(jnp.logical_not(active))
    def _():
        for out_ref in out_refs:
            out_ref[...] = jnp.zeros_like(out_ref)

    @pl.when(active)
    def _():
        for step in range(begin, end):
            group = step
            if relative:
                group = lax.rem(lax.div(me, 2) + step % 2, 2) * 2 + lax.rem(me + step // 2, 2)
            x_high, x_low = halves_of(jnp.concatenate([block_of(step, layer) for layer in range(layers)], axis=1))
            lhs = jnp.concatenate([x_high, x_low], axis=0)
            both = lax.dot_general(lhs, high_ref[group], lanes_contract, preferred_element_type=f32)
            part = both[:columns] + both[columns:]
            part += lax.dot_general(x_high, low_ref[group], lanes_contract, preferred_element_type=f32)
            if step > begin:
                total_ref[...] += part
            elif start_ref is None:
                total_ref[...] = part
            else:
                total_ref[...] = start_ref[...] + part
        start = 0
        for out_ref in out_refs:
            for first in range(0, out_ref.shape[0], 2 * sources):
                real = pl.ds(start + first, sources)
                imag = pl.ds(start + first + sources, sources)
                out_ref[first:first + sources, :] = total_ref[real, :own_rows] - total_ref[imag, own_rows:]
                out_ref[first + sources:first + 2 * sources, :] = total_ref[imag, :own_rows] + total_ref[real, own_rows:]
            start += out_ref.shape[0]


def product_part(split, onward, layout, blocks, own, begin, end, started, sources, shares, relative):
    groups, both_rows, width = split[0].shape
    block = blocks[0].shape[-1]
    vmem = pl.BlockSpec(memory_space=pltpu.VMEM)
    finish = end == groups
    whole = (sum(shares), both_rows)
    arrays = list(blocks) + list(own) + list(split) + ([] if started is None else [started])
    if finish:
        out_shape = [jax.ShapeDtypeStruct((rows, both_rows // 2), f32) for rows in shares]
    else:
        out_shape = jax.ShapeDtypeStruct(whole, f32)
    return pl.pallas_call(
        functools.partial(product_kernel, sources, layout, len(blocks), 2 if own else 1, block, begin, end, onward, relative),
        in_specs=[vmem] * len(arrays),
        out_specs=[vmem] * len(shares) if finish else vmem,
        out_shape=out_shape,
        scratch_shapes=[pltpu.VMEM(whole, f32)] if finish else [],
        compiler_params=kernel_params(20),
        cost_estimate=pl.CostEstimate(flops=6 * sum(shares) * both_rows * width * (end - begin), bytes_accessed=MIB, transcendentals=0),
    )(*arrays)


def tied(value, to):
    return lax.optimization_barrier((value, to))[0]


def solve_paired(reduced, diag_inverse, coupling, sources):
    chain_size = lax.axis_size("chain")
    tile_size = lax.axis_size("tile")
    own_rows = reduced[0].shape[1]
    shares = [each.shape[0] for each in reduced]
    layers = tile_size // 4

    def send(value, hop, target):
        if not hop:
            return lax.ppermute(value, "tile", [(t, target(t)) for t in range(tile_size)])
        pairs = [(c * tile_size + t, (c + 1) % chain_size * tile_size + target(t)) for c in range(chain_size) for t in range(tile_size)]
        return lax.ppermute(value, ("chain", "tile"), pairs)

    def first_stage(first, second, hop):
        pair = [second if across == 0 and not hop else send(second, hop, lambda t: t ^ (2 * across)) for across in range(2)]
        if hop:
            line = [send(first, True, lambda t: (t + 4 * by) % tile_size) for by in range(layers)]
        else:
            line = [first if by == 0 else send(first, False, lambda t: t ^ (4 * by)) for by in range(layers)]
        return jnp.stack(pair), jnp.stack(line)

    def second_stage(pair, line):
        far = send(line, False, lambda t: t ^ 2)
        rest = [pair if by == 0 else send(pair, False, lambda t: t ^ (4 * by)) for by in range(layers)]
        return [line, far, jnp.stack(rest)]

    layout = [lambda step, held, line: (step % 2, (line,)), lambda step, held, line: (2, (held, step % 2))]

    def products(split, onward, held, own, shares):
        other = [send(each, False, lambda t: t ^ 1) for each in held]
        mine, theirs = own if own else ([], [])
        started = product_part(split, onward, layout, held, mine, 0, 2, None, sources, shares, True)
        return product_part(split, onward, layout, other, theirs, 2, 4, started, sources, shares, True), other

    only = chain_size == 1
    pair, line = first_stage(*reduced, False)
    split = split_blocks(tied(diag_inverse if only else coupling, reduced[0]), own_rows, True)
    pair, line, split = lax.optimization_barrier((pair, line, split))
    held = second_stage(pair, line)
    if only:
        return products(split, False, held, None, [sum(shares)])[0][0]
    diag_split = split_blocks(tied(diag_inverse, line), own_rows, True)
    held[1], held[2], diag_split = lax.optimization_barrier((held[1], held[2], diag_split))
    carried, other = products(split, True, held, None, shares)
    own = (held, other)
    for step in range(chain_size - 1):
        held = second_stage(*lax.optimization_barrier(first_stage(*carried, True)))
        if step < chain_size - 2:
            carried = products(split, True, held, own, shares)[0]
    return products(diag_split, False, held, own, [sum(shares)])[0][0]


def solve_flat(reduced, diag_inverse, coupling, sources):
    chain_size = lax.axis_size("chain")
    reduced = reduced[0]
    columns = reduced.shape[0]
    full_rows = diag_inverse.shape[2]
    block = min(256, full_rows)
    count = full_rows // block
    layout = [lambda step, held, line: (0, (step * layers + held,))]
    onward = [(i, i + 1) for i in range(chain_size - 1)]
    diag_split = split_blocks(diag_inverse, block, False)
    coupling_split = split_blocks(coupling, block, False)
    groups = diag_split[0].shape[0]
    layers = count // groups

    def gathered(value):
        whole = lax.all_gather(value, "tile", axis=1, tiled=True)
        return [whole.reshape(columns, count, block).transpose(1, 0, 2)]

    current = reduced
    for _ in range(chain_size - 1):
        carried = product_part(coupling_split, True, layout, gathered(current), [], 0, groups, None, sources, [columns], False)[0]
        current = reduced - lax.ppermute(carried, "chain", onward)
    return product_part(diag_split, False, layout, gathered(current), [], 0, groups, None, sources, [columns], False)[0]


def body(right_side, diag_inverse, coupling, updates, update_rows, tile_counts):
    batches, halves, sources, own_rows = right_side.shape
    tile_size = lax.axis_size("tile")
    entries, columns = updates.shape
    tile_rows = entries // tile_counts.shape[0]
    cap = 2 * entries // tile_size
    slots = tile_size * cap
    vmem = pl.BlockSpec(memory_space=pltpu.VMEM)
    hbm = pl.BlockSpec(memory_space=pltpu.HBM)
    folded = cap % 16 == 0 and slots <= 1024 and columns == 192 and own_rows <= 256 and 128 % cap == 0
    width = 128 if folded else -(-(columns + 1) // 128) * 128
    height = cap + cap // 2 + 8 if folded else cap
    packed = pl.pallas_call(
        functools.partial(pack_kernel, own_rows, cap, tile_rows),
        in_specs=[hbm, hbm, hbm],
        out_specs=vmem,
        out_shape=jax.ShapeDtypeStruct((tile_size, height, width), f32),
        scratch_shapes=[
            pltpu.SMEM(tile_counts.shape, jnp.int32),
            pltpu.VMEM((1, entries), jnp.int32),
            pltpu.VMEM((columns, entries), f32),
            pltpu.SemaphoreType.DMA((3,)),
        ],
        compiler_params=kernel_params(56),
    )(tile_counts, update_rows[None, :], updates.T)
    received = lax.all_to_all(packed, "tile", 0, 0, tiled=False)
    paired = own_rows % 128 == 0 and tile_size >= 8 and tile_size & (tile_size - 1) == 0 and batches > 1
    early = batches * 2 // 3 * halves * sources
    shares = [early, columns - early] if paired else [columns]
    reduced = pl.pallas_call(
        functools.partial(reduce_kernel, cap),
        in_specs=[vmem, hbm],
        out_specs=[vmem] * len(shares),
        out_shape=[jax.ShapeDtypeStruct((rows, own_rows), f32) for rows in shares],
        scratch_shapes=[pltpu.VMEM((columns, own_rows), f32), pltpu.SemaphoreType.DMA(())],
        compiler_params=kernel_params(20),
    )(received, right_side.reshape(columns, own_rows))
    solve = solve_paired if paired else solve_flat
    return solve(reduced, diag_inverse, coupling, sources).reshape(right_side.shape)


def solution(mesh):
    in_specs = (
        P(None, None, None, ("chain", "tile")),
        P(None, ("chain", "tile"), None),
        P(None, ("chain", "tile"), None),
        P(("chain", "tile"), None),
        P(("chain", "tile")),
        P(("chain", "tile")),
    )
    out_specs = P(None, None, None, ("chain", "tile"))
    return jax.shard_map(body, mesh=mesh, in_specs=in_specs, out_specs=out_specs, check_vma=False)
```

```python
import functools

import jax
import jax.numpy as jnp
from jax import lax
from jax.experimental import pallas as pl
from jax.experimental.pallas import tpu as pltpu
from jax.sharding import PartitionSpec as P

MIB = 1 << 20
f32 = jnp.float32
bf16 = jnp.bfloat16
lanes_contract = (((1,), (1,)), ((), ()))


def halves_of(value):
    high = value.astype(bf16)
    return high, (value - high.astype(f32)).astype(bf16)


def kernel_params(size):
    return pltpu.CompilerParams(vmem_limit_bytes=int(size * MIB))


def pack_kernel(own_rows, cap, tile_rows, counts_hbm, rows_hbm, updates_hbm, packed_ref, counts_ref, rows_ref, updates_ref, sems):
    moves = [
        pltpu.make_async_copy(counts_hbm, counts_ref, sems.at[0]),
        pltpu.make_async_copy(rows_hbm, rows_ref, sems.at[1]),
        pltpu.make_async_copy(updates_hbm, updates_ref, sems.at[2]),
    ]
    for move in moves:
        move.start()
    columns, entries = updates_ref.shape
    owners, height, width = packed_ref.shape
    slots = owners * cap
    entry = lax.broadcasted_iota(jnp.int32, (1, entries), 1)
    earlier = lax.broadcasted_iota(jnp.int32, (entries, entries), 0) < lax.broadcasted_iota(jnp.int32, (entries, entries), 1)
    for move in moves:
        move.wait()
    live = jnp.zeros((1, entries), jnp.bool_)
    for tile in range(entries // tile_rows):
        start = tile * tile_rows
        live = live | ((entry >= start) & (entry < start + counts_ref[tile]))
    rows = rows_ref[...]
    owner = rows // own_rows
    lane_owner = jnp.broadcast_to(owner.astype(f32), (entries, entries))
    rank = jnp.sum(jnp.where(earlier & (lane_owner.T == lane_owner), 1, 0), axis=0, keepdims=True)
    slot = owner * cap + rank
    choose = jnp.where(lax.broadcasted_iota(jnp.int32, (slots, entries), 0) == slot, 1.0, 0.0).astype(bf16)
    data = jnp.where(live, updates_ref[...], 0.0)
    local_row = (rows - owner * own_rows).astype(f32)
    folded = height > cap
    if not folded:
        tail = jnp.where(lax.broadcasted_iota(jnp.int32, (width - columns, entries), 0) == 0, local_row, 0.0)
        data = jnp.concatenate([data, tail], axis=0)
    packed = jnp.zeros((slots, data.shape[0]), f32)
    for piece in halves_of(data):
        packed += lax.dot_general(choose, piece, lanes_contract, preferred_element_type=f32)
    packed = packed.reshape(owners, cap, data.shape[0])
    if not folded:
        packed_ref[...] = packed
        return
    half = cap // 2
    packed_ref[:, :cap, :] = packed[:, :, :width]
    packed_ref[:, cap:cap + half, :] = jnp.concatenate([packed[:, :half, width:], packed[:, half:, width:]], axis=2)
    first = lax.axis_index("tile") * cap
    by_owner = jnp.where(lax.broadcasted_iota(jnp.int32, (owners, entries), 0) == owner, local_row, 0.0).astype(bf16)
    by_lane = jnp.where(lax.broadcasted_iota(jnp.int32, (width, entries), 0) == first % width + rank, 1.0, 0.0).astype(bf16)
    numbers = lax.dot_general(by_owner, by_lane, lanes_contract, preferred_element_type=f32)
    line = lax.broadcasted_iota(jnp.int32, (owners, 8, width), 1)
    packed_ref[:, cap + half:, :] = jnp.where(line == first // width, numbers[:, None, :], 0.0)


def reduce_kernel(cap, received_ref, right_hbm, *refs):
    reduced_refs, right_ref, sem = refs[:-2], refs[-2], refs[-1]
    move = pltpu.make_async_copy(right_hbm, right_ref, sem)
    move.start()
    owners, height, width = received_ref.shape
    slots = owners * cap
    columns, own_rows = right_ref.shape
    if height > cap:
        half = cap // 2
        numbers = jnp.sum(received_ref[:, cap + half:, :], axis=0)
        numbers = jnp.concatenate([numbers[i:i + 1] for i in range(slots // width)], axis=1).astype(jnp.int32)
        rest = received_ref[:, cap:cap + half, :]
        rest = jnp.concatenate([rest[:, :, :width // 2], rest[:, :, width // 2:]], axis=1)
        sets = [received_ref[:, :cap, :].reshape(slots, width), rest.reshape(slots, width // 2)]
        place = jnp.where(lax.broadcasted_iota(jnp.int32, (own_rows, slots), 0) == numbers, 1.0, 0.0).astype(bf16)
        totals = []
        for value in sets:
            total = jnp.zeros((own_rows, value.shape[1]), f32)
            for piece in halves_of(value):
                total += jnp.dot(place, piece, preferred_element_type=f32)
            totals.append(total.T)
        total = jnp.concatenate(totals, axis=0)
    else:
        received = received_ref[...].reshape(slots, width)
        local_row = received[:, columns:columns + 1].astype(jnp.int32)
        place = jnp.where(lax.broadcasted_iota(jnp.int32, (slots, own_rows), 1) == local_row, 1.0, 0.0).astype(bf16)
        total = jnp.zeros((columns, own_rows), f32)
        for piece in halves_of(received[:, :columns].T):
            total += jnp.dot(piece, place, preferred_element_type=f32)
    move.wait()
    start = 0
    for reduced_ref in reduced_refs:
        rows = reduced_ref.shape[0]
        reduced_ref[...] = right_ref[start:start + rows, :] - total[start:start + rows]
        start += rows


def split_kernel(block, relative, matrix_ref, high_ref, low_ref):
    parts, own_rows, full_rows = matrix_ref.shape
    groups, rows, width = high_ref.shape
    layers = width // block
    height = 64
    for part in range(parts):
        for first in range(0, own_rows, height):
            start = part * own_rows + first
            for group in range(groups):
                for layer in range(layers):
                    column = (layer * groups + group if relative else group * layers + layer) * block
                    high, low = halves_of(matrix_ref[part, first:first + height, column:column + block])
                    high_ref[group, start:start + height, layer * block:(layer + 1) * block] = high
                    low_ref[group, start:start + height, layer * block:(layer + 1) * block] = low


def split_blocks(matrix, block, relative):
    parts, own_rows, full_rows = matrix.shape
    groups = 4 if full_rows % (4 * block) == 0 else 1
    vmem = pl.BlockSpec(memory_space=pltpu.VMEM)
    shape = jax.ShapeDtypeStruct((groups, parts * own_rows, full_rows // groups), bf16)
    return pl.pallas_call(
        functools.partial(split_kernel, block, relative),
        in_specs=[vmem],
        out_specs=[vmem, vmem],
        out_shape=[shape, shape],
        compiler_params=kernel_params(20),
        cost_estimate=pl.CostEstimate(flops=3 * matrix.size, bytes_accessed=8 * matrix.size, transcendentals=0),
    )(matrix)


def product_kernel(sources, layout, inputs, sets, block, begin, end, onward, relative, *refs):
    high_ref, low_ref = refs[inputs * sets:inputs * sets + 2]
    rest = refs[inputs * sets + 2:]
    groups, both_rows, width = high_ref.shape
    layers = width // block
    own_rows = both_rows // 2
    start_ref, rest = (rest[0], rest[1:]) if begin > 0 else (None, rest)
    out_refs, total_ref = (rest[:-1], rest[-1]) if end == groups else ((), rest[0])
    columns = total_ref.shape[0]
    me = lax.axis_index("tile")

    def block_of(step, layer):
        held = lax.div(me, 4) ^ layer if relative else layer
        hopped = lax.rem(lax.div(me, 4) + (layers - layer), layers)
        pieces = []
        for group in layout:
            which, place = group(step, held, held if sets == 1 else hopped)
            value = refs[which][place]
            if sets == 2:
                which, place = group(step, held, held)
                own = refs[inputs + which][place]
                value = jnp.where(lax.axis_index("chain") == 0, own, own - value)
            pieces.append(value)
        return jnp.concatenate(pieces, axis=0)

    active = jnp.logical_not(onward) | (lax.axis_index("chain") < lax.axis_size("chain") - 1)

    @pl.when(jnp.logical_not(active))
    def _():
        for out_ref in out_refs:
            out_ref[...] = jnp.zeros_like(out_ref)

    @pl.when(active)
    def _():
        for step in range(begin, end):
            group = step
            if relative:
                group = lax.rem(lax.div(me, 2) + step % 2, 2) * 2 + lax.rem(me + step // 2, 2)
            x_high, x_low = halves_of(jnp.concatenate([block_of(step, layer) for layer in range(layers)], axis=1))
            lhs = jnp.concatenate([x_high, x_low], axis=0)
            both = lax.dot_general(lhs, high_ref[group], lanes_contract, preferred_element_type=f32)
            part = both[:columns] + both[columns:]
            part += lax.dot_general(x_high, low_ref[group], lanes_contract, preferred_element_type=f32)
            if step > begin:
                total_ref[...] += part
            elif start_ref is None:
                total_ref[...] = part
            else:
                total_ref[...] = start_ref[...] + part
        start = 0
        for out_ref in out_refs:
            for first in range(0, out_ref.shape[0], 2 * sources):
                real = pl.ds(start + first, sources)
                imag = pl.ds(start + first + sources, sources)
                out_ref[first:first + sources, :] = total_ref[real, :own_rows] - total_ref[imag, own_rows:]
                out_ref[first + sources:first + 2 * sources, :] = total_ref[imag, :own_rows] + total_ref[real, own_rows:]
            start += out_ref.shape[0]


def product_part(split, onward, layout, blocks, own, begin, end, started, sources, shares, relative):
    groups, both_rows, width = split[0].shape
    block = blocks[0].shape[-1]
    vmem = pl.BlockSpec(memory_space=pltpu.VMEM)
    finish = end == groups
    whole = (sum(shares), both_rows)
    arrays = list(blocks) + list(own) + list(split) + ([] if started is None else [started])
    if finish:
        out_shape = [jax.ShapeDtypeStruct((rows, both_rows // 2), f32) for rows in shares]
    else:
        out_shape = jax.ShapeDtypeStruct(whole, f32)
    return pl.pallas_call(
        functools.partial(product_kernel, sources, layout, len(blocks), 2 if own else 1, block, begin, end, onward, relative),
        in_specs=[vmem] * len(arrays),
        out_specs=[vmem] * len(shares) if finish else vmem,
        out_shape=out_shape,
        scratch_shapes=[pltpu.VMEM(whole, f32)] if finish else [],
        compiler_params=kernel_params(20),
        cost_estimate=pl.CostEstimate(flops=6 * sum(shares) * both_rows * width * (end - begin), bytes_accessed=MIB, transcendentals=0),
    )(*arrays)


def tied(value, to):
    return lax.optimization_barrier((value, to))[0]


def solve_paired(reduced, diag_inverse, coupling, sources):
    chain_size = lax.axis_size("chain")
    tile_size = lax.axis_size("tile")
    own_rows = reduced[0].shape[1]
    shares = [each.shape[0] for each in reduced]
    layers = tile_size // 4

    def send(value, hop, target):
        if not hop:
            return lax.ppermute(value, "tile", [(t, target(t)) for t in range(tile_size)])
        pairs = [(c * tile_size + t, (c + 1) % chain_size * tile_size + target(t)) for c in range(chain_size) for t in range(tile_size)]
        return lax.ppermute(value, ("chain", "tile"), pairs)

    def first_stage(first, second, hop):
        pair = [second if across == 0 and not hop else send(second, hop, lambda t: t ^ (2 * across)) for across in range(2)]
        if hop:
            line = [send(first, True, lambda t: (t + 4 * by) % tile_size) for by in range(layers)]
        else:
            line = [first if by == 0 else send(first, False, lambda t: t ^ (4 * by)) for by in range(layers)]
        if hop:
            *pair, line[-1] = lax.optimization_barrier((*pair, line[-1]))
        return jnp.stack(pair), jnp.stack(line)

    def second_stage(pair, line):
        far = send(line, False, lambda t: t ^ 2)
        rest = [pair if by == 0 else send(pair, False, lambda t: t ^ (4 * by)) for by in range(layers)]
        return [line, far, jnp.stack(rest)]

    layout = [lambda step, held, line: (step % 2, (line,)), lambda step, held, line: (2, (held, step % 2))]

    def products(split, onward, held, own, shares):
        other = [send(each, False, lambda t: t ^ 1) for each in held]
        mine, theirs = own if own else ([], [])
        started = product_part(split, onward, layout, held, mine, 0, 2, None, sources, shares, True)
        return product_part(split, onward, layout, other, theirs, 2, 4, started, sources, shares, True), other

    only = chain_size == 1
    pair, line = first_stage(*reduced, False)
    split = split_blocks(tied(diag_inverse if only else coupling, reduced[0]), own_rows, True)
    pair, line, split = lax.optimization_barrier((pair, line, split))
    held = second_stage(pair, line)
    if only:
        return products(split, False, held, None, [sum(shares)])[0][0]
    diag_split = split_blocks(tied(diag_inverse, line), own_rows, True)
    held[1], held[2], diag_split = lax.optimization_barrier((held[1], held[2], diag_split))
    carried, other = products(split, True, held, None, shares)
    own = (held, other)
    for step in range(chain_size - 1):
        held = second_stage(*lax.optimization_barrier(first_stage(*carried, True)))
        if step < chain_size - 2:
            carried = products(split, True, held, own, shares)[0]
    return products(diag_split, False, held, own, [sum(shares)])[0][0]


def solve_flat(reduced, diag_inverse, coupling, sources):
    chain_size = lax.axis_size("chain")
    reduced = reduced[0]
    columns = reduced.shape[0]
    full_rows = diag_inverse.shape[2]
    block = min(256, full_rows)
    count = full_rows // block
    layout = [lambda step, held, line: (0, (step * layers + held,))]
    onward = [(i, i + 1) for i in range(chain_size - 1)]
    diag_split = split_blocks(diag_inverse, block, False)
    coupling_split = split_blocks(coupling, block, False)
    groups = diag_split[0].shape[0]
    layers = count // groups

    def gathered(value):
        whole = lax.all_gather(value, "tile", axis=1, tiled=True)
        return [whole.reshape(columns, count, block).transpose(1, 0, 2)]

    current = reduced
    for _ in range(chain_size - 1):
        carried = product_part(coupling_split, True, layout, gathered(current), [], 0, groups, None, sources, [columns], False)[0]
        current = reduced - lax.ppermute(carried, "chain", onward)
    return product_part(diag_split, False, layout, gathered(current), [], 0, groups, None, sources, [columns], False)[0]


def body(right_side, diag_inverse, coupling, updates, update_rows, tile_counts):
    batches, halves, sources, own_rows = right_side.shape
    tile_size = lax.axis_size("tile")
    entries, columns = updates.shape
    tile_rows = entries // tile_counts.shape[0]
    cap = 2 * entries // tile_size
    slots = tile_size * cap
    vmem = pl.BlockSpec(memory_space=pltpu.VMEM)
    hbm = pl.BlockSpec(memory_space=pltpu.HBM)
    folded = cap % 16 == 0 and slots <= 1024 and columns == 192 and own_rows <= 256 and 128 % cap == 0
    width = 128 if folded else -(-(columns + 1) // 128) * 128
    height = cap + cap // 2 + 8 if folded else cap
    packed = pl.pallas_call(
        functools.partial(pack_kernel, own_rows, cap, tile_rows),
        in_specs=[hbm, hbm, hbm],
        out_specs=vmem,
        out_shape=jax.ShapeDtypeStruct((tile_size, height, width), f32),
        scratch_shapes=[
            pltpu.SMEM(tile_counts.shape, jnp.int32),
            pltpu.VMEM((1, entries), jnp.int32),
            pltpu.VMEM((columns, entries), f32),
            pltpu.SemaphoreType.DMA((3,)),
        ],
        compiler_params=kernel_params(56),
    )(tile_counts, update_rows[None, :], updates.T)
    received = lax.all_to_all(packed, "tile", 0, 0, tiled=False)
    paired = own_rows % 128 == 0 and tile_size >= 8 and tile_size & (tile_size - 1) == 0 and batches > 1
    early = batches * 2 // 3 * halves * sources
    shares = [early, columns - early] if paired else [columns]
    reduced = pl.pallas_call(
        functools.partial(reduce_kernel, cap),
        in_specs=[vmem, hbm],
        out_specs=[vmem] * len(shares),
        out_shape=[jax.ShapeDtypeStruct((rows, own_rows), f32) for rows in shares],
        scratch_shapes=[pltpu.VMEM((columns, own_rows), f32), pltpu.SemaphoreType.DMA(())],
        compiler_params=kernel_params(20),
    )(received, right_side.reshape(columns, own_rows))
    solve = solve_paired if paired else solve_flat
    return solve(reduced, diag_inverse, coupling, sources).reshape(right_side.shape)


def solution(mesh):
    in_specs = (
        P(None, None, None, ("chain", "tile")),
        P(None, ("chain", "tile"), None),
        P(None, ("chain", "tile"), None),
        P(("chain", "tile"), None),
        P(("chain", "tile")),
        P(("chain", "tile")),
    )
    out_specs = P(None, None, None, ("chain", "tile"))
    return jax.shard_map(body, mesh=mesh, in_specs=in_specs, out_specs=out_specs, check_vma=False)
```

```python
import functools

import jax
import jax.numpy as jnp
from jax import lax
from jax.experimental import pallas as pl
from jax.experimental.pallas import tpu as pltpu
from jax.sharding import PartitionSpec as P

MIB = 1 << 20
STORE = 24
f32 = jnp.float32
bf16 = jnp.bfloat16
lanes_contract = (((1,), (1,)), ((), ()))


def halves_of(value):
    high = value.astype(bf16)
    return high, (value - high.astype(f32)).astype(bf16)


def kernel_params(size):
    return pltpu.CompilerParams(vmem_limit_bytes=int(size * MIB))


def pack_kernel(own_rows, cap, tile_rows, counts_hbm, rows_hbm, updates_hbm, right_hbm, packed_ref, store_hbm, *scratch):
    counts_ref, rows_ref, updates_ref, sems = scratch
    keep = pltpu.make_async_copy(right_hbm, store_hbm.at[0], sems.at[3])
    moves = [
        pltpu.make_async_copy(counts_hbm, counts_ref, sems.at[0]),
        pltpu.make_async_copy(rows_hbm, rows_ref, sems.at[1]),
        pltpu.make_async_copy(updates_hbm, updates_ref, sems.at[2]),
    ]
    for move in moves:
        move.start()
    keep.start()
    columns, entries = updates_ref.shape
    owners, height, width = packed_ref.shape
    slots = owners * cap
    entry = lax.broadcasted_iota(jnp.int32, (1, entries), 1)
    earlier = lax.broadcasted_iota(jnp.int32, (entries, entries), 0) < lax.broadcasted_iota(jnp.int32, (entries, entries), 1)
    for move in moves:
        move.wait()
    live = jnp.zeros((1, entries), jnp.bool_)
    for tile in range(entries // tile_rows):
        start = tile * tile_rows
        live = live | ((entry >= start) & (entry < start + counts_ref[tile]))
    rows = rows_ref[...]
    owner = rows // own_rows
    lane_owner = jnp.broadcast_to(owner.astype(f32), (entries, entries))
    rank = jnp.sum(jnp.where(earlier & (lane_owner.T == lane_owner), 1, 0), axis=0, keepdims=True)
    slot = owner * cap + rank
    choose = jnp.where(lax.broadcasted_iota(jnp.int32, (slots, entries), 0) == slot, 1.0, 0.0).astype(bf16)
    data = jnp.where(live, updates_ref[...], 0.0)
    local_row = (rows - owner * own_rows).astype(f32)
    folded = height > cap
    if not folded:
        tail = jnp.where(lax.broadcasted_iota(jnp.int32, (width - columns, entries), 0) == 0, local_row, 0.0)
        data = jnp.concatenate([data, tail], axis=0)
    packed = jnp.zeros((slots, data.shape[0]), f32)
    for piece in halves_of(data):
        packed += lax.dot_general(choose, piece, lanes_contract, preferred_element_type=f32)
    packed = packed.reshape(owners, cap, data.shape[0])
    keep.wait()
    if not folded:
        packed_ref[...] = packed
        return
    half = cap // 2
    packed_ref[:, :cap, :] = packed[:, :, :width]
    packed_ref[:, cap:cap + half, :] = jnp.concatenate([packed[:, :half, width:], packed[:, half:, width:]], axis=2)
    first = lax.axis_index("tile") * cap
    by_owner = jnp.where(lax.broadcasted_iota(jnp.int32, (owners, entries), 0) == owner, local_row, 0.0).astype(bf16)
    by_lane = jnp.where(lax.broadcasted_iota(jnp.int32, (width, entries), 0) == first % width + rank, 1.0, 0.0).astype(bf16)
    numbers = lax.dot_general(by_owner, by_lane, lanes_contract, preferred_element_type=f32)
    line = lax.broadcasted_iota(jnp.int32, (owners, 8, width), 1)
    packed_ref[:, cap + half:, :] = jnp.where(line == first // width, numbers[:, None, :], 0.0)


def reduce_kernel(cap, received_ref, right_hbm, *refs):
    reduced_refs, right_ref, sem = refs[:-2], refs[-2], refs[-1]
    move = pltpu.make_async_copy(right_hbm.at[0], right_ref, sem)
    move.start()
    owners, height, width = received_ref.shape
    slots = owners * cap
    columns, own_rows = right_ref.shape
    if height > cap:
        half = cap // 2
        numbers = jnp.sum(received_ref[:, cap + half:, :], axis=0)
        numbers = jnp.concatenate([numbers[i:i + 1] for i in range(slots // width)], axis=1).astype(jnp.int32)
        rest = received_ref[:, cap:cap + half, :]
        rest = jnp.concatenate([rest[:, :, :width // 2], rest[:, :, width // 2:]], axis=1)
        sets = [received_ref[:, :cap, :].reshape(slots, width), rest.reshape(slots, width // 2)]
        place = jnp.where(lax.broadcasted_iota(jnp.int32, (own_rows, slots), 0) == numbers, 1.0, 0.0).astype(bf16)
        totals = []
        for value in sets:
            total = jnp.zeros((own_rows, value.shape[1]), f32)
            for piece in halves_of(value):
                total += jnp.dot(place, piece, preferred_element_type=f32)
            totals.append(total.T)
        total = jnp.concatenate(totals, axis=0)
    else:
        received = received_ref[...].reshape(slots, width)
        local_row = received[:, columns:columns + 1].astype(jnp.int32)
        place = jnp.where(lax.broadcasted_iota(jnp.int32, (slots, own_rows), 1) == local_row, 1.0, 0.0).astype(bf16)
        total = jnp.zeros((columns, own_rows), f32)
        for piece in halves_of(received[:, :columns].T):
            total += jnp.dot(piece, place, preferred_element_type=f32)
    move.wait()
    start = 0
    for reduced_ref in reduced_refs:
        rows = reduced_ref.shape[0]
        reduced_ref[...] = right_ref[start:start + rows, :] - total[start:start + rows]
        start += rows


def split_kernel(block, relative, matrix_ref, high_ref, low_ref):
    parts, own_rows, full_rows = matrix_ref.shape
    groups, rows, width = high_ref.shape
    layers = width // block
    height = 64
    for part in range(parts):
        for first in range(0, own_rows, height):
            start = part * own_rows + first
            for group in range(groups):
                for layer in range(layers):
                    column = (layer * groups + group if relative else group * layers + layer) * block
                    high, low = halves_of(matrix_ref[part, first:first + height, column:column + block])
                    high_ref[group, start:start + height, layer * block:(layer + 1) * block] = high
                    low_ref[group, start:start + height, layer * block:(layer + 1) * block] = low


def split_blocks(matrix, block, relative):
    parts, own_rows, full_rows = matrix.shape
    groups = 4 if full_rows % (4 * block) == 0 else 1
    vmem = pl.BlockSpec(memory_space=pltpu.VMEM)
    shape = jax.ShapeDtypeStruct((groups, parts * own_rows, full_rows // groups), bf16)
    return pl.pallas_call(
        functools.partial(split_kernel, block, relative),
        in_specs=[vmem],
        out_specs=[vmem, vmem],
        out_shape=[shape, shape],
        compiler_params=kernel_params(20),
        cost_estimate=pl.CostEstimate(flops=3 * matrix.size, bytes_accessed=8 * matrix.size, transcendentals=0),
    )(matrix)


def product_kernel(sources, layout, inputs, sets, block, begin, end, onward, relative, *refs):
    high_ref, low_ref = refs[inputs * sets:inputs * sets + 2]
    rest = refs[inputs * sets + 2:]
    groups, both_rows, width = high_ref.shape
    layers = width // block
    own_rows = both_rows // 2
    start_ref, rest = (rest[0], rest[1:]) if begin > 0 else (None, rest)
    out_refs, total_ref = (rest[:-1], rest[-1]) if end == groups else ((), rest[0])
    columns = total_ref.shape[0]
    me = lax.axis_index("tile")

    def block_of(step, layer):
        held = lax.div(me, 4) ^ layer if relative else layer
        hopped = lax.rem(lax.div(me, 4) + (layers - layer), layers)
        pieces = []
        for group in layout:
            which, place = group(step, held, held if sets == 1 else hopped)
            value = refs[which][place]
            if sets == 2:
                which, place = group(step, held, held)
                own = refs[inputs + which][place]
                value = jnp.where(lax.axis_index("chain") == 0, own, own - value)
            pieces.append(value)
        return jnp.concatenate(pieces, axis=0)

    active = jnp.logical_not(onward) | (lax.axis_index("chain") < lax.axis_size("chain") - 1)

    @pl.when(jnp.logical_not(active))
    def _():
        for out_ref in out_refs:
            out_ref[...] = jnp.zeros_like(out_ref)

    @pl.when(active)
    def _():
        for step in range(begin, end):
            group = step
            if relative:
                group = lax.rem(lax.div(me, 2) + step % 2, 2) * 2 + lax.rem(me + step // 2, 2)
            x_high, x_low = halves_of(jnp.concatenate([block_of(step, layer) for layer in range(layers)], axis=1))
            lhs = jnp.concatenate([x_high, x_low], axis=0)
            both = lax.dot_general(lhs, high_ref[group], lanes_contract, preferred_element_type=f32)
            part = both[:columns] + both[columns:]
            part += lax.dot_general(x_high, low_ref[group], lanes_contract, preferred_element_type=f32)
            if step > begin:
                total_ref[...] += part
            elif start_ref is None:
                total_ref[...] = part
            else:
                total_ref[...] = start_ref[...] + part
        start = 0
        for out_ref in out_refs:
            for first in range(0, out_ref.shape[0], 2 * sources):
                real = pl.ds(start + first, sources)
                imag = pl.ds(start + first + sources, sources)
                out_ref[first:first + sources, :] = total_ref[real, :own_rows] - total_ref[imag, own_rows:]
                out_ref[first + sources:first + 2 * sources, :] = total_ref[imag, :own_rows] + total_ref[real, own_rows:]
            start += out_ref.shape[0]


def product_part(split, onward, layout, blocks, own, begin, end, started, sources, shares, relative):
    groups, both_rows, width = split[0].shape
    block = blocks[0].shape[-1]
    vmem = pl.BlockSpec(memory_space=pltpu.VMEM)
    finish = end == groups
    whole = (sum(shares), both_rows)
    arrays = list(blocks) + list(own) + list(split) + ([] if started is None else [started])
    if finish:
        out_shape = [jax.ShapeDtypeStruct((rows, both_rows // 2), f32) for rows in shares]
    else:
        out_shape = jax.ShapeDtypeStruct(whole, f32)
    return pl.pallas_call(
        functools.partial(product_kernel, sources, layout, len(blocks), 2 if own else 1, block, begin, end, onward, relative),
        in_specs=[vmem] * len(arrays),
        out_specs=[vmem] * len(shares) if finish else vmem,
        out_shape=out_shape,
        scratch_shapes=[pltpu.VMEM(whole, f32)] if finish else [],
        compiler_params=kernel_params(20),
        cost_estimate=pl.CostEstimate(flops=6 * sum(shares) * both_rows * width * (end - begin), bytes_accessed=MIB, transcendentals=0),
    )(*arrays)


def tied(value, to):
    return lax.optimization_barrier((value, to))[0]


def solve_paired(reduced, diag_inverse, coupling, sources):
    chain_size = lax.axis_size("chain")
    tile_size = lax.axis_size("tile")
    own_rows = reduced[0].shape[1]
    shares = [each.shape[0] for each in reduced]
    layers = tile_size // 4

    def send(value, hop, target):
        if not hop:
            return lax.ppermute(value, "tile", [(t, target(t)) for t in range(tile_size)])
        pairs = [(c * tile_size + t, (c + 1) % chain_size * tile_size + target(t)) for c in range(chain_size) for t in range(tile_size)]
        return lax.ppermute(value, ("chain", "tile"), pairs)

    def first_stage(first, second, hop):
        pair = [second if across == 0 and not hop else send(second, hop, lambda t: t ^ (2 * across)) for across in range(2)]
        if hop:
            line = [send(first, True, lambda t: (t + 4 * by) % tile_size) for by in range(layers)]
        else:
            line = [first if by == 0 else send(first, False, lambda t: t ^ (4 * by)) for by in range(layers)]
        if hop:
            *pair, line[-1] = lax.optimization_barrier((*pair, line[-1]))
        return jnp.stack(pair), jnp.stack(line)

    def second_stage(pair, line):
        far = send(line, False, lambda t: t ^ 2)
        rest = [pair if by == 0 else send(pair, False, lambda t: t ^ (4 * by)) for by in range(layers)]
        return [line, far, jnp.stack(rest)]

    layout = [lambda step, held, line: (step % 2, (line,)), lambda step, held, line: (2, (held, step % 2))]

    def products(split, onward, held, own, shares):
        other = [send(each, False, lambda t: t ^ 1) for each in held]
        mine, theirs = own if own else ([], [])
        started = product_part(split, onward, layout, held, mine, 0, 2, None, sources, shares, True)
        return product_part(split, onward, layout, other, theirs, 2, 4, started, sources, shares, True), other

    only = chain_size == 1
    pair, line = first_stage(*reduced, False)
    split = split_blocks(tied(diag_inverse if only else coupling, reduced[0]), own_rows, True)
    pair, line, split = lax.optimization_barrier((pair, line, split))
    held = second_stage(pair, line)
    if only:
        return products(split, False, held, None, [sum(shares)])[0][0]
    diag_split = split_blocks(tied(diag_inverse, line), own_rows, True)
    held[1], held[2], diag_split = lax.optimization_barrier((held[1], held[2], diag_split))
    carried, other = products(split, True, held, None, shares)
    own = (held, other)
    for step in range(chain_size - 1):
        held = second_stage(*lax.optimization_barrier(first_stage(*carried, True)))
        if step < chain_size - 2:
            carried = products(split, True, held, own, shares)[0]
    return products(diag_split, False, held, own, [sum(shares)])[0][0]


def solve_flat(reduced, diag_inverse, coupling, sources):
    chain_size = lax.axis_size("chain")
    reduced = reduced[0]
    columns = reduced.shape[0]
    full_rows = diag_inverse.shape[2]
    block = min(256, full_rows)
    count = full_rows // block
    layout = [lambda step, held, line: (0, (step * layers + held,))]
    onward = [(i, i + 1) for i in range(chain_size - 1)]
    diag_split = split_blocks(diag_inverse, block, False)
    coupling_split = split_blocks(coupling, block, False)
    groups = diag_split[0].shape[0]
    layers = count // groups

    def gathered(value):
        whole = lax.all_gather(value, "tile", axis=1, tiled=True)
        return [whole.reshape(columns, count, block).transpose(1, 0, 2)]

    current = reduced
    for _ in range(chain_size - 1):
        carried = product_part(coupling_split, True, layout, gathered(current), [], 0, groups, None, sources, [columns], False)[0]
        current = reduced - lax.ppermute(carried, "chain", onward)
    return product_part(diag_split, False, layout, gathered(current), [], 0, groups, None, sources, [columns], False)[0]


def body(right_side, diag_inverse, coupling, updates, update_rows, tile_counts):
    batches, halves, sources, own_rows = right_side.shape
    tile_size = lax.axis_size("tile")
    entries, columns = updates.shape
    tile_rows = entries // tile_counts.shape[0]
    cap = 2 * entries // tile_size
    slots = tile_size * cap
    vmem = pl.BlockSpec(memory_space=pltpu.VMEM)
    hbm = pl.BlockSpec(memory_space=pltpu.HBM)
    folded = cap % 16 == 0 and slots <= 1024 and columns == 192 and own_rows <= 256 and 128 % cap == 0
    width = 128 if folded else -(-(columns + 1) // 128) * 128
    height = cap + cap // 2 + 8 if folded else cap
    packed, stored = pl.pallas_call(
        functools.partial(pack_kernel, own_rows, cap, tile_rows),
        in_specs=[hbm, hbm, hbm, hbm],
        out_specs=[vmem, hbm],
        out_shape=[
            jax.ShapeDtypeStruct((tile_size, height, width), f32),
            jax.ShapeDtypeStruct((STORE, columns, own_rows), f32),
        ],
        scratch_shapes=[
            pltpu.SMEM(tile_counts.shape, jnp.int32),
            pltpu.VMEM((1, entries), jnp.int32),
            pltpu.VMEM((columns, entries), f32),
            pltpu.SemaphoreType.DMA((4,)),
        ],
        compiler_params=kernel_params(56),
    )(tile_counts, update_rows[None, :], updates.T, right_side.reshape(columns, own_rows))
    received = lax.all_to_all(packed, "tile", 0, 0, tiled=False)
    paired = own_rows % 128 == 0 and tile_size >= 8 and tile_size & (tile_size - 1) == 0 and batches > 1
    early = batches * 2 // 3 * halves * sources
    shares = [early, columns - early] if paired else [columns]
    reduced = pl.pallas_call(
        functools.partial(reduce_kernel, cap),
        in_specs=[vmem, hbm],
        out_specs=[vmem] * len(shares),
        out_shape=[jax.ShapeDtypeStruct((rows, own_rows), f32) for rows in shares],
        scratch_shapes=[pltpu.VMEM((columns, own_rows), f32), pltpu.SemaphoreType.DMA(())],
        compiler_params=kernel_params(50),
    )(received, stored)
    solve = solve_paired if paired else solve_flat
    return solve(reduced, diag_inverse, coupling, sources).reshape(right_side.shape)


def solution(mesh):
    in_specs = (
        P(None, None, None, ("chain", "tile")),
        P(None, ("chain", "tile"), None),
        P(None, ("chain", "tile"), None),
        P(("chain", "tile"), None),
        P(("chain", "tile")),
        P(("chain", "tile")),
    )
    out_specs = P(None, None, None, ("chain", "tile"))
    return jax.shard_map(body, mesh=mesh, in_specs=in_specs, out_specs=out_specs, check_vma=False)
```

```python
import functools

import jax
import jax.numpy as jnp
from jax import lax
from jax.experimental import pallas as pl
from jax.experimental.pallas import tpu as pltpu
from jax.sharding import PartitionSpec as P

MIB = 1 << 20
STORE = 24
f32 = jnp.float32
bf16 = jnp.bfloat16
lanes_contract = (((1,), (1,)), ((), ()))


def halves_of(value):
    high = value.astype(bf16)
    return high, (value - high.astype(f32)).astype(bf16)


def kernel_params(size):
    return pltpu.CompilerParams(vmem_limit_bytes=int(size * MIB))


def pack_kernel(own_rows, cap, tile_rows, counts_hbm, rows_hbm, updates_hbm, right_hbm, packed_ref, store_hbm, *scratch):
    counts_ref, rows_ref, updates_ref, right_ref, sems = scratch
    fetch = pltpu.make_async_copy(right_hbm, right_ref, sems.at[3])
    keep = pltpu.make_async_copy(right_ref, store_hbm.at[0], sems.at[4])
    moves = [
        pltpu.make_async_copy(counts_hbm, counts_ref, sems.at[0]),
        pltpu.make_async_copy(rows_hbm, rows_ref, sems.at[1]),
        pltpu.make_async_copy(updates_hbm, updates_ref, sems.at[2]),
    ]
    for move in moves:
        move.start()
    fetch.start()
    columns, entries = updates_ref.shape
    owners, height, width = packed_ref.shape
    slots = owners * cap
    entry = lax.broadcasted_iota(jnp.int32, (1, entries), 1)
    earlier = lax.broadcasted_iota(jnp.int32, (entries, entries), 0) < lax.broadcasted_iota(jnp.int32, (entries, entries), 1)
    for move in moves:
        move.wait()
    fetch.wait()
    keep.start()
    live = jnp.zeros((1, entries), jnp.bool_)
    for tile in range(entries // tile_rows):
        start = tile * tile_rows
        live = live | ((entry >= start) & (entry < start + counts_ref[tile]))
    rows = rows_ref[...]
    owner = rows // own_rows
    lane_owner = jnp.broadcast_to(owner.astype(f32), (entries, entries))
    rank = jnp.sum(jnp.where(earlier & (lane_owner.T == lane_owner), 1, 0), axis=0, keepdims=True)
    slot = owner * cap + rank
    choose = jnp.where(lax.broadcasted_iota(jnp.int32, (slots, entries), 0) == slot, 1.0, 0.0).astype(bf16)
    data = jnp.where(live, updates_ref[...], 0.0)
    local_row = (rows - owner * own_rows).astype(f32)
    folded = height > cap
    if not folded:
        tail = jnp.where(lax.broadcasted_iota(jnp.int32, (width - columns, entries), 0) == 0, local_row, 0.0)
        data = jnp.concatenate([data, tail], axis=0)
    packed = jnp.zeros((slots, data.shape[0]), f32)
    for piece in halves_of(data):
        packed += lax.dot_general(choose, piece, lanes_contract, preferred_element_type=f32)
    packed = packed.reshape(owners, cap, data.shape[0])
    keep.wait()
    if not folded:
        packed_ref[...] = packed
        return
    half = cap // 2
    packed_ref[:, :cap, :] = packed[:, :, :width]
    packed_ref[:, cap:cap + half, :] = jnp.concatenate([packed[:, :half, width:], packed[:, half:, width:]], axis=2)
    first = lax.axis_index("tile") * cap
    by_owner = jnp.where(lax.broadcasted_iota(jnp.int32, (owners, entries), 0) == owner, local_row, 0.0).astype(bf16)
    by_lane = jnp.where(lax.broadcasted_iota(jnp.int32, (width, entries), 0) == first % width + rank, 1.0, 0.0).astype(bf16)
    numbers = lax.dot_general(by_owner, by_lane, lanes_contract, preferred_element_type=f32)
    line = lax.broadcasted_iota(jnp.int32, (owners, 8, width), 1)
    packed_ref[:, cap + half:, :] = jnp.where(line == first // width, numbers[:, None, :], 0.0)


def reduce_kernel(cap, received_ref, right_hbm, *refs):
    reduced_refs, right_ref, sem = refs[:-2], refs[-2], refs[-1]
    move = pltpu.make_async_copy(right_hbm.at[0], right_ref, sem)
    move.start()
    owners, height, width = received_ref.shape
    slots = owners * cap
    columns, own_rows = right_ref.shape
    if height > cap:
        half = cap // 2
        numbers = jnp.sum(received_ref[:, cap + half:, :], axis=0)
        numbers = jnp.concatenate([numbers[i:i + 1] for i in range(slots // width)], axis=1).astype(jnp.int32)
        rest = received_ref[:, cap:cap + half, :]
        rest = jnp.concatenate([rest[:, :, :width // 2], rest[:, :, width // 2:]], axis=1)
        sets = [received_ref[:, :cap, :].reshape(slots, width), rest.reshape(slots, width // 2)]
        place = jnp.where(lax.broadcasted_iota(jnp.int32, (own_rows, slots), 0) == numbers, 1.0, 0.0).astype(bf16)
        totals = []
        for value in sets:
            total = jnp.zeros((own_rows, value.shape[1]), f32)
            for piece in halves_of(value):
                total += jnp.dot(place, piece, preferred_element_type=f32)
            totals.append(total.T)
        total = jnp.concatenate(totals, axis=0)
    else:
        received = received_ref[...].reshape(slots, width)
        local_row = received[:, columns:columns + 1].astype(jnp.int32)
        place = jnp.where(lax.broadcasted_iota(jnp.int32, (slots, own_rows), 1) == local_row, 1.0, 0.0).astype(bf16)
        total = jnp.zeros((columns, own_rows), f32)
        for piece in halves_of(received[:, :columns].T):
            total += jnp.dot(piece, place, preferred_element_type=f32)
    move.wait()
    start = 0
    for reduced_ref in reduced_refs:
        rows = reduced_ref.shape[0]
        reduced_ref[...] = right_ref[start:start + rows, :] - total[start:start + rows]
        start += rows


def split_kernel(block, relative, matrix_ref, high_ref, low_ref):
    parts, own_rows, full_rows = matrix_ref.shape
    groups, rows, width = high_ref.shape
    layers = width // block
    height = 64
    for part in range(parts):
        for first in range(0, own_rows, height):
            start = part * own_rows + first
            for group in range(groups):
                for layer in range(layers):
                    column = (layer * groups + group if relative else group * layers + layer) * block
                    high, low = halves_of(matrix_ref[part, first:first + height, column:column + block])
                    high_ref[group, start:start + height, layer * block:(layer + 1) * block] = high
                    low_ref[group, start:start + height, layer * block:(layer + 1) * block] = low


def split_blocks(matrix, block, relative):
    parts, own_rows, full_rows = matrix.shape
    groups = 4 if full_rows % (4 * block) == 0 else 1
    vmem = pl.BlockSpec(memory_space=pltpu.VMEM)
    shape = jax.ShapeDtypeStruct((groups, parts * own_rows, full_rows // groups), bf16)
    return pl.pallas_call(
        functools.partial(split_kernel, block, relative),
        in_specs=[vmem],
        out_specs=[vmem, vmem],
        out_shape=[shape, shape],
        compiler_params=kernel_params(20),
        cost_estimate=pl.CostEstimate(flops=3 * matrix.size, bytes_accessed=8 * matrix.size, transcendentals=0),
    )(matrix)


def product_kernel(sources, layout, inputs, sets, block, begin, end, onward, relative, *refs):
    high_ref, low_ref = refs[inputs * sets:inputs * sets + 2]
    rest = refs[inputs * sets + 2:]
    groups, both_rows, width = high_ref.shape
    layers = width // block
    own_rows = both_rows // 2
    start_ref, rest = (rest[0], rest[1:]) if begin > 0 else (None, rest)
    out_refs, total_ref = (rest[:-1], rest[-1]) if end == groups else ((), rest[0])
    columns = total_ref.shape[0]
    me = lax.axis_index("tile")

    def block_of(step, layer):
        held = lax.div(me, 4) ^ layer if relative else layer
        hopped = lax.rem(lax.div(me, 4) + (layers - layer), layers)
        pieces = []
        for group in layout:
            which, place = group(step, held, held if sets == 1 else hopped)
            value = refs[which][place]
            if sets == 2:
                which, place = group(step, held, held)
                own = refs[inputs + which][place]
                value = jnp.where(lax.axis_index("chain") == 0, own, own - value)
            pieces.append(value)
        return jnp.concatenate(pieces, axis=0)

    active = jnp.logical_not(onward) | (lax.axis_index("chain") < lax.axis_size("chain") - 1)

    @pl.when(jnp.logical_not(active))
    def _():
        for out_ref in out_refs:
            out_ref[...] = jnp.zeros_like(out_ref)

    @pl.when(active)
    def _():
        for step in range(begin, end):
            group = step
            if relative:
                group = lax.rem(lax.div(me, 2) + step % 2, 2) * 2 + lax.rem(me + step // 2, 2)
            x_high, x_low = halves_of(jnp.concatenate([block_of(step, layer) for layer in range(layers)], axis=1))
            lhs = jnp.concatenate([x_high, x_low], axis=0)
            both = lax.dot_general(lhs, high_ref[group], lanes_contract, preferred_element_type=f32)
            part = both[:columns] + both[columns:]
            part += lax.dot_general(x_high, low_ref[group], lanes_contract, preferred_element_type=f32)
            if step > begin:
                total_ref[...] += part
            elif start_ref is None:
                total_ref[...] = part
            else:
                total_ref[...] = start_ref[...] + part
        start = 0
        for out_ref in out_refs:
            for first in range(0, out_ref.shape[0], 2 * sources):
                real = pl.ds(start + first, sources)
                imag = pl.ds(start + first + sources, sources)
                out_ref[first:first + sources, :] = total_ref[real, :own_rows] - total_ref[imag, own_rows:]
                out_ref[first + sources:first + 2 * sources, :] = total_ref[imag, :own_rows] + total_ref[real, own_rows:]
            start += out_ref.shape[0]


def product_part(split, onward, layout, blocks, own, begin, end, started, sources, shares, relative):
    groups, both_rows, width = split[0].shape
    block = blocks[0].shape[-1]
    vmem = pl.BlockSpec(memory_space=pltpu.VMEM)
    finish = end == groups
    whole = (sum(shares), both_rows)
    arrays = list(blocks) + list(own) + list(split) + ([] if started is None else [started])
    if finish:
        out_shape = [jax.ShapeDtypeStruct((rows, both_rows // 2), f32) for rows in shares]
    else:
        out_shape = jax.ShapeDtypeStruct(whole, f32)
    return pl.pallas_call(
        functools.partial(product_kernel, sources, layout, len(blocks), 2 if own else 1, block, begin, end, onward, relative),
        in_specs=[vmem] * len(arrays),
        out_specs=[vmem] * len(shares) if finish else vmem,
        out_shape=out_shape,
        scratch_shapes=[pltpu.VMEM(whole, f32)] if finish else [],
        compiler_params=kernel_params(20),
        cost_estimate=pl.CostEstimate(flops=6 * sum(shares) * both_rows * width * (end - begin), bytes_accessed=MIB, transcendentals=0),
    )(*arrays)


def tied(value, to):
    return lax.optimization_barrier((value, to))[0]


def solve_paired(reduced, diag_inverse, coupling, sources):
    chain_size = lax.axis_size("chain")
    tile_size = lax.axis_size("tile")
    own_rows = reduced[0].shape[1]
    shares = [each.shape[0] for each in reduced]
    layers = tile_size // 4

    def send(value, hop, target):
        if not hop:
            return lax.ppermute(value, "tile", [(t, target(t)) for t in range(tile_size)])
        pairs = [(c * tile_size + t, (c + 1) % chain_size * tile_size + target(t)) for c in range(chain_size) for t in range(tile_size)]
        return lax.ppermute(value, ("chain", "tile"), pairs)

    def first_stage(first, second, hop):
        pair = [second if across == 0 and not hop else send(second, hop, lambda t: t ^ (2 * across)) for across in range(2)]
        if hop:
            line = [send(first, True, lambda t: (t + 4 * by) % tile_size) for by in range(layers)]
        else:
            line = [first if by == 0 else send(first, False, lambda t: t ^ (4 * by)) for by in range(layers)]
        if hop:
            *pair, line[-1] = lax.optimization_barrier((*pair, line[-1]))
        return jnp.stack(pair), jnp.stack(line)

    def second_stage(pair, line):
        far = send(line, False, lambda t: t ^ 2)
        rest = [pair if by == 0 else send(pair, False, lambda t: t ^ (4 * by)) for by in range(layers)]
        return [line, far, jnp.stack(rest)]

    layout = [lambda step, held, line: (step % 2, (line,)), lambda step, held, line: (2, (held, step % 2))]

    def products(split, onward, held, own, shares):
        other = [send(each, False, lambda t: t ^ 1) for each in held]
        mine, theirs = own if own else ([], [])
        started = product_part(split, onward, layout, held, mine, 0, 2, None, sources, shares, True)
        return product_part(split, onward, layout, other, theirs, 2, 4, started, sources, shares, True), other

    only = chain_size == 1
    pair, line = first_stage(*reduced, False)
    split = split_blocks(tied(diag_inverse if only else coupling, reduced[0]), own_rows, True)
    pair, line, split = lax.optimization_barrier((pair, line, split))
    held = second_stage(pair, line)
    if only:
        return products(split, False, held, None, [sum(shares)])[0][0]
    diag_split = split_blocks(tied(diag_inverse, line), own_rows, True)
    held[1], held[2], diag_split = lax.optimization_barrier((held[1], held[2], diag_split))
    carried, other = products(split, True, held, None, shares)
    own = (held, other)
    for step in range(chain_size - 1):
        held = second_stage(*lax.optimization_barrier(first_stage(*carried, True)))
        if step < chain_size - 2:
            carried = products(split, True, held, own, shares)[0]
    return products(diag_split, False, held, own, [sum(shares)])[0][0]


def solve_flat(reduced, diag_inverse, coupling, sources):
    chain_size = lax.axis_size("chain")
    reduced = reduced[0]
    columns = reduced.shape[0]
    full_rows = diag_inverse.shape[2]
    block = min(256, full_rows)
    count = full_rows // block
    layout = [lambda step, held, line: (0, (step * layers + held,))]
    onward = [(i, i + 1) for i in range(chain_size - 1)]
    diag_split = split_blocks(diag_inverse, block, False)
    coupling_split = split_blocks(coupling, block, False)
    groups = diag_split[0].shape[0]
    layers = count // groups

    def gathered(value):
        whole = lax.all_gather(value, "tile", axis=1, tiled=True)
        return [whole.reshape(columns, count, block).transpose(1, 0, 2)]

    current = reduced
    for _ in range(chain_size - 1):
        carried = product_part(coupling_split, True, layout, gathered(current), [], 0, groups, None, sources, [columns], False)[0]
        current = reduced - lax.ppermute(carried, "chain", onward)
    return product_part(diag_split, False, layout, gathered(current), [], 0, groups, None, sources, [columns], False)[0]


def body(right_side, diag_inverse, coupling, updates, update_rows, tile_counts):
    batches, halves, sources, own_rows = right_side.shape
    tile_size = lax.axis_size("tile")
    entries, columns = updates.shape
    tile_rows = entries // tile_counts.shape[0]
    cap = 2 * entries // tile_size
    slots = tile_size * cap
    vmem = pl.BlockSpec(memory_space=pltpu.VMEM)
    hbm = pl.BlockSpec(memory_space=pltpu.HBM)
    folded = cap % 16 == 0 and slots <= 1024 and columns == 192 and own_rows <= 256 and 128 % cap == 0
    width = 128 if folded else -(-(columns + 1) // 128) * 128
    height = cap + cap // 2 + 8 if folded else cap
    packed, stored = pl.pallas_call(
        functools.partial(pack_kernel, own_rows, cap, tile_rows),
        in_specs=[hbm, hbm, hbm, hbm],
        out_specs=[vmem, hbm],
        out_shape=[
            jax.ShapeDtypeStruct((tile_size, height, width), f32),
            jax.ShapeDtypeStruct((STORE, columns, own_rows), f32),
        ],
        scratch_shapes=[
            pltpu.SMEM(tile_counts.shape, jnp.int32),
            pltpu.VMEM((1, entries), jnp.int32),
            pltpu.VMEM((columns, entries), f32),
            pltpu.VMEM((columns, own_rows), f32),
            pltpu.SemaphoreType.DMA((5,)),
        ],
        compiler_params=kernel_params(56),
    )(tile_counts, update_rows[None, :], updates.T, right_side.reshape(columns, own_rows))
    received = lax.all_to_all(packed, "tile", 0, 0, tiled=False)
    paired = own_rows % 128 == 0 and tile_size >= 8 and tile_size & (tile_size - 1) == 0 and batches > 1
    early = batches * 2 // 3 * halves * sources
    shares = [early, columns - early] if paired else [columns]
    reduced = pl.pallas_call(
        functools.partial(reduce_kernel, cap),
        in_specs=[vmem, hbm],
        out_specs=[vmem] * len(shares),
        out_shape=[jax.ShapeDtypeStruct((rows, own_rows), f32) for rows in shares],
        scratch_shapes=[pltpu.VMEM((columns, own_rows), f32), pltpu.SemaphoreType.DMA(())],
        compiler_params=kernel_params(50),
    )(received, stored)
    solve = solve_paired if paired else solve_flat
    return solve(reduced, diag_inverse, coupling, sources).reshape(right_side.shape)


def solution(mesh):
    in_specs = (
        P(None, None, None, ("chain", "tile")),
        P(None, ("chain", "tile"), None),
        P(None, ("chain", "tile"), None),
        P(("chain", "tile"), None),
        P(("chain", "tile")),
        P(("chain", "tile")),
    )
    out_specs = P(None, None, None, ("chain", "tile"))
    return jax.shard_map(body, mesh=mesh, in_specs=in_specs, out_specs=out_specs, check_vma=False)
```

```python
import functools

import jax
import jax.numpy as jnp
from jax import lax
from jax.experimental import pallas as pl
from jax.experimental.pallas import tpu as pltpu
from jax.sharding import PartitionSpec as P

MIB = 1 << 20
STORE = 24
f32 = jnp.float32
bf16 = jnp.bfloat16
lanes_contract = (((1,), (1,)), ((), ()))


def halves_of(value):
    high = value.astype(bf16)
    return high, (value - high.astype(f32)).astype(bf16)


def kernel_params(size):
    return pltpu.CompilerParams(vmem_limit_bytes=int(size * MIB))


def pack_kernel(own_rows, cap, tile_rows, counts_hbm, rows_hbm, updates_hbm, right_hbm, packed_ref, store_hbm, *scratch):
    counts_ref, rows_ref, updates_ref, right_ref, sems = scratch
    fetch = pltpu.make_async_copy(right_hbm, right_ref, sems.at[3])
    keep = pltpu.make_async_copy(right_ref, store_hbm.at[0], sems.at[4])
    moves = [
        pltpu.make_async_copy(counts_hbm, counts_ref, sems.at[0]),
        pltpu.make_async_copy(rows_hbm, rows_ref, sems.at[1]),
        pltpu.make_async_copy(updates_hbm, updates_ref, sems.at[2]),
    ]
    for move in moves:
        move.start()
    fetch.start()
    columns, entries = updates_ref.shape
    owners, height, width = packed_ref.shape
    slots = owners * cap
    entry = lax.broadcasted_iota(jnp.int32, (1, entries), 1)
    earlier = lax.broadcasted_iota(jnp.int32, (entries, entries), 0) < lax.broadcasted_iota(jnp.int32, (entries, entries), 1)
    for move in moves:
        move.wait()
    live = jnp.zeros((1, entries), jnp.bool_)
    for tile in range(entries // tile_rows):
        start = tile * tile_rows
        live = live | ((entry >= start) & (entry < start + counts_ref[tile]))
    rows = rows_ref[...]
    owner = rows // own_rows
    lane_owner = jnp.broadcast_to(owner.astype(f32), (entries, entries))
    rank = jnp.sum(jnp.where(earlier & (lane_owner.T == lane_owner), 1, 0), axis=0, keepdims=True)
    slot = owner * cap + rank
    choose = jnp.where(lax.broadcasted_iota(jnp.int32, (slots, entries), 0) == slot, 1.0, 0.0).astype(bf16)
    data = jnp.where(live, updates_ref[...], 0.0)
    local_row = (rows - owner * own_rows).astype(f32)
    folded = height > cap
    if not folded:
        tail = jnp.where(lax.broadcasted_iota(jnp.int32, (width - columns, entries), 0) == 0, local_row, 0.0)
        data = jnp.concatenate([data, tail], axis=0)
    fetch.wait()
    keep.start()
    packed = jnp.zeros((slots, data.shape[0]), f32)
    for piece in halves_of(data):
        packed += lax.dot_general(choose, piece, lanes_contract, preferred_element_type=f32)
    packed = packed.reshape(owners, cap, data.shape[0])
    keep.wait()
    if not folded:
        packed_ref[...] = packed
        return
    half = cap // 2
    packed_ref[:, :cap, :] = packed[:, :, :width]
    packed_ref[:, cap:cap + half, :] = jnp.concatenate([packed[:, :half, width:], packed[:, half:, width:]], axis=2)
    first = lax.axis_index("tile") * cap
    by_owner = jnp.where(lax.broadcasted_iota(jnp.int32, (owners, entries), 0) == owner, local_row, 0.0).astype(bf16)
    by_lane = jnp.where(lax.broadcasted_iota(jnp.int32, (width, entries), 0) == first % width + rank, 1.0, 0.0).astype(bf16)
    numbers = lax.dot_general(by_owner, by_lane, lanes_contract, preferred_element_type=f32)
    line = lax.broadcasted_iota(jnp.int32, (owners, 8, width), 1)
    packed_ref[:, cap + half:, :] = jnp.where(line == first // width, numbers[:, None, :], 0.0)


def reduce_kernel(cap, received_ref, right_hbm, *refs):
    reduced_refs, right_ref, sem = refs[:-2], refs[-2], refs[-1]
    move = pltpu.make_async_copy(right_hbm.at[0], right_ref, sem)
    move.start()
    owners, height, width = received_ref.shape
    slots = owners * cap
    columns, own_rows = right_ref.shape
    if height > cap:
        half = cap // 2
        numbers = jnp.sum(received_ref[:, cap + half:, :], axis=0)
        numbers = jnp.concatenate([numbers[i:i + 1] for i in range(slots // width)], axis=1).astype(jnp.int32)
        rest = received_ref[:, cap:cap + half, :]
        rest = jnp.concatenate([rest[:, :, :width // 2], rest[:, :, width // 2:]], axis=1)
        sets = [received_ref[:, :cap, :].reshape(slots, width), rest.reshape(slots, width // 2)]
        place = jnp.where(lax.broadcasted_iota(jnp.int32, (own_rows, slots), 0) == numbers, 1.0, 0.0).astype(bf16)
        totals = []
        for value in sets:
            total = jnp.zeros((own_rows, value.shape[1]), f32)
            for piece in halves_of(value):
                total += jnp.dot(place, piece, preferred_element_type=f32)
            totals.append(total.T)
        total = jnp.concatenate(totals, axis=0)
    else:
        received = received_ref[...].reshape(slots, width)
        local_row = received[:, columns:columns + 1].astype(jnp.int32)
        place = jnp.where(lax.broadcasted_iota(jnp.int32, (slots, own_rows), 1) == local_row, 1.0, 0.0).astype(bf16)
        total = jnp.zeros((columns, own_rows), f32)
        for piece in halves_of(received[:, :columns].T):
            total += jnp.dot(piece, place, preferred_element_type=f32)
    move.wait()
    start = 0
    for reduced_ref in reduced_refs:
        rows = reduced_ref.shape[0]
        reduced_ref[...] = right_ref[start:start + rows, :] - total[start:start + rows]
        start += rows


def split_kernel(block, relative, matrix_ref, high_ref, low_ref):
    parts, own_rows, full_rows = matrix_ref.shape
    groups, rows, width = high_ref.shape
    layers = width // block
    height = 64
    for part in range(parts):
        for first in range(0, own_rows, height):
            start = part * own_rows + first
            for group in range(groups):
                for layer in range(layers):
                    column = (layer * groups + group if relative else group * layers + layer) * block
                    high, low = halves_of(matrix_ref[part, first:first + height, column:column + block])
                    high_ref[group, start:start + height, layer * block:(layer + 1) * block] = high
                    low_ref[group, start:start + height, layer * block:(layer + 1) * block] = low


def split_blocks(matrix, block, relative):
    parts, own_rows, full_rows = matrix.shape
    groups = 4 if full_rows % (4 * block) == 0 else 1
    vmem = pl.BlockSpec(memory_space=pltpu.VMEM)
    shape = jax.ShapeDtypeStruct((groups, parts * own_rows, full_rows // groups), bf16)
    return pl.pallas_call(
        functools.partial(split_kernel, block, relative),
        in_specs=[vmem],
        out_specs=[vmem, vmem],
        out_shape=[shape, shape],
        compiler_params=kernel_params(20),
        cost_estimate=pl.CostEstimate(flops=3 * matrix.size, bytes_accessed=8 * matrix.size, transcendentals=0),
    )(matrix)


def product_kernel(sources, layout, inputs, sets, block, begin, end, onward, relative, *refs):
    high_ref, low_ref = refs[inputs * sets:inputs * sets + 2]
    rest = refs[inputs * sets + 2:]
    groups, both_rows, width = high_ref.shape
    layers = width // block
    own_rows = both_rows // 2
    start_ref, rest = (rest[0], rest[1:]) if begin > 0 else (None, rest)
    out_refs, total_ref = (rest[:-1], rest[-1]) if end == groups else ((), rest[0])
    columns = total_ref.shape[0]
    me = lax.axis_index("tile")

    def block_of(step, layer):
        held = lax.div(me, 4) ^ layer if relative else layer
        hopped = lax.rem(lax.div(me, 4) + (layers - layer), layers)
        pieces = []
        for group in layout:
            which, place = group(step, held, held if sets == 1 else hopped)
            value = refs[which][place]
            if sets == 2:
                which, place = group(step, held, held)
                own = refs[inputs + which][place]
                value = jnp.where(lax.axis_index("chain") == 0, own, own - value)
            pieces.append(value)
        return jnp.concatenate(pieces, axis=0)

    active = jnp.logical_not(onward) | (lax.axis_index("chain") < lax.axis_size("chain") - 1)

    @pl.when(jnp.logical_not(active))
    def _():
        for out_ref in out_refs:
            out_ref[...] = jnp.zeros_like(out_ref)

    @pl.when(active)
    def _():
        for step in range(begin, end):
            group = step
            if relative:
                group = lax.rem(lax.div(me, 2) + step % 2, 2) * 2 + lax.rem(me + step // 2, 2)
            x_high, x_low = halves_of(jnp.concatenate([block_of(step, layer) for layer in range(layers)], axis=1))
            lhs = jnp.concatenate([x_high, x_low], axis=0)
            both = lax.dot_general(lhs, high_ref[group], lanes_contract, preferred_element_type=f32)
            part = both[:columns] + both[columns:]
            part += lax.dot_general(x_high, low_ref[group], lanes_contract, preferred_element_type=f32)
            if step > begin:
                total_ref[...] += part
            elif start_ref is None:
                total_ref[...] = part
            else:
                total_ref[...] = start_ref[...] + part
        start = 0
        for out_ref in out_refs:
            for first in range(0, out_ref.shape[0], 2 * sources):
                real = pl.ds(start + first, sources)
                imag = pl.ds(start + first + sources, sources)
                out_ref[first:first + sources, :] = total_ref[real, :own_rows] - total_ref[imag, own_rows:]
                out_ref[first + sources:first + 2 * sources, :] = total_ref[imag, :own_rows] + total_ref[real, own_rows:]
            start += out_ref.shape[0]


def product_part(split, onward, layout, blocks, own, begin, end, started, sources, shares, relative):
    groups, both_rows, width = split[0].shape
    block = blocks[0].shape[-1]
    vmem = pl.BlockSpec(memory_space=pltpu.VMEM)
    finish = end == groups
    whole = (sum(shares), both_rows)
    arrays = list(blocks) + list(own) + list(split) + ([] if started is None else [started])
    if finish:
        out_shape = [jax.ShapeDtypeStruct((rows, both_rows // 2), f32) for rows in shares]
    else:
        out_shape = jax.ShapeDtypeStruct(whole, f32)
    return pl.pallas_call(
        functools.partial(product_kernel, sources, layout, len(blocks), 2 if own else 1, block, begin, end, onward, relative),
        in_specs=[vmem] * len(arrays),
        out_specs=[vmem] * len(shares) if finish else vmem,
        out_shape=out_shape,
        scratch_shapes=[pltpu.VMEM(whole, f32)] if finish else [],
        compiler_params=kernel_params(20),
        cost_estimate=pl.CostEstimate(flops=6 * sum(shares) * both_rows * width * (end - begin), bytes_accessed=MIB, transcendentals=0),
    )(*arrays)


def tied(value, to):
    return lax.optimization_barrier((value, to))[0]


def solve_paired(reduced, diag_inverse, coupling, sources):
    chain_size = lax.axis_size("chain")
    tile_size = lax.axis_size("tile")
    own_rows = reduced[0].shape[1]
    shares = [each.shape[0] for each in reduced]
    layers = tile_size // 4

    def send(value, hop, target):
        if not hop:
            return lax.ppermute(value, "tile", [(t, target(t)) for t in range(tile_size)])
        pairs = [(c * tile_size + t, (c + 1) % chain_size * tile_size + target(t)) for c in range(chain_size) for t in range(tile_size)]
        return lax.ppermute(value, ("chain", "tile"), pairs)

    def first_stage(first, second, hop):
        pair = [second if across == 0 and not hop else send(second, hop, lambda t: t ^ (2 * across)) for across in range(2)]
        if hop:
            line = [send(first, True, lambda t: (t + 4 * by) % tile_size) for by in range(layers)]
        else:
            line = [first if by == 0 else send(first, False, lambda t: t ^ (4 * by)) for by in range(layers)]
        if hop:
            *pair, line[-1] = lax.optimization_barrier((*pair, line[-1]))
        return jnp.stack(pair), jnp.stack(line)

    def second_stage(pair, line):
        far = send(line, False, lambda t: t ^ 2)
        rest = [pair if by == 0 else send(pair, False, lambda t: t ^ (4 * by)) for by in range(layers)]
        return [line, far, jnp.stack(rest)]

    layout = [lambda step, held, line: (step % 2, (line,)), lambda step, held, line: (2, (held, step % 2))]

    def products(split, onward, held, own, shares):
        other = [send(each, False, lambda t: t ^ 1) for each in held]
        mine, theirs = own if own else ([], [])
        started = product_part(split, onward, layout, held, mine, 0, 2, None, sources, shares, True)
        return product_part(split, onward, layout, other, theirs, 2, 4, started, sources, shares, True), other

    only = chain_size == 1
    pair, line = first_stage(*reduced, False)
    split = split_blocks(tied(diag_inverse if only else coupling, reduced[0]), own_rows, True)
    pair, line, split = lax.optimization_barrier((pair, line, split))
    held = second_stage(pair, line)
    if only:
        return products(split, False, held, None, [sum(shares)])[0][0]
    diag_split = split_blocks(tied(diag_inverse, line), own_rows, True)
    held[1], held[2], diag_split = lax.optimization_barrier((held[1], held[2], diag_split))
    carried, other = products(split, True, held, None, shares)
    own = (held, other)
    for step in range(chain_size - 1):
        held = second_stage(*lax.optimization_barrier(first_stage(*carried, True)))
        if step < chain_size - 2:
            carried = products(split, True, held, own, shares)[0]
    return products(diag_split, False, held, own, [sum(shares)])[0][0]


def solve_flat(reduced, diag_inverse, coupling, sources):
    chain_size = lax.axis_size("chain")
    reduced = reduced[0]
    columns = reduced.shape[0]
    full_rows = diag_inverse.shape[2]
    block = min(256, full_rows)
    count = full_rows // block
    layout = [lambda step, held, line: (0, (step * layers + held,))]
    onward = [(i, i + 1) for i in range(chain_size - 1)]
    diag_split = split_blocks(diag_inverse, block, False)
    coupling_split = split_blocks(coupling, block, False)
    groups = diag_split[0].shape[0]
    layers = count // groups

    def gathered(value):
        whole = lax.all_gather(value, "tile", axis=1, tiled=True)
        return [whole.reshape(columns, count, block).transpose(1, 0, 2)]

    current = reduced
    for _ in range(chain_size - 1):
        carried = product_part(coupling_split, True, layout, gathered(current), [], 0, groups, None, sources, [columns], False)[0]
        current = reduced - lax.ppermute(carried, "chain", onward)
    return product_part(diag_split, False, layout, gathered(current), [], 0, groups, None, sources, [columns], False)[0]


def body(right_side, diag_inverse, coupling, updates, update_rows, tile_counts):
    batches, halves, sources, own_rows = right_side.shape
    tile_size = lax.axis_size("tile")
    entries, columns = updates.shape
    tile_rows = entries // tile_counts.shape[0]
    cap = 2 * entries // tile_size
    slots = tile_size * cap
    vmem = pl.BlockSpec(memory_space=pltpu.VMEM)
    hbm = pl.BlockSpec(memory_space=pltpu.HBM)
    folded = cap % 16 == 0 and slots <= 1024 and columns == 192 and own_rows <= 256 and 128 % cap == 0
    width = 128 if folded else -(-(columns + 1) // 128) * 128
    height = cap + cap // 2 + 8 if folded else cap
    packed, stored = pl.pallas_call(
        functools.partial(pack_kernel, own_rows, cap, tile_rows),
        in_specs=[hbm, hbm, hbm, hbm],
        out_specs=[vmem, hbm],
        out_shape=[
            jax.ShapeDtypeStruct((tile_size, height, width), f32),
            jax.ShapeDtypeStruct((STORE, columns, own_rows), f32),
        ],
        scratch_shapes=[
            pltpu.SMEM(tile_counts.shape, jnp.int32),
            pltpu.VMEM((1, entries), jnp.int32),
            pltpu.VMEM((columns, entries), f32),
            pltpu.VMEM((columns, own_rows), f32),
            pltpu.SemaphoreType.DMA((5,)),
        ],
        compiler_params=kernel_params(56),
    )(tile_counts, update_rows[None, :], updates.T, right_side.reshape(columns, own_rows))
    received = lax.all_to_all(packed, "tile", 0, 0, tiled=False)
    paired = own_rows % 128 == 0 and tile_size >= 8 and tile_size & (tile_size - 1) == 0 and batches > 1
    early = batches * 2 // 3 * halves * sources
    shares = [early, columns - early] if paired else [columns]
    reduced = pl.pallas_call(
        functools.partial(reduce_kernel, cap),
        in_specs=[vmem, hbm],
        out_specs=[vmem] * len(shares),
        out_shape=[jax.ShapeDtypeStruct((rows, own_rows), f32) for rows in shares],
        scratch_shapes=[pltpu.VMEM((columns, own_rows), f32), pltpu.SemaphoreType.DMA(())],
        compiler_params=kernel_params(50),
    )(received, stored)
    solve = solve_paired if paired else solve_flat
    return solve(reduced, diag_inverse, coupling, sources).reshape(right_side.shape)


def solution(mesh):
    in_specs = (
        P(None, None, None, ("chain", "tile")),
        P(None, ("chain", "tile"), None),
        P(None, ("chain", "tile"), None),
        P(("chain", "tile"), None),
        P(("chain", "tile")),
        P(("chain", "tile")),
    )
    out_specs = P(None, None, None, ("chain", "tile"))
    return jax.shard_map(body, mesh=mesh, in_specs=in_specs, out_specs=out_specs, check_vma=False)
```

```python
import functools

import jax
import jax.numpy as jnp
from jax import lax
from jax.experimental import pallas as pl
from jax.experimental.pallas import tpu as pltpu
from jax.sharding import PartitionSpec as P

MIB = 1 << 20
STORE = 24
f32 = jnp.float32
bf16 = jnp.bfloat16
lanes_contract = (((1,), (1,)), ((), ()))


def halves_of(value):
    high = value.astype(bf16)
    return high, (value - high.astype(f32)).astype(bf16)


def kernel_params(size):
    return pltpu.CompilerParams(vmem_limit_bytes=int(size * MIB))


def pack_kernel(own_rows, cap, tile_rows, counts_hbm, rows_hbm, updates_hbm, right_hbm, packed_ref, store_hbm, *scratch):
    counts_ref, rows_ref, updates_ref, right_ref, sems = scratch
    fetch = pltpu.make_async_copy(right_hbm, right_ref, sems.at[3])
    keep = pltpu.make_async_copy(right_ref, store_hbm.at[0], sems.at[4])
    moves = [
        pltpu.make_async_copy(counts_hbm, counts_ref, sems.at[0]),
        pltpu.make_async_copy(rows_hbm, rows_ref, sems.at[1]),
        pltpu.make_async_copy(updates_hbm, updates_ref, sems.at[2]),
    ]
    for move in moves:
        move.start()
    fetch.start()
    columns, entries = updates_ref.shape
    owners, height, width = packed_ref.shape
    slots = owners * cap
    entry = lax.broadcasted_iota(jnp.int32, (1, entries), 1)
    earlier = lax.broadcasted_iota(jnp.int32, (entries, entries), 0) < lax.broadcasted_iota(jnp.int32, (entries, entries), 1)
    for move in moves:
        move.wait()
    fetch.wait()
    keep.start()
    live = jnp.zeros((1, entries), jnp.bool_)
    for tile in range(entries // tile_rows):
        start = tile * tile_rows
        live = live | ((entry >= start) & (entry < start + counts_ref[tile]))
    rows = rows_ref[...]
    owner = rows // own_rows
    lane_owner = jnp.broadcast_to(owner.astype(f32), (entries, entries))
    rank = jnp.sum(jnp.where(earlier & (lane_owner.T == lane_owner), 1, 0), axis=0, keepdims=True)
    slot = owner * cap + rank
    choose = jnp.where(lax.broadcasted_iota(jnp.int32, (slots, entries), 0) == slot, 1.0, 0.0).astype(bf16)
    data = jnp.where(live, updates_ref[...], 0.0)
    local_row = (rows - owner * own_rows).astype(f32)
    folded = height > cap
    if not folded:
        tail = jnp.where(lax.broadcasted_iota(jnp.int32, (width - columns, entries), 0) == 0, local_row, 0.0)
        data = jnp.concatenate([data, tail], axis=0)
    packed = jnp.zeros((slots, data.shape[0]), f32)
    for piece in halves_of(data):
        packed += lax.dot_general(choose, piece, lanes_contract, preferred_element_type=f32)
    packed = packed.reshape(owners, cap, data.shape[0])
    keep.wait()
    if not folded:
        packed_ref[...] = packed
        return
    half = cap // 2
    packed_ref[:, :cap, :] = packed[:, :, :width]
    packed_ref[:, cap:cap + half, :] = jnp.concatenate([packed[:, :half, width:], packed[:, half:, width:]], axis=2)
    first = lax.axis_index("tile") * cap
    by_owner = jnp.where(lax.broadcasted_iota(jnp.int32, (owners, entries), 0) == owner, local_row, 0.0).astype(bf16)
    by_lane = jnp.where(lax.broadcasted_iota(jnp.int32, (width, entries), 0) == first % width + rank, 1.0, 0.0).astype(bf16)
    numbers = lax.dot_general(by_owner, by_lane, lanes_contract, preferred_element_type=f32)
    line = lax.broadcasted_iota(jnp.int32, (owners, 8, width), 1)
    packed_ref[:, cap + half:, :] = jnp.where(line == first // width, numbers[:, None, :], 0.0)


def reduce_kernel(cap, received_ref, right_hbm, *refs):
    reduced_refs, right_ref, sem = refs[:-2], refs[-2], refs[-1]
    move = pltpu.make_async_copy(right_hbm.at[0], right_ref, sem)
    move.start()
    owners, height, width = received_ref.shape
    slots = owners * cap
    columns, own_rows = right_ref.shape
    if height > cap:
        half = cap // 2
        numbers = jnp.sum(received_ref[:, cap + half:, :], axis=0)
        numbers = jnp.concatenate([numbers[i:i + 1] for i in range(slots // width)], axis=1).astype(jnp.int32)
        rest = received_ref[:, cap:cap + half, :]
        rest = jnp.concatenate([rest[:, :, :width // 2], rest[:, :, width // 2:]], axis=1)
        sets = [received_ref[:, :cap, :].reshape(slots, width), rest.reshape(slots, width // 2)]
        place = jnp.where(lax.broadcasted_iota(jnp.int32, (own_rows, slots), 0) == numbers, 1.0, 0.0).astype(bf16)
        totals = []
        for value in sets:
            total = jnp.zeros((own_rows, value.shape[1]), f32)
            for piece in halves_of(value):
                total += jnp.dot(place, piece, preferred_element_type=f32)
            totals.append(total.T)
        total = jnp.concatenate(totals, axis=0)
    else:
        received = received_ref[...].reshape(slots, width)
        local_row = received[:, columns:columns + 1].astype(jnp.int32)
        place = jnp.where(lax.broadcasted_iota(jnp.int32, (slots, own_rows), 1) == local_row, 1.0, 0.0).astype(bf16)
        total = jnp.zeros((columns, own_rows), f32)
        for piece in halves_of(received[:, :columns].T):
            total += jnp.dot(piece, place, preferred_element_type=f32)
    move.wait()
    start = 0
    for reduced_ref in reduced_refs:
        rows = reduced_ref.shape[0]
        reduced_ref[...] = right_ref[start:start + rows, :] - total[start:start + rows]
        start += rows


def split_kernel(block, relative, matrix_ref, high_ref, low_ref):
    parts, own_rows, full_rows = matrix_ref.shape
    groups, rows, width = high_ref.shape
    layers = width // block
    height = 64
    for part in range(parts):
        for first in range(0, own_rows, height):
            start = part * own_rows + first
            for group in range(groups):
                for layer in range(layers):
                    column = (layer * groups + group if relative else group * layers + layer) * block
                    high, low = halves_of(matrix_ref[part, first:first + height, column:column + block])
                    high_ref[group, start:start + height, layer * block:(layer + 1) * block] = high
                    low_ref[group, start:start + height, layer * block:(layer + 1) * block] = low


def split_blocks(matrix, block, relative):
    parts, own_rows, full_rows = matrix.shape
    groups = 4 if full_rows % (4 * block) == 0 else 1
    vmem = pl.BlockSpec(memory_space=pltpu.VMEM)
    shape = jax.ShapeDtypeStruct((groups, parts * own_rows, full_rows // groups), bf16)
    return pl.pallas_call(
        functools.partial(split_kernel, block, relative),
        in_specs=[vmem],
        out_specs=[vmem, vmem],
        out_shape=[shape, shape],
        compiler_params=kernel_params(20),
        cost_estimate=pl.CostEstimate(flops=3 * matrix.size, bytes_accessed=8 * matrix.size, transcendentals=0),
    )(matrix)


def product_kernel(sources, layout, inputs, sets, block, begin, end, onward, relative, *refs):
    high_ref, low_ref = refs[inputs * sets:inputs * sets + 2]
    rest = refs[inputs * sets + 2:]
    groups, both_rows, width = high_ref.shape
    layers = width // block
    own_rows = both_rows // 2
    start_ref, rest = (rest[0], rest[1:]) if begin > 0 else (None, rest)
    out_refs, total_ref = (rest[:-1], rest[-1]) if end == groups else ((), rest[0])
    columns = total_ref.shape[0]
    me = lax.axis_index("tile")

    def block_of(step, layer):
        held = lax.div(me, 4) ^ layer if relative else layer
        hopped = lax.rem(lax.div(me, 4) + (layers - layer), layers)
        pieces = []
        for group in layout:
            which, place = group(step, held, held if sets == 1 else hopped)
            value = refs[which][place]
            if sets == 2:
                which, place = group(step, held, held)
                own = refs[inputs + which][place]
                value = jnp.where(lax.axis_index("chain") == 0, own, own - value)
            pieces.append(value)
        return jnp.concatenate(pieces, axis=0)

    active = jnp.logical_not(onward) | (lax.axis_index("chain") < lax.axis_size("chain") - 1)

    @pl.when(jnp.logical_not(active))
    def _():
        for out_ref in out_refs:
            out_ref[...] = jnp.zeros_like(out_ref)

    @pl.when(active)
    def _():
        for step in range(begin, end):
            group = step
            if relative:
                group = lax.rem(lax.div(me, 2) + step % 2, 2) * 2 + lax.rem(me + step // 2, 2)
            x_high, x_low = halves_of(jnp.concatenate([block_of(step, layer) for layer in range(layers)], axis=1))
            lhs = jnp.concatenate([x_high, x_low], axis=0)
            both = lax.dot_general(lhs, high_ref[group], lanes_contract, preferred_element_type=f32)
            part = both[:columns] + both[columns:]
            part += lax.dot_general(x_high, low_ref[group], lanes_contract, preferred_element_type=f32)
            if step > begin:
                total_ref[...] += part
            elif start_ref is None:
                total_ref[...] = part
            else:
                total_ref[...] = start_ref[...] + part
        start = 0
        for out_ref in out_refs:
            start = 0 if start == columns else start
            for first in range(0, out_ref.shape[0], 2 * sources):
                real = pl.ds(start + first, sources)
                imag = pl.ds(start + first + sources, sources)
                out_ref[first:first + sources, :] = total_ref[real, :own_rows] - total_ref[imag, own_rows:]
                out_ref[first + sources:first + 2 * sources, :] = total_ref[imag, :own_rows] + total_ref[real, own_rows:]
            start += out_ref.shape[0]


def product_part(split, onward, layout, blocks, own, begin, end, started, sources, shares, relative):
    groups, both_rows, width = split[0].shape
    block = blocks[0].shape[-1]
    vmem = pl.BlockSpec(memory_space=pltpu.VMEM)
    finish = end == groups
    columns = shares[-1] if len(shares) == 3 else sum(shares)
    whole = (columns, both_rows)
    arrays = list(blocks) + list(own) + list(split) + ([] if started is None else [started])
    if finish:
        out_shape = [jax.ShapeDtypeStruct((rows, both_rows // 2), f32) for rows in shares]
    else:
        out_shape = jax.ShapeDtypeStruct(whole, f32)
    return pl.pallas_call(
        functools.partial(product_kernel, sources, layout, len(blocks), 2 if own else 1, block, begin, end, onward, relative),
        in_specs=[vmem] * len(arrays),
        out_specs=[vmem] * len(shares) if finish else vmem,
        out_shape=out_shape,
        scratch_shapes=[pltpu.VMEM(whole, f32)] if finish else [],
        compiler_params=kernel_params(20),
        cost_estimate=pl.CostEstimate(flops=6 * columns * both_rows * width * (end - begin), bytes_accessed=MIB, transcendentals=0),
    )(*arrays)


def tied(value, to):
    return lax.optimization_barrier((value, to))[0]


def solve_paired(reduced, diag_inverse, coupling, sources):
    chain_size = lax.axis_size("chain")
    tile_size = lax.axis_size("tile")
    own_rows = reduced[0].shape[1]
    shares = [each.shape[0] for each in reduced]
    layers = tile_size // 4

    def send(value, hop, target):
        if not hop:
            return lax.ppermute(value, "tile", [(t, target(t)) for t in range(tile_size)])
        pairs = [(c * tile_size + t, (c + 1) % chain_size * tile_size + target(t)) for c in range(chain_size) for t in range(tile_size)]
        return lax.ppermute(value, ("chain", "tile"), pairs)

    def first_stage(first, second, whole=None):
        if whole is None:
            line = [first if by == 0 else send(first, False, lambda t: t ^ (4 * by)) for by in range(layers)]
            pair = [second, send(second, False, lambda t: t ^ 2)]
            return jnp.stack(pair), jnp.stack(line)
        line = [send(first, True, lambda t: (t + 4 * by) % tile_size) for by in range(1, layers)]
        pair = send(second, True, lambda t: t ^ 2)
        straight = send(whole, True, lambda t: t)
        early = first.shape[0]
        return jnp.stack([straight[early:], pair]), jnp.stack([straight[:early], *line])

    def second_stage(pair, line):
        far = send(line, False, lambda t: t ^ 2)
        rest = [pair if by == 0 else send(pair, False, lambda t: t ^ (4 * by)) for by in range(layers)]
        return [line, far, jnp.stack(rest)]

    layout = [lambda step, held, line: (step % 2, (line,)), lambda step, held, line: (2, (held, step % 2))]

    def products(split, onward, held, own, shares):
        other = [send(each, False, lambda t: t ^ 1) for each in held]
        mine, theirs = own if own else ([], [])
        started = product_part(split, onward, layout, held, mine, 0, 2, None, sources, shares, True)
        return product_part(split, onward, layout, other, theirs, 2, 4, started, sources, shares, True), other

    only = chain_size == 1
    pair, line = first_stage(*reduced)
    split = split_blocks(tied(diag_inverse if only else coupling, reduced[0]), own_rows, True)
    pair, line, split = lax.optimization_barrier((pair, line, split))
    held = second_stage(pair, line)
    if only:
        return products(split, False, held, None, [sum(shares)])[0][0]
    diag_split = split_blocks(tied(diag_inverse, line), own_rows, True)
    held[1], held[2], diag_split = lax.optimization_barrier((held[1], held[2], diag_split))
    carried, other = products(split, True, held, None, [*shares, sum(shares)])
    own = (held, other)
    for step in range(chain_size - 1):
        held = second_stage(*lax.optimization_barrier(first_stage(*carried)))
        if step < chain_size - 2:
            carried = products(split, True, held, own, [*shares, sum(shares)])[0]
    return products(diag_split, False, held, own, [sum(shares)])[0][0]


def solve_flat(reduced, diag_inverse, coupling, sources):
    chain_size = lax.axis_size("chain")
    reduced = reduced[0]
    columns = reduced.shape[0]
    full_rows = diag_inverse.shape[2]
    block = min(256, full_rows)
    count = full_rows // block
    layout = [lambda step, held, line: (0, (step * layers + held,))]
    onward = [(i, i + 1) for i in range(chain_size - 1)]
    diag_split = split_blocks(diag_inverse, block, False)
    coupling_split = split_blocks(coupling, block, False)
    groups = diag_split[0].shape[0]
    layers = count // groups

    def gathered(value):
        whole = lax.all_gather(value, "tile", axis=1, tiled=True)
        return [whole.reshape(columns, count, block).transpose(1, 0, 2)]

    current = reduced
    for _ in range(chain_size - 1):
        carried = product_part(coupling_split, True, layout, gathered(current), [], 0, groups, None, sources, [columns], False)[0]
        current = reduced - lax.ppermute(carried, "chain", onward)
    return product_part(diag_split, False, layout, gathered(current), [], 0, groups, None, sources, [columns], False)[0]


def body(right_side, diag_inverse, coupling, updates, update_rows, tile_counts):
    batches, halves, sources, own_rows = right_side.shape
    tile_size = lax.axis_size("tile")
    entries, columns = updates.shape
    tile_rows = entries // tile_counts.shape[0]
    cap = 2 * entries // tile_size
    slots = tile_size * cap
    vmem = pl.BlockSpec(memory_space=pltpu.VMEM)
    hbm = pl.BlockSpec(memory_space=pltpu.HBM)
    folded = cap % 16 == 0 and slots <= 1024 and columns == 192 and own_rows <= 256 and 128 % cap == 0
    width = 128 if folded else -(-(columns + 1) // 128) * 128
    height = cap + cap // 2 + 8 if folded else cap
    packed, stored = pl.pallas_call(
        functools.partial(pack_kernel, own_rows, cap, tile_rows),
        in_specs=[hbm, hbm, hbm, hbm],
        out_specs=[vmem, hbm],
        out_shape=[
            jax.ShapeDtypeStruct((tile_size, height, width), f32),
            jax.ShapeDtypeStruct((STORE, columns, own_rows), f32),
        ],
        scratch_shapes=[
            pltpu.SMEM(tile_counts.shape, jnp.int32),
            pltpu.VMEM((1, entries), jnp.int32),
            pltpu.VMEM((columns, entries), f32),
            pltpu.VMEM((columns, own_rows), f32),
            pltpu.SemaphoreType.DMA((5,)),
        ],
        compiler_params=kernel_params(56),
    )(tile_counts, update_rows[None, :], updates.T, right_side.reshape(columns, own_rows))
    received = lax.all_to_all(packed, "tile", 0, 0, tiled=False)
    paired = own_rows % 128 == 0 and tile_size >= 8 and tile_size & (tile_size - 1) == 0 and batches > 1
    early = batches * 2 // 3 * halves * sources
    shares = [early, columns - early] if paired else [columns]
    reduced = pl.pallas_call(
        functools.partial(reduce_kernel, cap),
        in_specs=[vmem, hbm],
        out_specs=[vmem] * len(shares),
        out_shape=[jax.ShapeDtypeStruct((rows, own_rows), f32) for rows in shares],
        scratch_shapes=[pltpu.VMEM((columns, own_rows), f32), pltpu.SemaphoreType.DMA(())],
        compiler_params=kernel_params(50),
    )(received, stored)
    solve = solve_paired if paired else solve_flat
    return solve(reduced, diag_inverse, coupling, sources).reshape(right_side.shape)


def solution(mesh):
    in_specs = (
        P(None, None, None, ("chain", "tile")),
        P(None, ("chain", "tile"), None),
        P(None, ("chain", "tile"), None),
        P(("chain", "tile"), None),
        P(("chain", "tile")),
        P(("chain", "tile")),
    )
    out_specs = P(None, None, None, ("chain", "tile"))
    return jax.shard_map(body, mesh=mesh, in_specs=in_specs, out_specs=out_specs, check_vma=False)
```
